32 devices in a mesh: seq: 2 (over x), shard: 16 (over z, y, core).
Axes of the slice: x: 2, y: 2, z: 4, core: 2. Of those that a mesh axis runs over, the one named last changes fastest.
Arguments:
- tokens: bfloat16 [16, 320, 2048], P('shard', 'seq'), may hold values from -6 to 6
- cotangent: bfloat16 [16, 320, 2048], P('shard', 'seq'), may hold values from -6 to 6
- norm1_gain: bfloat16 [2048], P(('seq', 'shard')), may hold values from 0.25 to 1.75
- norm1_bias: bfloat16 [2048], P(('seq', 'shard')), may hold values from -3 to 3
- qkv_weight: bfloat16 [2048, 6144], P(('seq', 'shard')), may hold values from -0.125 to 0.125
- qkv_bias: bfloat16 [6144], P(('seq', 'shard')), may hold values from -3 to 3
- out_weight: bfloat16 [2048, 2048], P(('seq', 'shard')), may hold values from -0.5 to 0.5
- norm2_gain: bfloat16 [2048], P(('seq', 'shard')), may hold values from 0.25 to 1.75
- norm2_bias: bfloat16 [2048], P(('seq', 'shard')), may hold values from -3 to 3
- gate_weight: bfloat16 [2048, 5632], P(('seq', 'shard')), may hold values from -0.125 to 0.125
- up_weight: bfloat16 [2048, 5632], P(('seq', 'shard')), may hold values from -0.125 to 0.125
- down_weight: bfloat16 [5632, 2048], P(('seq', 'shard')), may hold values from -0.078125 to 0.078125
Outputs:
- out: bfloat16 [16, 320, 2048], P('shard', 'seq')
- d_input: float32 [16, 320, 2048], P('shard', 'seq')
- norm1_gain_grad: float32 [2048], P(('seq', 'shard'))
- norm1_bias_grad: float32 [2048], P(('seq', 'shard'))
- qkv_weight_grad: float32 [2048, 6144], P(('seq', 'shard'))
- qkv_bias_grad: float32 [6144], P(('seq', 'shard'))
- out_weight_grad: float32 [2048, 2048], P(('seq', 'shard'))
- norm2_gain_grad: float32 [2048], P(('seq', 'shard'))
- norm2_bias_grad: float32 [2048], P(('seq', 'shard'))
- gate_weight_grad: float32 [2048, 5632], P(('seq', 'shard'))
- up_weight_grad: float32 [2048, 5632], P(('seq', 'shard'))
- down_weight_grad: float32 [5632, 2048], P(('seq', 'shard'))
The draws below stay inside these ranges and needn't reach their ends.
All inputs are finite; a program needn't handle non-finite values.
Results may differ from the reference program's by a relative error of at most 0.012.
Values may be sent and summed in bfloat16 or wider, within the bound.
A program may use at most 448 MiB of HBM per device.

```python
import jax
import jax.numpy as jnp
from jax import lax

D = 2048
HEADS = 32
HEAD_DIM = 64
ROTARY = 16
FF = 5632
SEQS = 16
LEN = 320


def steps_of(key, extent, pieces, smallest, high):
    loudness, own = 1.0, jax.random.fold_in(key, 6)
    for axis_at, shards_of in pieces:
        draws = jnp.exp(jax.random.uniform(jax.random.fold_in(own, axis_at), (shards_of,), jnp.float32, smallest / len(pieces), high / len(pieces)))
        loudness = loudness * jnp.repeat(draws, extent[axis_at] // shards_of).reshape([-1 if axis == axis_at else 1 for axis in range(len(extent))])
    return loudness


def bell_draw(key, shape, width, most, shards=(), held_as=jnp.bfloat16):
    values = jax.random.normal(key, shape, jnp.float32) * width
    if len(shards) > 0:
        values = steps_of(key, shape, shards, -0.22, 0.18) * values
    return jnp.clip(values, min=-most, max=most).astype(held_as)


def setup_inputs(seed: int = 0) -> dict:
    arg_keys = jax.random.split(jax.random.key(seed), 13)
    return {
        "tokens": bell_draw(arg_keys[0], (SEQS, LEN, D), 1.0, 6.0, ((0, 16), (1, 2))),
        "cotangent": bell_draw(arg_keys[1], (SEQS, LEN, D), 1.0, 6.0, ((0, 16), (1, 2))),
        "norm1_gain": jnp.clip(1.0 + 0.15 * jax.random.normal(arg_keys[2], (D,), jnp.float32), 0.25, 1.75).astype(jnp.bfloat16),
        "norm1_bias": bell_draw(arg_keys[3], (D,), 0.5, 3.0, ((0, 32),)),
        "qkv_weight": bell_draw(arg_keys[4], (D, 3 * D), D ** -0.5, 0.125, ((0, 32),)),
        "qkv_bias": bell_draw(arg_keys[5], (3 * D,), 0.5, 3.0, ((0, 32),)),
        "out_weight": bell_draw(arg_keys[6], (D, D), (D // 16) ** -0.5, 0.5, ((0, 32),)),
        "norm2_gain": jnp.clip(1.0 + 0.15 * jax.random.normal(arg_keys[7], (D,), jnp.float32), 0.25, 1.75).astype(jnp.bfloat16),
        "norm2_bias": bell_draw(arg_keys[8], (D,), 0.5, 3.0, ((0, 32),)),
        "gate_weight": bell_draw(arg_keys[9], (D, FF), D ** -0.5, 0.125, ((0, 32),)),
        "up_weight": bell_draw(arg_keys[10], (D, FF), D ** -0.5, 0.125, ((0, 32),)),
        "down_weight": bell_draw(arg_keys[11], (FF, D), FF ** -0.5, 0.078125, ((0, 32),)),
    }


@jax.custom_vjp
def low(v):
    return lax.optimization_barrier(v.astype(jnp.bfloat16)).astype(jnp.float32)

@jax.custom_vjp
def low_back(v):
    return v

def low_keep(v):
    return (low(v), None)

def low_pass(kept, grad):
    return (grad,)

def back_keep(v):
    return (v, None)

def back_low(kept, grad):
    return (low(grad),)
low.defvjp(low_keep, low_pass)
low_back.defvjp(back_keep, back_low)

def product(left, right):
    return jnp.dot(left, right, precision=lax.Precision.HIGHEST)

def rounded(values):
    return low_back(low(values))

def layer_norm(values, gain_row, bias_row):
    centre = lax.optimization_barrier(jnp.mean(values, axis=-1, keepdims=True))
    centred = values - centre
    spread = lax.optimization_barrier(jnp.mean(centred * centred, axis=-1, keepdims=True))
    return centred * lax.rsqrt(spread + 1e-05) * gain_row + bias_row

def rotate(values, positions):
    halves = ROTARY // 2
    frequency = 10000.0 ** (-2.0 * jnp.arange(halves, dtype=jnp.float32) / ROTARY)
    angles = positions.astype(jnp.float32)[:, None] * frequency[None, :]
    cosine_table = jnp.cos(angles)[:, None, :]
    sine_table = jnp.sin(angles)[:, None, :]
    first_half = values[..., :halves]
    second_half = values[..., halves:ROTARY]
    return jnp.concatenate([first_half * cosine_table - second_half * sine_table, second_half * cosine_table + first_half * sine_table, values[..., ROTARY:]], axis=-1)

def block_forward(params, inputs):
    norm1_gain, norm1_bias, qkv_weight, qkv_bias, out_weight, norm2_gain, norm2_bias, gate_weight, up_weight, down_weight = params
    length = inputs.shape[0]
    positions = jnp.arange(length, dtype=jnp.int32)
    first_input = low(layer_norm(inputs, norm1_gain, norm1_bias))
    projected = low_back(product(first_input, qkv_weight) + qkv_bias)
    queries = rounded(rotate(projected[:, :D].reshape(length, HEADS, HEAD_DIM), positions))
    key_rows = rounded(rotate(projected[:, D:2 * D].reshape(length, HEADS, HEAD_DIM), positions))
    value_rows = rounded(projected[:, 2 * D:].reshape(length, HEADS, HEAD_DIM))
    scores = low_back(jnp.einsum('qhd,khd->hqk', queries, key_rows, precision=lax.Precision.HIGHEST) * 0.125)
    causal = positions[:, None] >= positions[None, :]
    scores = jnp.where(causal[None, :, :], scores, -1e+30)
    weights = jax.nn.softmax(scores, axis=-1)
    mixed = rounded(jnp.einsum('hqk,khd->qhd', low(weights), value_rows, precision=lax.Precision.HIGHEST))
    mixed = mixed.reshape(length, D)
    middle = inputs + low_back(product(mixed, out_weight))
    second_input = low(layer_norm(middle, norm2_gain, norm2_bias))
    gate_rows = low_back(product(second_input, gate_weight))
    up_rows = low_back(product(second_input, up_weight))
    hidden = low(jax.nn.silu(gate_rows) * up_rows)
    return middle + low_back(product(hidden, down_weight))

def reference(tokens, cotangent, norm1_gain, norm1_bias, qkv_weight, qkv_bias, out_weight, norm2_gain, norm2_bias, gate_weight, up_weight, down_weight):
    params = tuple((argument.astype(jnp.float32) for argument in (norm1_gain, norm1_bias, qkv_weight, qkv_bias, out_weight, norm2_gain, norm2_bias, gate_weight, up_weight, down_weight)))
    totals = jax.tree.map(jnp.zeros_like, params)

    def sequence_step(carried, inputs_pair):
        inputs, upstream = inputs_pair
        outputs, pullback = jax.vjp(block_forward, params, inputs.astype(jnp.float32))
        grads_params, grads_inputs = pullback(upstream.astype(jnp.float32))
        return (jax.tree.map(jnp.add, carried, grads_params), (outputs.astype(jnp.bfloat16), grads_inputs))
    totals, (outputs, input_grads) = lax.scan(sequence_step, totals, (tokens, cotangent))
    return (outputs, input_grads, totals[0], totals[1], totals[2], totals[3], totals[4], totals[5], totals[6], totals[7], totals[8], totals[9])
```

```python
import jax
import jax.numpy as jnp
import numpy as np
from jax import lax
from jax.sharding import PartitionSpec as P

HEADS = 32
HEAD_DIM = 64
ROTARY = 16
TEAM = ("seq", "zl")
PEERS = ("zh", "y", "c")
ALL = ("seq", "zh", "zl", "y", "c")
BF = jnp.bfloat16
F32 = jnp.float32


def norm_rows(values):
    centre = jnp.mean(values, axis=-1, keepdims=True)
    centred = values - centre
    spread = jnp.mean(centred * centred, axis=-1, keepdims=True)
    scale_rows = lax.rsqrt(spread + 1e-05)
    return (centred * scale_rows, scale_rows)


def norm_back(grad_normed, normed, scale_rows):
    return scale_rows * (
        grad_normed
        - jnp.mean(grad_normed, axis=-1, keepdims=True)
        - normed * jnp.mean(grad_normed * normed, axis=-1, keepdims=True)
    )


def rotate(values, positions, direction):
    halves = ROTARY // 2
    frequency = 10000.0 ** (-2.0 * jnp.arange(halves, dtype=F32) / ROTARY)
    angles = positions.astype(F32)[:, None] * frequency[None, :]
    cosine_table = jnp.cos(angles)[:, None, :]
    sine_table = jnp.sin(angles)[:, None, :] * direction
    first_half = values[..., :halves]
    second_half = values[..., halves:ROTARY]
    return jnp.concatenate(
        [
            first_half * cosine_table - second_half * sine_table,
            second_half * cosine_table + first_half * sine_table,
            values[..., ROTARY:],
        ],
        axis=-1,
    )


def dot(left, right):
    return jnp.dot(left, right, preferred_element_type=F32)


def dot_nt(left, right):
    return lax.dot_general(left, right, (((1,), (1,)), ((), ())), preferred_element_type=F32)


def dot_tn(left, right):
    return lax.dot_general(left, right, (((0,), (0,)), ((), ())), preferred_element_type=F32)


def per_device(
    tokens, cotangent, norm1_gain, norm1_bias, qkv_weight, qkv_bias, out_weight,
    norm2_gain, norm2_bias, gate_weight, up_weight, down_weight,
):
    zh = lax.axis_size("zh")
    rows = tokens.shape[1]
    width = tokens.shape[2]
    own = qkv_weight.shape[0]
    ff = gate_weight.shape[1]
    half = lax.axis_size("seq")
    length = rows * half
    team = half * lax.axis_size("zl")
    seqs = lax.axis_size("zl")

    def cut_columns(shard, parts):
        block = shard.shape[1] // parts // (half * zh * seqs)
        cut = shard.reshape(own, parts, half, zh, seqs, block).transpose(2, 4, 0, 1, 3, 5)
        return cut.reshape(team, own, parts * zh * block)

    def join_columns(cut, parts):
        block = cut.shape[2] // parts // zh
        cut = cut.reshape(half, seqs, own, parts, zh, block).transpose(2, 3, 0, 4, 1, 5)
        return cut.reshape(own, -1)

    def mine_columns(whole, parts):
        block = whole.shape[0] // parts // (half * zh * seqs)
        cut = whole.reshape(parts, half, zh, seqs, block)
        cut = lax.dynamic_index_in_dim(cut, lax.axis_index("seq"), 1, keepdims=False)
        cut = lax.dynamic_index_in_dim(cut, lax.axis_index("zl"), 2, keepdims=False)
        return cut.reshape(-1)

    def to_owner_order(values):
        n = values.shape[0]
        return values.reshape(n, half, zh, seqs, 4, own).transpose(0, 2, 4, 1, 3, 5).reshape(n, width)

    def from_owner_order(values):
        n = values.shape[0]
        return values.reshape(n, zh, 4, half, seqs, own).transpose(0, 3, 1, 4, 2, 5).reshape(n, width)

    def gather_columns(shard, parts):
        cut = cut_columns(shard, parts)
        cut = lax.all_to_all(cut, TEAM, split_axis=0, concat_axis=0, tiled=True)
        return lax.all_gather(cut.reshape(team * own, -1), PEERS, axis=0, tiled=True)

    def gather_rows(shard):
        return lax.all_gather(shard, PEERS, axis=0, tiled=True)

    def gather_tokens(values):
        return lax.all_gather(values, ("zl", "seq"), axis=0, tiled=True)

    def sum_tokens(values):
        return lax.psum_scatter(values.astype(BF), ("zl", "seq"), scatter_dimension=0, tiled=True).astype(F32)

    def sum_rows(values):
        return lax.psum_scatter(values.astype(BF), PEERS, scatter_dimension=0, tiled=True)

    def sum_columns(values, parts):
        part = sum_rows(values).reshape(team, own, -1)
        part = lax.all_to_all(part, TEAM, split_axis=0, concat_axis=0, tiled=True)
        return join_columns(part, parts).astype(F32)

    small = jnp.concatenate([norm1_gain, norm1_bias, norm2_gain, norm2_bias, qkv_bias])
    small = lax.all_gather(small, ALL, axis=0, tiled=False)
    first_gain = small[:, :own].reshape(-1).astype(F32)
    first_bias = small[:, own : 2 * own].reshape(-1).astype(F32)
    second_gain = small[:, 2 * own : 3 * own].reshape(-1).astype(F32)
    second_bias = small[:, 3 * own : 4 * own].reshape(-1).astype(F32)
    qkv_offset = mine_columns(small[:, 4 * own :].reshape(-1), 3).astype(F32)

    inputs = tokens[0].astype(F32)
    first_normed, first_scale = norm_rows(inputs)
    first_own = to_owner_order((first_normed * first_gain + first_bias).astype(BF))
    first_input = gather_tokens(first_own)
    qkv_matrix = gather_columns(qkv_weight, 3)
    out_matrix = gather_rows(out_weight)
    gate_matrix = gather_columns(gate_weight, 1)
    up_matrix = gather_columns(up_weight, 1)
    down_matrix = gather_rows(down_weight)
    upstream = gather_tokens(cotangent[0])

    projected = dot(first_input, qkv_matrix) + qkv_offset
    part = width // team
    group_heads = part // HEAD_DIM
    positions = jnp.tile(jnp.arange(length, dtype=jnp.int32), seqs)

    def heads_of(values):
        return values.reshape(seqs, length, group_heads, HEAD_DIM).transpose(0, 2, 1, 3)

    def unheads(values):
        return values.transpose(0, 2, 1, 3).reshape(seqs * length, part)

    queries = heads_of(rotate(projected[:, :part].reshape(-1, group_heads, HEAD_DIM), positions, 1.0).astype(BF))
    keys = heads_of(rotate(projected[:, part : 2 * part].reshape(-1, group_heads, HEAD_DIM), positions, 1.0).astype(BF))
    values = heads_of(projected[:, 2 * part :].astype(BF))
    causal = jnp.arange(length)[:, None] >= jnp.arange(length)[None, :]
    scores = jnp.einsum("shqd,shkd->shqk", queries, keys, preferred_element_type=F32) * 0.125
    scores = jnp.where(causal, scores, -1e30)
    highest = jnp.max(scores, axis=-1, keepdims=True)
    exponent = jnp.exp(scores - highest)
    probs = exponent / jnp.sum(exponent, axis=-1, keepdims=True)
    probs_low = probs.astype(BF)
    mixed = unheads(jnp.einsum("shqk,shkd->shqd", probs_low, values, preferred_element_type=F32).astype(BF))
    middle = inputs + sum_tokens(dot(mixed, out_matrix))

    second_normed, second_scale = norm_rows(middle)
    second_own = to_owner_order((second_normed * second_gain + second_bias).astype(BF))
    second_input = gather_tokens(second_own)
    gate_rows = dot(second_input, gate_matrix)
    up_rows = dot(second_input, up_matrix)
    sigmoid_gate = jax.nn.sigmoid(gate_rows)
    silu_gate = gate_rows * sigmoid_gate
    hidden = (silu_gate * up_rows).astype(BF)
    result = middle + sum_tokens(dot(hidden, down_matrix))

    down_total = sum_rows(dot_tn(hidden, upstream)).astype(F32)
    grad_hidden = dot_nt(upstream, down_matrix)
    grad_gate = (grad_hidden * up_rows * sigmoid_gate * (1.0 + gate_rows * (1.0 - sigmoid_gate))).astype(BF)
    grad_up = (grad_hidden * silu_gate).astype(BF)
    gate_total = sum_columns(dot_tn(second_input, grad_gate), 1)
    up_total = sum_columns(dot_tn(second_input, grad_up), 1)
    grad_second = from_owner_order(sum_tokens(dot_nt(grad_gate, gate_matrix) + dot_nt(grad_up, up_matrix)))
    grad_middle = cotangent[0].astype(F32) + norm_back(grad_second * second_gain, second_normed, second_scale)
    grad_attended = gather_tokens(grad_middle.astype(BF))
    out_total = sum_rows(dot_tn(mixed, grad_attended)).astype(F32)
    grad_mixed = heads_of(dot_nt(grad_attended, out_matrix).astype(BF))
    grad_probs = jnp.einsum("shqd,shkd->shqk", grad_mixed, values, preferred_element_type=F32)
    grad_scores = (probs * (grad_probs - jnp.sum(probs * grad_probs, axis=-1, keepdims=True))).astype(BF)
    grad_queries = (jnp.einsum("shqk,shkd->shqd", grad_scores, keys, preferred_element_type=F32) * 0.125).astype(BF)
    grad_keys = (jnp.einsum("shqk,shqd->shkd", grad_scores, queries, preferred_element_type=F32) * 0.125).astype(BF)
    grad_values = jnp.einsum("shqk,shqd->shkd", probs_low, grad_mixed, preferred_element_type=F32).astype(BF)
    grad_queries = rotate(unheads(grad_queries).astype(F32).reshape(-1, group_heads, HEAD_DIM), positions, -1.0)
    grad_keys = rotate(unheads(grad_keys).astype(F32).reshape(-1, group_heads, HEAD_DIM), positions, -1.0)
    grad_projected = jnp.concatenate(
        [grad_queries.reshape(-1, part).astype(BF), grad_keys.reshape(-1, part).astype(BF), unheads(grad_values)],
        axis=1,
    )
    qkv_total = sum_columns(dot_tn(first_input, grad_projected), 3)
    grad_first = from_owner_order(sum_tokens(dot_nt(grad_projected, qkv_matrix)))
    grad_inputs = grad_middle + norm_back(grad_first * first_gain, first_normed, first_scale)

    bias_part = jnp.sum(grad_projected.astype(F32), axis=0).reshape(3, zh, -1)
    bias_whole = jnp.zeros((3, half, zh, seqs, bias_part.shape[2]), F32)
    bias_whole = lax.dynamic_update_slice(
        bias_whole, bias_part[:, None, :, None], (0, lax.axis_index("seq"), 0, lax.axis_index("zl"), 0)
    ).reshape(-1)
    count = width // own
    sums = jnp.concatenate(
        [
            jnp.sum(grad_first * first_normed, axis=0).reshape(count, own),
            jnp.sum(grad_first, axis=0).reshape(count, own),
            jnp.sum(grad_second * second_normed, axis=0).reshape(count, own),
            jnp.sum(grad_second, axis=0).reshape(count, own),
            bias_whole.reshape(count, 3 * own),
        ],
        axis=1,
    )
    sums = lax.psum_scatter(sums, ALL, scatter_dimension=0, tiled=True)[0]
    return (
        result.astype(BF)[None],
        grad_inputs[None],
        sums[:own],
        sums[own : 2 * own],
        qkv_total,
        sums[4 * own :],
        out_total,
        sums[2 * own : 3 * own],
        sums[3 * own : 4 * own],
        gate_total,
        up_total,
        down_total,
    )


def solution(mesh):
    half, shards = mesh.shape["seq"], mesh.shape["shard"]
    fine = jax.sharding.Mesh(mesh.devices.reshape(half, shards // 8, 2, 2, 2), ALL)
    token = P(("zh", "zl", "y", "c"), "seq", None)
    row = P(ALL)
    return jax.shard_map(
        per_device,
        mesh=fine,
        in_specs=(token, token) + (row,) * 10,
        out_specs=(token, token) + (row,) * 10,
        check_vma=False,
    )
```

```python
import jax
import jax.numpy as jnp
from jax import lax
from jax.experimental import pallas as pl
from jax.experimental.pallas import tpu as pltpu
from jax.sharding import PartitionSpec as P

HEADS = 32
HEAD_DIM = 64
ROTARY = 16
TEAM = ("seq", "zl")
PEERS = ("zh", "y", "c")
ALL = ("seq", "zh", "zl", "y", "c")
BF = jnp.bfloat16
F32 = jnp.float32


def norm_rows(values):
    centre = jnp.mean(values, axis=-1, keepdims=True)
    centred = values - centre
    spread = jnp.mean(centred * centred, axis=-1, keepdims=True)
    scale_rows = lax.rsqrt(spread + 1e-05)
    return (centred * scale_rows, scale_rows)


def norm_back(grad_normed, normed, scale_rows):
    return scale_rows * (
        grad_normed
        - jnp.mean(grad_normed, axis=-1, keepdims=True)
        - normed * jnp.mean(grad_normed * normed, axis=-1, keepdims=True)
    )


def rotate(values, positions, direction):
    halves = ROTARY // 2
    frequency = 10000.0 ** (-2.0 * jnp.arange(halves, dtype=F32) / ROTARY)
    angles = positions.astype(F32)[:, None] * frequency[None, :]
    cosine_table = jnp.cos(angles)[:, None, :]
    sine_table = jnp.sin(angles)[:, None, :] * direction
    first_half = values[..., :halves]
    second_half = values[..., halves:ROTARY]
    return jnp.concatenate(
        [
            first_half * cosine_table - second_half * sine_table,
            second_half * cosine_table + first_half * sine_table,
            values[..., ROTARY:],
        ],
        axis=-1,
    )


def dot(left, right):
    return jnp.dot(left, right, preferred_element_type=F32)


def dot_nt(left, right):
    return lax.dot_general(left, right, (((1,), (1,)), ((), ())), preferred_element_type=F32)


def dot_tn(left, right):
    return lax.dot_general(left, right, (((0,), (0,)), ((), ())), preferred_element_type=F32)


def plain_device(
    tokens, cotangent, norm1_gain, norm1_bias, qkv_weight, qkv_bias, out_weight,
    norm2_gain, norm2_bias, gate_weight, up_weight, down_weight,
):
    zh = lax.axis_size("zh")
    rows = tokens.shape[1]
    width = tokens.shape[2]
    own = qkv_weight.shape[0]
    ff = gate_weight.shape[1]
    half = lax.axis_size("seq")
    length = rows * half
    team = half * lax.axis_size("zl")
    seqs = lax.axis_size("zl")

    def cut_columns(shard, parts):
        block = shard.shape[1] // parts // (half * zh * seqs)
        cut = shard.reshape(own, parts, half, zh, seqs, block).transpose(2, 4, 0, 1, 3, 5)
        return cut.reshape(team, own, parts * zh * block)

    def join_columns(cut, parts):
        block = cut.shape[2] // parts // zh
        cut = cut.reshape(half, seqs, own, parts, zh, block).transpose(2, 3, 0, 4, 1, 5)
        return cut.reshape(own, -1)

    def mine_columns(whole, parts):
        block = whole.shape[0] // parts // (half * zh * seqs)
        cut = whole.reshape(parts, half, zh, seqs, block)
        cut = lax.dynamic_index_in_dim(cut, lax.axis_index("seq"), 1, keepdims=False)
        cut = lax.dynamic_index_in_dim(cut, lax.axis_index("zl"), 2, keepdims=False)
        return cut.reshape(-1)

    def to_owner_order(values):
        n = values.shape[0]
        return values.reshape(n, half, zh, seqs, 4, own).transpose(0, 2, 4, 1, 3, 5).reshape(n, width)

    def from_owner_order(values):
        n = values.shape[0]
        return values.reshape(n, zh, 4, half, seqs, own).transpose(0, 3, 1, 4, 2, 5).reshape(n, width)

    def gather_columns(shard, parts):
        cut = cut_columns(shard, parts)
        cut = lax.all_to_all(cut, TEAM, split_axis=0, concat_axis=0, tiled=True)
        return lax.all_gather(cut.reshape(team * own, -1), PEERS, axis=0, tiled=True)

    def gather_rows(shard):
        return lax.all_gather(shard, PEERS, axis=0, tiled=True)

    def gather_tokens(values):
        return lax.all_gather(values, ("zl", "seq"), axis=0, tiled=True)

    def sum_tokens(values):
        return lax.psum_scatter(values.astype(BF), ("zl", "seq"), scatter_dimension=0, tiled=True).astype(F32)

    def sum_rows(values):
        return lax.psum_scatter(values.astype(BF), PEERS, scatter_dimension=0, tiled=True)

    def sum_columns(values, parts):
        part = sum_rows(values).reshape(team, own, -1)
        part = lax.all_to_all(part, TEAM, split_axis=0, concat_axis=0, tiled=True)
        return join_columns(part, parts).astype(F32)

    small = jnp.concatenate([norm1_gain, norm1_bias, norm2_gain, norm2_bias, qkv_bias])
    small = lax.all_gather(small, ALL, axis=0, tiled=False)
    first_gain = small[:, :own].reshape(-1).astype(F32)
    first_bias = small[:, own : 2 * own].reshape(-1).astype(F32)
    second_gain = small[:, 2 * own : 3 * own].reshape(-1).astype(F32)
    second_bias = small[:, 3 * own : 4 * own].reshape(-1).astype(F32)
    qkv_offset = mine_columns(small[:, 4 * own :].reshape(-1), 3).astype(F32)

    inputs = tokens[0].astype(F32)
    first_normed, first_scale = norm_rows(inputs)
    first_own = to_owner_order((first_normed * first_gain + first_bias).astype(BF))
    first_input = gather_tokens(first_own)
    qkv_matrix = gather_columns(qkv_weight, 3)
    out_matrix = gather_rows(out_weight)
    gate_matrix = gather_columns(gate_weight, 1)
    up_matrix = gather_columns(up_weight, 1)
    down_matrix = gather_rows(down_weight)
    upstream = gather_tokens(cotangent[0])

    projected = dot(first_input, qkv_matrix) + qkv_offset
    part = width // team
    group_heads = part // HEAD_DIM
    positions = jnp.tile(jnp.arange(length, dtype=jnp.int32), seqs)

    def heads_of(values):
        return values.reshape(seqs, length, group_heads, HEAD_DIM).transpose(0, 2, 1, 3)

    def unheads(values):
        return values.transpose(0, 2, 1, 3).reshape(seqs * length, part)

    queries = heads_of(rotate(projected[:, :part].reshape(-1, group_heads, HEAD_DIM), positions, 1.0).astype(BF))
    keys = heads_of(rotate(projected[:, part : 2 * part].reshape(-1, group_heads, HEAD_DIM), positions, 1.0).astype(BF))
    values = heads_of(projected[:, 2 * part :].astype(BF))
    causal = jnp.arange(length)[:, None] >= jnp.arange(length)[None, :]
    scores = jnp.einsum("shqd,shkd->shqk", queries, keys, preferred_element_type=F32) * 0.125
    scores = jnp.where(causal, scores, -1e30)
    highest = jnp.max(scores, axis=-1, keepdims=True)
    exponent = jnp.exp(scores - highest)
    probs = exponent / jnp.sum(exponent, axis=-1, keepdims=True)
    probs_low = probs.astype(BF)
    mixed = unheads(jnp.einsum("shqk,shkd->shqd", probs_low, values, preferred_element_type=F32).astype(BF))
    middle = inputs + sum_tokens(dot(mixed, out_matrix))

    second_normed, second_scale = norm_rows(middle)
    second_own = to_owner_order((second_normed * second_gain + second_bias).astype(BF))
    second_input = gather_tokens(second_own)
    gate_rows = dot(second_input, gate_matrix)
    up_rows = dot(second_input, up_matrix)
    sigmoid_gate = jax.nn.sigmoid(gate_rows)
    silu_gate = gate_rows * sigmoid_gate
    hidden = (silu_gate * up_rows).astype(BF)
    result = middle + sum_tokens(dot(hidden, down_matrix))

    down_total = sum_rows(dot_tn(hidden, upstream)).astype(F32)
    grad_hidden = dot_nt(upstream, down_matrix)
    grad_gate = (grad_hidden * up_rows * sigmoid_gate * (1.0 + gate_rows * (1.0 - sigmoid_gate))).astype(BF)
    grad_up = (grad_hidden * silu_gate).astype(BF)
    gate_total = sum_columns(dot_tn(second_input, grad_gate), 1)
    up_total = sum_columns(dot_tn(second_input, grad_up), 1)
    grad_second = from_owner_order(sum_tokens(dot_nt(grad_gate, gate_matrix) + dot_nt(grad_up, up_matrix)))
    grad_middle = cotangent[0].astype(F32) + norm_back(grad_second * second_gain, second_normed, second_scale)
    grad_attended = gather_tokens(grad_middle.astype(BF))
    out_total = sum_rows(dot_tn(mixed, grad_attended)).astype(F32)
    grad_mixed = heads_of(dot_nt(grad_attended, out_matrix).astype(BF))
    grad_probs = jnp.einsum("shqd,shkd->shqk", grad_mixed, values, preferred_element_type=F32)
    grad_scores = (probs * (grad_probs - jnp.sum(probs * grad_probs, axis=-1, keepdims=True))).astype(BF)
    grad_queries = (jnp.einsum("shqk,shkd->shqd", grad_scores, keys, preferred_element_type=F32) * 0.125).astype(BF)
    grad_keys = (jnp.einsum("shqk,shqd->shkd", grad_scores, queries, preferred_element_type=F32) * 0.125).astype(BF)
    grad_values = jnp.einsum("shqk,shqd->shkd", probs_low, grad_mixed, preferred_element_type=F32).astype(BF)
    grad_queries = rotate(unheads(grad_queries).astype(F32).reshape(-1, group_heads, HEAD_DIM), positions, -1.0)
    grad_keys = rotate(unheads(grad_keys).astype(F32).reshape(-1, group_heads, HEAD_DIM), positions, -1.0)
    grad_projected = jnp.concatenate(
        [grad_queries.reshape(-1, part).astype(BF), grad_keys.reshape(-1, part).astype(BF), unheads(grad_values)],
        axis=1,
    )
    qkv_total = sum_columns(dot_tn(first_input, grad_projected), 3)
    grad_first = from_owner_order(sum_tokens(dot_nt(grad_projected, qkv_matrix)))
    grad_inputs = grad_middle + norm_back(grad_first * first_gain, first_normed, first_scale)

    bias_part = jnp.sum(grad_projected.astype(F32), axis=0).reshape(3, zh, -1)
    bias_whole = jnp.zeros((3, half, zh, seqs, bias_part.shape[2]), F32)
    bias_whole = lax.dynamic_update_slice(
        bias_whole, bias_part[:, None, :, None], (0, lax.axis_index("seq"), 0, lax.axis_index("zl"), 0)
    ).reshape(-1)
    count = width // own
    sums = jnp.concatenate(
        [
            jnp.sum(grad_first * first_normed, axis=0).reshape(count, own),
            jnp.sum(grad_first, axis=0).reshape(count, own),
            jnp.sum(grad_second * second_normed, axis=0).reshape(count, own),
            jnp.sum(grad_second, axis=0).reshape(count, own),
            bias_whole.reshape(count, 3 * own),
        ],
        axis=1,
    )
    sums = lax.psum_scatter(sums, ALL, scatter_dimension=0, tiled=True)[0]
    return (
        result.astype(BF)[None],
        grad_inputs[None],
        sums[:own],
        sums[own : 2 * own],
        qkv_total,
        sums[4 * own :],
        out_total,
        sums[2 * own : 3 * own],
        sums[3 * own : 4 * own],
        gate_total,
        up_total,
        down_total,
    )


MESH = pl.DeviceIdType.MESH
ROWS = 16


class Place:
    def __init__(self, zhs):
        self.s, self.zh, self.zl, self.y, self.c = (lax.axis_index(axis) for axis in ALL)
        self.zhs = zhs

    def at(self, **changed):
        return tuple(changed.get(name, getattr(self, name)) for name in ("s", "zh", "zl", "y", "c"))

    def mates(self):
        for flip_s, flip_z in ((0, 1), (1, 0), (1, 1)):
            yield (1 - self.s if flip_s else self.s), (1 - self.zl if flip_z else self.zl)

    def highs(self):
        for step in range(1, self.zhs):
            yield (self.zh + step) % self.zhs

    def greet(self):
        partners = [self.at(s=s, zl=zl) for s, zl in self.mates()]
        partners += [self.at(zh=zh) for zh in self.highs()]
        partners += [self.at(y=1 - self.y), self.at(c=1 - self.c)]
        barrier = pltpu.get_barrier_semaphore()
        for partner in partners:
            pl.semaphore_signal(barrier, inc=1, device_id=partner, device_id_type=MESH)
        pl.semaphore_wait(barrier, len(partners))


class Lines:
    def __init__(self, send, recv, local):
        self.send, self.recv, self.local = send, recv, local
        self.sent, self.copied = [], 0

    def push(self, source, target, device):
        at = len(self.sent)
        copy = pltpu.make_async_remote_copy(
            src_ref=source, dst_ref=target, send_sem=self.send.at[at], recv_sem=self.recv.at[at],
            device_id=device, device_id_type=MESH,
        )
        copy.start()
        self.sent.append(copy)
        return copy.wait_recv

    def copy(self, source, target):
        copy = pltpu.make_async_copy(source, target, self.local.at[self.copied])
        copy.start()
        self.copied += 1
        return copy.wait

    def finish(self):
        for copy in self.sent:
            copy.wait_send()


def wait_all(waits):
    for wait in waits:
        wait()


def run(*works):
    works = list(works)
    while works:
        works = [work for work in works if next(work, works) is not works]


def gather_team(lines, me, source, whole):
    waits = [lines.copy(source, whole.at[me.zl, me.s])]
    for s, zl in me.mates():
        waits.append(lines.push(source, whole.at[me.zl, me.s], me.at(s=s, zl=zl)))
    return waits


def gather_columns(lines, me, cut, whole, other):
    s = 1 - me.s if other else me.s
    mine = whole.at[me.s, me.zh, me.zl, me.y, me.c]
    waits = []
    for flip in (0, 1):
        zl = 1 - me.zl if flip else me.zl
        if other or flip:
            waits.append(lines.push(cut.at[s * 2 + zl], mine, me.at(s=s, zl=zl)))
        else:
            waits.append(lines.copy(cut.at[s * 2 + zl], mine))
    yield
    wait_all(waits)
    part = whole.at[s, me.zh, :, me.y, me.c]
    waits = [lines.push(part, part, me.at(zh=zh)) for zh in me.highs()]
    yield
    wait_all(waits)
    part = whole.at[s, :, :, me.y, me.c]
    wait = lines.push(part, part, me.at(y=1 - me.y))
    yield
    wait()
    part = whole.at[s, :, :, :, me.c]
    wait = lines.push(part, part, me.at(c=1 - me.c))
    yield
    wait()


def gather_rows(lines, me, source, whole, start, size):
    rows = pl.ds(start, size)
    mine = whole.at[me.zh, me.y, me.c, rows]
    waits = [lines.copy(source.at[rows], mine)]
    waits += [lines.push(source.at[rows], mine, me.at(zh=zh)) for zh in me.highs()]
    yield
    wait_all(waits)
    part = whole.at[:, me.y, me.c, rows]
    wait = lines.push(part, part, me.at(y=1 - me.y))
    yield
    wait()
    part = whole.at[:, :, me.c, rows]
    wait = lines.push(part, part, me.at(c=1 - me.c))
    yield
    wait()


def add_into(target, sources, result=None):
    result = target if result is None else result

    def step(at, carry):
        rows = pl.ds(pl.multiple_of(at * ROWS, ROWS), ROWS)
        total = target[rows].astype(F32)
        for source in sources:
            total = total + source[rows].astype(F32)
        result[rows] = total.astype(result.dtype)
        return carry

    lax.fori_loop(0, target.shape[0] // ROWS, step, 0)


def sum_columns(lines, me, grad, cut, buffers, other):
    mine, first, second, third = buffers
    s = 1 - me.s if other else me.s
    loaded = lines.copy(grad.at[s, :, :, :, me.c], mine)
    wait = lines.push(grad.at[s, :, :, :, 1 - me.c], first, me.at(c=1 - me.c))
    yield
    loaded()
    wait()
    for y in (1 - me.y, me.y):
        for zh in range(me.zhs):
            for zl in range(2):
                add_into(mine.at[zh, zl, y], [first.at[zh, zl, y]])
        if y is not me.y:
            wait = lines.push(mine.at[:, :, y], second, me.at(y=y))
    yield
    wait()
    waits = []
    for step, zh in enumerate([*me.highs(), me.zh]):
        for zl in range(2):
            add_into(mine.at[zh, zl, me.y], [second.at[zh, zl]])
        if step < me.zhs - 1:
            waits.append(lines.push(mine.at[zh, :, me.y], third.at[step], me.at(zh=zh)))
    yield
    wait_all(waits)
    for zl in range(2):
        add_into(mine.at[me.zh, zl, me.y], [third.at[step, zl] for step in range(me.zhs - 1)])
    waits = []
    for flip in (0, 1):
        zl = 1 - me.zl if flip else me.zl
        source, target = mine.at[me.zh, zl, me.y], cut.at[me.s * 2 + me.zl]
        if other or flip:
            waits.append(lines.push(source, target, me.at(s=s, zl=zl)))
        else:
            waits.append(lines.copy(source, target))
    yield
    wait_all(waits)


def sum_rows(lines, me, grad, total, buffers, start):
    mine, first, second, third, final = buffers
    rows = pl.ds(start, final.shape[0])
    loaded = lines.copy(grad.at[:, :, me.c, rows], mine)
    wait = lines.push(grad.at[:, :, 1 - me.c, rows], first, me.at(c=1 - me.c))
    yield
    loaded()
    wait()
    for y in (1 - me.y, me.y):
        for zh in range(me.zhs):
            add_into(mine.at[zh, y], [first.at[zh, y]])
        if y is not me.y:
            wait = lines.push(mine.at[:, y], second, me.at(y=y))
    yield
    wait()
    waits = []
    for step, zh in enumerate([*me.highs(), me.zh]):
        add_into(mine.at[zh, me.y], [second.at[zh]])
        if step < me.zhs - 1:
            waits.append(lines.push(mine.at[zh, me.y], third.at[step], me.at(zh=zh)))
    yield
    wait_all(waits)
    add_into(mine.at[me.zh, me.y], [third.at[step] for step in range(me.zhs - 1)], final)
    wait = lines.copy(final, total.at[rows])
    yield
    wait()


def sum_team(lines, me, partial, own, taken):
    waits = []
    for step, (s, zl) in enumerate(me.mates()):
        waits.append(lines.push(partial.at[zl, s], taken.at[step], me.at(s=s, zl=zl)))
    waits.append(lines.copy(partial.at[me.zl, me.s], own))
    return waits


def team_total(own, taken, rows):
    total = own[rows].astype(F32)
    for step in range(3):
        total = total + taken[step, rows].astype(F32)
    return total


def by_rows(count, body):
    def step(at, carry):
        body(pl.ds(pl.multiple_of(at * ROWS, ROWS), ROWS))
        return carry

    lax.fori_loop(0, count // ROWS, step, 0)


def halves(size):
    first = (size // ROWS + 1) // 2 * ROWS
    return ((0, first), (first, size - first)) if size > first else ((0, size),)


def enter_kernel(zhs, tokens, small, qkv_cut, out, tokens_all, small_all, qkv_all, out_all, send, recv, local):
    me, lines = Place(zhs), Lines(send, recv, local)
    me.greet()
    waits = gather_team(lines, me, tokens, tokens_all)
    run(
        gather_rows(lines, me, out, out_all, 0, out.shape[0]),
        gather_columns(lines, me, qkv_cut, qkv_all, False),
        gather_columns(lines, me, qkv_cut, qkv_all, True),
        gather_columns(lines, me, small, small_all, False),
        gather_columns(lines, me, small, small_all, True),
    )
    wait_all(waits)
    lines.finish()


def middle_kernel(
    zhs, tokens, partial, upstream, gate_cut, up_cut, down, gain, bias,
    middle, input_all, upstream_all, gate_all, up_all, down_all,
    own, taken, second, send, recv, local,
):
    me, lines = Place(zhs), Lines(send, recv, local)
    me.greet()
    waits = sum_team(lines, me, partial, own, taken)
    late = []

    def tokens_work():
        yield
        wait_all(waits)

        def body(rows):
            values = tokens[rows].astype(F32) + team_total(own, taken, rows)
            middle[rows] = values
            second[rows] = (norm_rows(values)[0] * gain[...] + bias[...]).astype(BF)

        by_rows(middle.shape[0], body)
        late.extend(gather_team(lines, me, second, input_all))
        late.extend(gather_team(lines, me, upstream, upstream_all))

    run(
        *[gather_rows(lines, me, down, down_all, start, size) for start, size in halves(down.shape[0])],
        gather_columns(lines, me, gate_cut, gate_all, False),
        gather_columns(lines, me, up_cut, up_all, False),
        tokens_work(),
        gather_columns(lines, me, gate_cut, gate_all, True),
        gather_columns(lines, me, up_cut, up_all, True),
    )
    wait_all(late)
    lines.finish()


def back_kernel(
    zhs, middle, upstream, gain, partial_down, partial_second, grad_down, grad_gate, grad_up,
    result, grad_middle, sums, attended_all, down_total, gate_cut, up_cut,
    own_down, taken_down, own_second, taken_second, attended, buffers, send, recv, local,
):
    me, lines = Place(zhs), Lines(send, recv, local)
    me.greet()
    waits = sum_team(lines, me, partial_second, own_second, taken_second)
    late = []

    def tokens_work():
        yield
        wait_all(waits)
        late.extend(sum_team(lines, me, partial_down, own_down, taken_down))
        sums[...] = jnp.zeros_like(sums)

        def body(rows):
            normed, scale_rows = norm_rows(middle[rows])
            grad = team_total(own_second, taken_second, rows)
            sums[0:1] += jnp.sum(grad * normed, axis=0, keepdims=True)
            sums[1:2] += jnp.sum(grad, axis=0, keepdims=True)
            grad = upstream[rows].astype(F32) + norm_back(grad * gain[...], normed, scale_rows)
            grad_middle[rows] = grad
            attended[rows] = grad.astype(BF)

        by_rows(middle.shape[0], body)
        shared = gather_team(lines, me, attended, attended_all)
        yield
        wait_all(late)

        def last(rows):
            result[rows] = (middle[rows] + team_total(own_down, taken_down, rows)).astype(BF)

        by_rows(middle.shape[0], last)
        yield
        wait_all(shared)

    pieces = halves(down_total.shape[0])
    run(
        *[
            sum_rows(lines, me, grad_down, down_total, buffers[at], start)
            for at, (start, size) in enumerate(pieces)
        ],
        tokens_work(),
        sum_columns(lines, me, grad_gate, gate_cut, buffers[len(pieces)], False),
        sum_columns(lines, me, grad_up, up_cut, buffers[len(pieces) + 1], False),
        sum_columns(lines, me, grad_gate, gate_cut, buffers[len(pieces) + 2], True),
        sum_columns(lines, me, grad_up, up_cut, buffers[len(pieces) + 3], True),
    )
    lines.finish()


def leave_kernel(
    zhs, tokens, grad_middle, gain, partial, vector, grad_out, grad_qkv,
    grad_inputs, sums, out_total, qkv_cut,
    own, taken, steps, buffers, send, recv, local,
):
    me, lines = Place(zhs), Lines(send, recv, local)
    me.greet()
    waits = sum_team(lines, me, partial, own, taken)

    def tokens_work():
        yield
        wait_all(waits)
        steps[0] = vector[...]

        def body(rows):
            normed, scale_rows = norm_rows(tokens[rows].astype(F32))
            grad = team_total(own, taken, rows)
            steps[0, 0:1] += jnp.sum(grad * normed, axis=0, keepdims=True)
            steps[0, 1:2] += jnp.sum(grad, axis=0, keepdims=True)
            grad_inputs[rows] = grad_middle[rows] + norm_back(grad * gain[...], normed, scale_rows)

        by_rows(tokens.shape[0], body)
        groups = [
            [me.at(s=1 - me.s)], [me.at(zl=1 - me.zl)], [me.at(c=1 - me.c)], [me.at(y=1 - me.y)],
            [me.at(zh=zh) for zh in me.highs()],
        ]
        at = 0
        for group in groups:
            arrived = [
                lines.push(steps.at[at], steps.at[at + 1 + number], device)
                for number, device in enumerate(group)
            ]
            yield
            wait_all(arrived)
            total = steps[at]
            for number in range(len(group)):
                total = total + steps[at + 1 + number]
            at += len(group) + 1
            steps[at] = total
        sums[...] = steps[at]

    pieces = halves(out_total.shape[0])
    run(
        *[
            sum_rows(lines, me, grad_out, out_total, buffers[at], start)
            for at, (start, size) in enumerate(pieces)
        ],
        tokens_work(),
        sum_columns(lines, me, grad_qkv, qkv_cut, buffers[len(pieces)], False),
        sum_columns(lines, me, grad_qkv, qkv_cut, buffers[len(pieces) + 1], True),
    )
    lines.finish()


def row_buffers(zhs, size, width):
    return tuple(
        pltpu.VMEM(shape + (size, width), BF) for shape in ((zhs, 2), (zhs, 2), (zhs,), (zhs - 1,))
    ) + (pltpu.VMEM((size, width), F32),)


def column_buffers(zhs, own, columns):
    return tuple(
        pltpu.VMEM(shape + (own, columns), BF)
        for shape in ((zhs, 2, 2), (zhs, 2, 2), (zhs, 2), (zhs - 1, 2))
    )


IN_HBM = pl.BlockSpec(memory_space=pl.ANY)
IN_VMEM = pl.BlockSpec(memory_space=pltpu.VMEM)


def call(kernel, zhs, number, inputs, outputs, scratch, copies, locals_, limit):
    return pl.pallas_call(
        lambda *refs: kernel(zhs, *refs),
        out_shape=[jax.ShapeDtypeStruct(shape, kind) for shape, kind, _ in outputs],
        in_specs=[spec for _, spec in inputs],
        out_specs=[spec for _, _, spec in outputs],
        scratch_shapes=[
            *scratch,
            pltpu.SemaphoreType.DMA((copies,)),
            pltpu.SemaphoreType.DMA((copies,)),
            pltpu.SemaphoreType.DMA((locals_,)),
        ],
        compiler_params=pltpu.CompilerParams(
            collective_id=number, has_side_effects=True, vmem_limit_bytes=limit << 20
        ),
    )(*[array for array, _ in inputs])


def per_device(
    tokens, cotangent, norm1_gain, norm1_bias, qkv_weight, qkv_bias, out_weight,
    norm2_gain, norm2_bias, gate_weight, up_weight, down_weight,
):
    zh = lax.axis_size("zh")
    rows = tokens.shape[1]
    width = tokens.shape[2]
    own = qkv_weight.shape[0]
    ff = gate_weight.shape[1]
    ff_own = down_weight.shape[0]
    half = lax.axis_size("seq")
    length = rows * half
    seqs = lax.axis_size("zl")
    team = half * seqs
    part = width // team
    ff_part = ff // team
    devices = width // own
    tokens, cotangent = tokens[0], cotangent[0]
    index = (lax.axis_index("seq") * (devices // half)
             + ((lax.axis_index("zh") * 2 + lax.axis_index("zl")) * 2 + lax.axis_index("y")) * 2
             + lax.axis_index("c"))

    def cut_columns(shard, parts):
        block = shard.shape[1] // parts // (half * zh * seqs)
        cut = shard.reshape(own, parts, half, zh, seqs, block).transpose(2, 4, 0, 1, 3, 5)
        return cut.reshape(team, own, parts * zh * block)

    def join_columns(cut, parts):
        block = cut.shape[2] // parts // zh
        cut = cut.reshape(half, seqs, own, parts, zh, block).transpose(2, 3, 0, 4, 1, 5)
        return cut.reshape(own, -1).astype(F32)

    def mine_columns(whole, parts):
        block = whole.shape[0] // parts // (half * zh * seqs)
        cut = whole.reshape(parts, half, zh, seqs, block)
        cut = lax.dynamic_index_in_dim(cut, lax.axis_index("seq"), 1, keepdims=False)
        cut = lax.dynamic_index_in_dim(cut, lax.axis_index("zl"), 2, keepdims=False)
        return cut.reshape(-1)

    small = jnp.concatenate([norm1_gain, norm1_bias, norm2_gain, norm2_bias, qkv_bias]).astype(F32)
    small = jnp.pad(small, (0, 1024 - small.shape[0])).reshape(8, 128)
    small = jnp.broadcast_to(small, (team, 8, 128))
    token_shape = (seqs, half, rows, width)
    owners = (half, zh, seqs, 2, 2)
    tokens_all, small_all, qkv_all, out_all = call(
        enter_kernel, zh, 0,
        [(tokens, IN_HBM), (small, IN_HBM), (cut_columns(qkv_weight, 3), IN_HBM), (out_weight, IN_HBM)],
        [
            (token_shape, BF, IN_HBM),
            (owners + (8, 128), F32, IN_HBM),
            (owners + (own, 3 * part), BF, IN_HBM),
            ((zh, 2, 2, own, width), BF, IN_HBM),
        ],
        [], 12 + 5 * (zh + 4), 8, 16,
    )
    small = small_all.reshape(devices, 1024)
    first_gain = small[:, :own].reshape(1, width)
    first_bias = small[:, own : 2 * own].reshape(1, width)
    second_gain = small[:, 2 * own : 3 * own].reshape(1, width)
    second_bias = small[:, 3 * own : 4 * own].reshape(1, width)
    qkv_offset = mine_columns(small[:, 4 * own : 7 * own].reshape(-1), 3)
    qkv_matrix = qkv_all.reshape(width, 3 * part)
    out_matrix = out_all.reshape(part, width)

    first_input = (
        norm_rows(tokens_all.reshape(-1, width).astype(F32))[0] * first_gain + first_bias
    ).astype(BF)
    projected = dot(first_input, qkv_matrix) + qkv_offset
    group_heads = part // HEAD_DIM
    positions = jnp.tile(jnp.arange(length, dtype=jnp.int32), seqs)

    def heads_of(values):
        return values.reshape(seqs, length, group_heads, HEAD_DIM).transpose(0, 2, 1, 3)

    def unheads(values):
        return values.transpose(0, 2, 1, 3).reshape(seqs * length, part)

    queries = heads_of(rotate(projected[:, :part].reshape(-1, group_heads, HEAD_DIM), positions, 1.0).astype(BF))
    keys = heads_of(rotate(projected[:, part : 2 * part].reshape(-1, group_heads, HEAD_DIM), positions, 1.0).astype(BF))
    values = heads_of(projected[:, 2 * part :].astype(BF))
    causal = jnp.arange(length)[:, None] >= jnp.arange(length)[None, :]
    scores = jnp.einsum("shqd,shkd->shqk", queries, keys, preferred_element_type=F32) * 0.125
    scores = jnp.where(causal, scores, -1e30)
    highest = jnp.max(scores, axis=-1, keepdims=True)
    exponent = jnp.exp(scores - highest)
    probs = exponent / jnp.sum(exponent, axis=-1, keepdims=True)
    probs_low = probs.astype(BF)
    mixed = unheads(jnp.einsum("shqk,shkd->shqd", probs_low, values, preferred_element_type=F32).astype(BF))
    partial = dot(mixed, out_matrix).astype(BF).reshape(token_shape)

    limit = 48
    token_scratch = [pltpu.VMEM((rows, width), BF), pltpu.VMEM((3, rows, width), BF)]
    middle, input_all, upstream_all, gate_all, up_all, down_all = call(
        middle_kernel, zh, 1,
        [
            (tokens, IN_VMEM), (partial, IN_HBM), (cotangent, IN_HBM),
            (cut_columns(gate_weight, 1), IN_HBM), (cut_columns(up_weight, 1), IN_HBM),
            (down_weight, IN_HBM), (second_gain, IN_VMEM), (second_bias, IN_VMEM),
        ],
        [
            ((rows, width), F32, IN_VMEM),
            (token_shape, BF, IN_HBM),
            (token_shape, BF, IN_HBM),
            (owners + (own, ff_part), BF, IN_HBM),
            (owners + (own, ff_part), BF, IN_HBM),
            ((zh, 2, 2, ff_own, width), BF, IN_HBM),
        ],
        [*token_scratch, pltpu.VMEM((rows, width), BF)],
        9 + 6 * (zh + 4), 16, limit,
    )
    second_input = input_all.reshape(-1, width)
    upstream = upstream_all.reshape(-1, width)
    gate_matrix = gate_all.reshape(width, ff_part)
    up_matrix = up_all.reshape(width, ff_part)
    down_matrix = down_all.reshape(ff_part, width)
    gate_rows = dot(second_input, gate_matrix)
    up_rows = dot(second_input, up_matrix)
    sigmoid_gate = jax.nn.sigmoid(gate_rows)
    silu_gate = gate_rows * sigmoid_gate
    hidden = (silu_gate * up_rows).astype(BF)
    partial_down = dot(hidden, down_matrix).astype(BF).reshape(token_shape)

    grad_down = dot_tn(hidden, upstream).astype(BF).reshape(down_all.shape)
    grad_hidden = dot_nt(upstream, down_matrix)
    grad_gate = (grad_hidden * up_rows * sigmoid_gate * (1.0 + gate_rows * (1.0 - sigmoid_gate))).astype(BF)
    grad_up = (grad_hidden * silu_gate).astype(BF)
    partial_second = (dot_nt(grad_gate, gate_matrix) + dot_nt(grad_up, up_matrix)).astype(BF).reshape(token_shape)
    pieces = [size for _, size in halves(ff_own)]
    result, grad_middle, second_sums, attended_all, down_total, gate_cut, up_cut = call(
        back_kernel, zh, 2,
        [
            (middle, IN_VMEM), (cotangent, IN_VMEM), (second_gain, IN_VMEM),
            (partial_down, IN_HBM), (partial_second, IN_HBM), (grad_down, IN_HBM),
            (dot_tn(second_input, grad_gate).astype(BF).reshape(gate_all.shape), IN_HBM),
            (dot_tn(second_input, grad_up).astype(BF).reshape(up_all.shape), IN_HBM),
        ],
        [
            ((rows, width), BF, IN_VMEM),
            ((rows, width), F32, IN_VMEM),
            ((8, width), F32, IN_VMEM),
            (token_shape, BF, IN_HBM),
            ((ff_own, width), F32, IN_HBM),
            ((team, own, ff_part), BF, IN_HBM),
            ((team, own, ff_part), BF, IN_HBM),
        ],
        [
            *token_scratch, *token_scratch, pltpu.VMEM((rows, width), BF),
            [row_buffers(zh, size, width) for size in pieces]
            + [column_buffers(zh, own, ff_part) for _ in range(4)],
        ],
        9 + 6 * (zh + 4), 20, limit,
    )

    grad_attended = attended_all.reshape(-1, width)
    grad_out = dot_tn(mixed, grad_attended).astype(BF).reshape(out_all.shape)
    grad_mixed = heads_of(dot_nt(grad_attended, out_matrix).astype(BF))
    grad_probs = jnp.einsum("shqd,shkd->shqk", grad_mixed, values, preferred_element_type=F32)
    grad_scores = (probs * (grad_probs - jnp.sum(probs * grad_probs, axis=-1, keepdims=True))).astype(BF)
    grad_queries = (jnp.einsum("shqk,shkd->shqd", grad_scores, keys, preferred_element_type=F32) * 0.125).astype(BF)
    grad_keys = (jnp.einsum("shqk,shqd->shkd", grad_scores, queries, preferred_element_type=F32) * 0.125).astype(BF)
    grad_values = jnp.einsum("shqk,shqd->shkd", probs_low, grad_mixed, preferred_element_type=F32).astype(BF)
    grad_queries = rotate(unheads(grad_queries).astype(F32).reshape(-1, group_heads, HEAD_DIM), positions, -1.0)
    grad_keys = rotate(unheads(grad_keys).astype(F32).reshape(-1, group_heads, HEAD_DIM), positions, -1.0)
    grad_projected = jnp.concatenate(
        [grad_queries.reshape(-1, part).astype(BF), grad_keys.reshape(-1, part).astype(BF), unheads(grad_values)],
        axis=1,
    )
    partial_first = dot_nt(grad_projected, qkv_matrix).astype(BF).reshape(token_shape)
    bias_part = jnp.sum(grad_projected.astype(F32), axis=0).reshape(3, zh, -1)
    bias_whole = jnp.zeros((3, half, zh, seqs, bias_part.shape[2]), F32)
    bias_whole = lax.dynamic_update_slice(
        bias_whole, bias_part[:, None, :, None], (0, lax.axis_index("seq"), 0, lax.axis_index("zl"), 0)
    ).reshape(3, width)
    vector = jnp.concatenate(
        [jnp.zeros((2, width), F32), second_sums[:2], bias_whole, jnp.zeros((1, width), F32)], axis=0
    )
    pieces = [size for _, size in halves(own)]
    grad_inputs, sums, out_total, qkv_cut = call(
        leave_kernel, zh, 3,
        [
            (tokens, IN_VMEM), (grad_middle, IN_VMEM), (first_gain, IN_VMEM),
            (partial_first, IN_HBM), (vector, IN_VMEM), (grad_out, IN_HBM),
            (dot_tn(first_input, grad_projected).astype(BF).reshape(qkv_all.shape), IN_HBM),
        ],
        [
            ((rows, width), F32, IN_VMEM),
            ((8, width), F32, IN_VMEM),
            ((own, width), F32, IN_HBM),
            ((team, own, 3 * part), BF, IN_HBM),
        ],
        [
            *token_scratch, pltpu.VMEM((zh + 9, 8, width), F32),
            [row_buffers(zh, size, width) for size in pieces]
            + [column_buffers(zh, own, 3 * part) for _ in range(2)],
        ],
        3 + zh + 3 + 4 * (zh + 4), 12, limit,
    )

    def mine(vector_row, size):
        return lax.dynamic_slice_in_dim(vector_row, index * size, size, 0)

    return (
        result[None],
        grad_inputs[None],
        mine(sums[0], own),
        mine(sums[1], own),
        join_columns(qkv_cut, 3),
        mine(sums[4:7].reshape(-1), 3 * own),
        out_total,
        mine(sums[2], own),
        mine(sums[3], own),
        join_columns(gate_cut, 1),
        join_columns(up_cut, 1),
        down_total,
    )


def solution(mesh):
    half, shards = mesh.shape["seq"], mesh.shape["shard"]
    fine = jax.sharding.Mesh(mesh.devices.reshape(half, shards // 8, 2, 2, 2), ALL)
    token = P(("zh", "zl", "y", "c"), "seq", None)
    row = P(ALL)

    def program(*arguments):
        whole_tiles = arguments[-1].shape[0] // (half * shards) % ROWS == 0
        return jax.shard_map(
            per_device if whole_tiles else plain_device,
            mesh=fine,
            in_specs=(token, token) + (row,) * 10,
            out_specs=(token, token) + (row,) * 10,
            check_vma=False,
        )(*arguments)

    return program
```

```python
import jax
import jax.numpy as jnp
import numpy as np
from jax import lax
from jax.experimental import pallas as pl
from jax.experimental.pallas import tpu as pltpu
from jax.sharding import PartitionSpec as P

HEADS = 32
HEAD_DIM = 64
ROTARY = 16
TEAM = ("seq", "zl")
PEERS = ("zh", "y", "c")
ALL = ("seq", "zh", "zl", "y", "c")
BF = jnp.bfloat16
F32 = jnp.float32


def norm_rows(values):
    centre = jnp.mean(values, axis=-1, keepdims=True)
    centred = values - centre
    spread = jnp.mean(centred * centred, axis=-1, keepdims=True)
    scale_rows = lax.rsqrt(spread + 1e-05)
    return (centred * scale_rows, scale_rows)


def norm_back(grad_normed, normed, scale_rows):
    return scale_rows * (
        grad_normed
        - jnp.mean(grad_normed, axis=-1, keepdims=True)
        - normed * jnp.mean(grad_normed * normed, axis=-1, keepdims=True)
    )


def rotate(values, positions, direction):
    halves = ROTARY // 2
    frequency = 10000.0 ** (-2.0 * jnp.arange(halves, dtype=F32) / ROTARY)
    angles = positions.astype(F32)[:, None] * frequency[None, :]
    cosine_table = jnp.cos(angles)[:, None, :]
    sine_table = jnp.sin(angles)[:, None, :] * direction
    first_half = values[..., :halves]
    second_half = values[..., halves:ROTARY]
    return jnp.concatenate(
        [
            first_half * cosine_table - second_half * sine_table,
            second_half * cosine_table + first_half * sine_table,
            values[..., ROTARY:],
        ],
        axis=-1,
    )


def dot(left, right):
    return jnp.dot(left, right, preferred_element_type=F32)


def dot_nt(left, right):
    return lax.dot_general(left, right, (((1,), (1,)), ((), ())), preferred_element_type=F32)


def dot_tn(left, right):
    return lax.dot_general(left, right, (((0,), (0,)), ((), ())), preferred_element_type=F32)


def plain_device(
    tokens, cotangent, norm1_gain, norm1_bias, qkv_weight, qkv_bias, out_weight,
    norm2_gain, norm2_bias, gate_weight, up_weight, down_weight,
):
    zh = lax.axis_size("zh")
    rows = tokens.shape[1]
    width = tokens.shape[2]
    own = qkv_weight.shape[0]
    ff = gate_weight.shape[1]
    half = lax.axis_size("seq")
    length = rows * half
    team = half * lax.axis_size("zl")
    seqs = lax.axis_size("zl")

    def cut_columns(shard, parts):
        block = shard.shape[1] // parts // (half * zh * seqs)
        cut = shard.reshape(own, parts, half, zh, seqs, block).transpose(2, 4, 0, 1, 3, 5)
        return cut.reshape(team, own, parts * zh * block)

    def join_columns(cut, parts):
        block = cut.shape[2] // parts // zh
        cut = cut.reshape(half, seqs, own, parts, zh, block).transpose(2, 3, 0, 4, 1, 5)
        return cut.reshape(own, -1)

    def mine_columns(whole, parts):
        block = whole.shape[0] // parts // (half * zh * seqs)
        cut = whole.reshape(parts, half, zh, seqs, block)
        cut = lax.dynamic_index_in_dim(cut, lax.axis_index("seq"), 1, keepdims=False)
        cut = lax.dynamic_index_in_dim(cut, lax.axis_index("zl"), 2, keepdims=False)
        return cut.reshape(-1)

    def to_owner_order(values):
        n = values.shape[0]
        return values.reshape(n, half, zh, seqs, 4, own).transpose(0, 2, 4, 1, 3, 5).reshape(n, width)

    def from_owner_order(values):
        n = values.shape[0]
        return values.reshape(n, zh, 4, half, seqs, own).transpose(0, 3, 1, 4, 2, 5).reshape(n, width)

    def gather_columns(shard, parts):
        cut = cut_columns(shard, parts)
        cut = lax.all_to_all(cut, TEAM, split_axis=0, concat_axis=0, tiled=True)
        return lax.all_gather(cut.reshape(team * own, -1), PEERS, axis=0, tiled=True)

    def gather_rows(shard):
        return lax.all_gather(shard, PEERS, axis=0, tiled=True)

    def gather_tokens(values):
        return lax.all_gather(values, ("zl", "seq"), axis=0, tiled=True)

    def sum_tokens(values):
        return lax.psum_scatter(values.astype(BF), ("zl", "seq"), scatter_dimension=0, tiled=True).astype(F32)

    def sum_rows(values):
        return lax.psum_scatter(values.astype(BF), PEERS, scatter_dimension=0, tiled=True)

    def sum_columns(values, parts):
        part = sum_rows(values).reshape(team, own, -1)
        part = lax.all_to_all(part, TEAM, split_axis=0, concat_axis=0, tiled=True)
        return join_columns(part, parts).astype(F32)

    small = jnp.concatenate([norm1_gain, norm1_bias, norm2_gain, norm2_bias, qkv_bias])
    small = lax.all_gather(small, ALL, axis=0, tiled=False)
    first_gain = small[:, :own].reshape(-1).astype(F32)
    first_bias = small[:, own : 2 * own].reshape(-1).astype(F32)
    second_gain = small[:, 2 * own : 3 * own].reshape(-1).astype(F32)
    second_bias = small[:, 3 * own : 4 * own].reshape(-1).astype(F32)
    qkv_offset = mine_columns(small[:, 4 * own :].reshape(-1), 3).astype(F32)

    inputs = tokens[0].astype(F32)
    first_normed, first_scale = norm_rows(inputs)
    first_own = to_owner_order((first_normed * first_gain + first_bias).astype(BF))
    first_input = gather_tokens(first_own)
    qkv_matrix = gather_columns(qkv_weight, 3)
    out_matrix = gather_rows(out_weight)
    gate_matrix = gather_columns(gate_weight, 1)
    up_matrix = gather_columns(up_weight, 1)
    down_matrix = gather_rows(down_weight)
    upstream = gather_tokens(cotangent[0])

    projected = dot(first_input, qkv_matrix) + qkv_offset
    part = width // team
    group_heads = part // HEAD_DIM
    positions = jnp.tile(jnp.arange(length, dtype=jnp.int32), seqs)

    def heads_of(values):
        return values.reshape(seqs, length, group_heads, HEAD_DIM).transpose(0, 2, 1, 3)

    def unheads(values):
        return values.transpose(0, 2, 1, 3).reshape(seqs * length, part)

    queries = heads_of(rotate(projected[:, :part].reshape(-1, group_heads, HEAD_DIM), positions, 1.0).astype(BF))
    keys = heads_of(rotate(projected[:, part : 2 * part].reshape(-1, group_heads, HEAD_DIM), positions, 1.0).astype(BF))
    values = heads_of(projected[:, 2 * part :].astype(BF))
    causal = jnp.arange(length)[:, None] >= jnp.arange(length)[None, :]
    scores = jnp.einsum("shqd,shkd->shqk", queries, keys, preferred_element_type=F32) * 0.125
    scores = jnp.where(causal, scores, -1e30)
    highest = jnp.max(scores, axis=-1, keepdims=True)
    exponent = jnp.exp(scores - highest)
    probs = exponent / jnp.sum(exponent, axis=-1, keepdims=True)
    probs_low = probs.astype(BF)
    mixed = unheads(jnp.einsum("shqk,shkd->shqd", probs_low, values, preferred_element_type=F32).astype(BF))
    middle = inputs + sum_tokens(dot(mixed, out_matrix))

    second_normed, second_scale = norm_rows(middle)
    second_own = to_owner_order((second_normed * second_gain + second_bias).astype(BF))
    second_input = gather_tokens(second_own)
    gate_rows = dot(second_input, gate_matrix)
    up_rows = dot(second_input, up_matrix)
    sigmoid_gate = jax.nn.sigmoid(gate_rows)
    silu_gate = gate_rows * sigmoid_gate
    hidden = (silu_gate * up_rows).astype(BF)
    result = middle + sum_tokens(dot(hidden, down_matrix))

    down_total = sum_rows(dot_tn(hidden, upstream)).astype(F32)
    grad_hidden = dot_nt(upstream, down_matrix)
    grad_gate = (grad_hidden * up_rows * sigmoid_gate * (1.0 + gate_rows * (1.0 - sigmoid_gate))).astype(BF)
    grad_up = (grad_hidden * silu_gate).astype(BF)
    gate_total = sum_columns(dot_tn(second_input, grad_gate), 1)
    up_total = sum_columns(dot_tn(second_input, grad_up), 1)
    grad_second = from_owner_order(sum_tokens(dot_nt(grad_gate, gate_matrix) + dot_nt(grad_up, up_matrix)))
    grad_middle = cotangent[0].astype(F32) + norm_back(grad_second * second_gain, second_normed, second_scale)
    grad_attended = gather_tokens(grad_middle.astype(BF))
    out_total = sum_rows(dot_tn(mixed, grad_attended)).astype(F32)
    grad_mixed = heads_of(dot_nt(grad_attended, out_matrix).astype(BF))
    grad_probs = jnp.einsum("shqd,shkd->shqk", grad_mixed, values, preferred_element_type=F32)
    grad_scores = (probs * (grad_probs - jnp.sum(probs * grad_probs, axis=-1, keepdims=True))).astype(BF)
    grad_queries = (jnp.einsum("shqk,shkd->shqd", grad_scores, keys, preferred_element_type=F32) * 0.125).astype(BF)
    grad_keys = (jnp.einsum("shqk,shqd->shkd", grad_scores, queries, preferred_element_type=F32) * 0.125).astype(BF)
    grad_values = jnp.einsum("shqk,shqd->shkd", probs_low, grad_mixed, preferred_element_type=F32).astype(BF)
    grad_queries = rotate(unheads(grad_queries).astype(F32).reshape(-1, group_heads, HEAD_DIM), positions, -1.0)
    grad_keys = rotate(unheads(grad_keys).astype(F32).reshape(-1, group_heads, HEAD_DIM), positions, -1.0)
    grad_projected = jnp.concatenate(
        [grad_queries.reshape(-1, part).astype(BF), grad_keys.reshape(-1, part).astype(BF), unheads(grad_values)],
        axis=1,
    )
    qkv_total = sum_columns(dot_tn(first_input, grad_projected), 3)
    grad_first = from_owner_order(sum_tokens(dot_nt(grad_projected, qkv_matrix)))
    grad_inputs = grad_middle + norm_back(grad_first * first_gain, first_normed, first_scale)

    bias_part = jnp.sum(grad_projected.astype(F32), axis=0).reshape(3, zh, -1)
    bias_whole = jnp.zeros((3, half, zh, seqs, bias_part.shape[2]), F32)
    bias_whole = lax.dynamic_update_slice(
        bias_whole, bias_part[:, None, :, None], (0, lax.axis_index("seq"), 0, lax.axis_index("zl"), 0)
    ).reshape(-1)
    count = width // own
    sums = jnp.concatenate(
        [
            jnp.sum(grad_first * first_normed, axis=0).reshape(count, own),
            jnp.sum(grad_first, axis=0).reshape(count, own),
            jnp.sum(grad_second * second_normed, axis=0).reshape(count, own),
            jnp.sum(grad_second, axis=0).reshape(count, own),
            bias_whole.reshape(count, 3 * own),
        ],
        axis=1,
    )
    sums = lax.psum_scatter(sums, ALL, scatter_dimension=0, tiled=True)[0]
    return (
        result.astype(BF)[None],
        grad_inputs[None],
        sums[:own],
        sums[own : 2 * own],
        qkv_total,
        sums[4 * own :],
        out_total,
        sums[2 * own : 3 * own],
        sums[3 * own : 4 * own],
        gate_total,
        up_total,
        down_total,
    )


MESH = pl.DeviceIdType.MESH
ROWS = 16
QKV_PARTS, OUT_PARTS, FF_PARTS, DOWN_PARTS = 2, 2, 2, 4


class Place:
    def __init__(self, zhs):
        self.s, self.zh, self.zl, self.y, self.c = (lax.axis_index(axis) for axis in ALL)
        self.zhs = zhs

    def at(self, **changed):
        return tuple(changed.get(name, getattr(self, name)) for name in ("s", "zh", "zl", "y", "c"))

    def mates(self):
        for flip_s, flip_z in ((0, 1), (1, 0), (1, 1)):
            yield (1 - self.s if flip_s else self.s), (1 - self.zl if flip_z else self.zl)

    def highs(self):
        for step in range(1, self.zhs):
            yield (self.zh + step) % self.zhs

    def greet(self):
        partners = [self.at(s=s, zl=zl) for s, zl in self.mates()]
        partners += [self.at(zh=zh) for zh in self.highs()]
        partners += [self.at(y=1 - self.y), self.at(c=1 - self.c)]
        barrier = pltpu.get_barrier_semaphore()
        for partner in partners:
            pl.semaphore_signal(barrier, inc=1, device_id=partner, device_id_type=MESH)
        pl.semaphore_wait(barrier, len(partners))


class Lines:
    def __init__(self, send, recv, local):
        self.send, self.recv, self.local = send, recv, local
        self.sent, self.copied = [], 0

    def push(self, source, target, device):
        at = len(self.sent)
        copy = pltpu.make_async_remote_copy(
            src_ref=source, dst_ref=target, send_sem=self.send.at[at], recv_sem=self.recv.at[at],
            device_id=device, device_id_type=MESH,
        )
        copy.start()
        self.sent.append(copy)
        return copy.wait_recv

    def copy(self, source, target):
        copy = pltpu.make_async_copy(source, target, self.local.at[self.copied])
        copy.start()
        self.copied += 1
        return copy.wait

    def finish(self):
        for copy in self.sent:
            copy.wait_send()


def wait_all(waits):
    for wait in waits:
        wait()


def run(*plan, spawned=()):
    plan, opened, turn = list(plan), [], 0
    while plan or opened or spawned:
        opened = [*spawned, *[work for start, work in plan if start == turn], *opened]
        if spawned:
            spawned.clear()
        plan = [item for item in plan if item[0] != turn]
        opened = [work for work in opened if next(work, run) is not run]
        turn += 1


def rest(turns):
    for _ in range(turns):
        yield


def gather_team(lines, me, source, whole, turns):
    mine, other = whole.at[me.zl, me.s], whole.at[1 - me.zl, me.s]
    waits = [
        lines.copy(source, mine),
        lines.push(source, mine, me.at(s=1 - me.s)),
    ]
    across = lines.push(source, mine, me.at(zl=1 - me.zl))
    yield from rest(turns)
    across()
    waits.append(lines.push(other, other, me.at(s=1 - me.s)))
    yield from rest(turns)
    wait_all(waits)


def gather_columns(lines, me, cut, whole, piece):
    other, start, size = piece
    s, columns = 1 - me.s if other else me.s, pl.ds(start, size)
    mine = whole.at[me.s, me.zh, me.zl, me.y, me.c, :, columns]
    waits = []
    for flip in (0, 1):
        zl = 1 - me.zl if flip else me.zl
        if other or flip:
            waits.append(lines.push(cut.at[s * 2 + zl, :, columns], mine, me.at(s=s, zl=zl)))
        else:
            waits.append(lines.copy(cut.at[s * 2 + zl, :, columns], mine))
    yield
    wait_all(waits)
    part = whole.at[s, me.zh, :, me.y, me.c, :, columns]
    waits = [lines.push(part, part, me.at(zh=zh)) for zh in me.highs()]
    yield
    wait_all(waits)
    part = whole.at[s, :, :, me.y, me.c, :, columns]
    wait = lines.push(part, part, me.at(y=1 - me.y))
    yield
    wait()
    part = whole.at[s, :, :, :, me.c, :, columns]
    wait = lines.push(part, part, me.at(c=1 - me.c))
    yield
    wait()


def gather_rows(lines, me, source, whole, start, size):
    rows = pl.ds(start, size)
    mine = whole.at[me.zh, me.y, me.c, rows]
    waits = [lines.copy(source.at[rows], mine)]
    waits += [lines.push(source.at[rows], mine, me.at(zh=zh)) for zh in me.highs()]
    yield
    wait_all(waits)
    part = whole.at[:, me.y, me.c, rows]
    wait = lines.push(part, part, me.at(y=1 - me.y))
    yield
    wait()
    part = whole.at[:, :, me.c, rows]
    wait = lines.push(part, part, me.at(c=1 - me.c))
    yield
    wait()


def add_into(target, sources, result=None):
    result = target if result is None else result

    def step(at, carry):
        rows = pl.ds(pl.multiple_of(at * ROWS, ROWS), ROWS)
        total = target[rows].astype(F32)
        for source in sources:
            total = total + source[rows].astype(F32)
        result[rows] = total.astype(result.dtype)
        return carry

    lax.fori_loop(0, target.shape[0] // ROWS, step, 0)


def sum_columns(lines, me, grad, cut, buffers, piece):
    mine, first, second, third = buffers
    other, start, size = piece
    s, columns = 1 - me.s if other else me.s, pl.ds(start, size)
    loaded = lines.copy(grad.at[s, :, :, :, me.c, :, columns], mine)
    wait = lines.push(grad.at[s, :, :, :, 1 - me.c, :, columns], first, me.at(c=1 - me.c))
    yield
    loaded()
    wait()
    for y in (1 - me.y, me.y):
        for zh in range(me.zhs):
            for zl in range(2):
                add_into(mine.at[zh, zl, y], [first.at[zh, zl, y]])
        if y is not me.y:
            wait = lines.push(mine.at[:, :, y], second, me.at(y=y))
    yield
    wait()
    waits = []
    for step, zh in enumerate([*me.highs(), me.zh]):
        for zl in range(2):
            add_into(mine.at[zh, zl, me.y], [second.at[zh, zl]])
        if step < me.zhs - 1:
            waits.append(lines.push(mine.at[zh, :, me.y], third.at[step], me.at(zh=zh)))
    yield
    wait_all(waits)
    for zl in range(2):
        add_into(mine.at[me.zh, zl, me.y], [third.at[step, zl] for step in range(me.zhs - 1)])
    waits = []
    for flip in (0, 1):
        zl = 1 - me.zl if flip else me.zl
        source, target = mine.at[me.zh, zl, me.y], cut.at[me.s * 2 + me.zl, :, columns]
        if other or flip:
            waits.append(lines.push(source, target, me.at(s=s, zl=zl)))
        else:
            waits.append(lines.copy(source, target))
    yield
    wait_all(waits)


def sum_rows(lines, me, grad, total, buffers, start):
    mine, first, second, third, final = buffers
    rows = pl.ds(start, final.shape[0])
    loaded = lines.copy(grad.at[:, :, me.c, rows], mine)
    wait = lines.push(grad.at[:, :, 1 - me.c, rows], first, me.at(c=1 - me.c))
    yield
    loaded()
    wait()
    for y in (1 - me.y, me.y):
        for zh in range(me.zhs):
            add_into(mine.at[zh, y], [first.at[zh, y]])
        if y is not me.y:
            wait = lines.push(mine.at[:, y], second, me.at(y=y))
    yield
    wait()
    waits = []
    for step, zh in enumerate([*me.highs(), me.zh]):
        add_into(mine.at[zh, me.y], [second.at[zh]])
        if step < me.zhs - 1:
            waits.append(lines.push(mine.at[zh, me.y], third.at[step], me.at(zh=zh)))
    yield
    wait_all(waits)
    add_into(mine.at[me.zh, me.y], [third.at[step] for step in range(me.zhs - 1)], final)
    wait = lines.copy(final, total.at[rows])
    yield
    wait()


def sum_team(lines, me, partial, own, passed, taken, turns):
    first = [
        lines.copy(partial.at[1 - me.zl, me.s], passed),
        lines.push(partial.at[1 - me.zl, 1 - me.s], taken.at[0], me.at(s=1 - me.s)),
    ]
    waits = [
        lines.push(partial.at[me.zl, 1 - me.s], taken.at[1], me.at(s=1 - me.s)),
        lines.copy(partial.at[me.zl, me.s], own),
    ]
    yield from rest(turns)
    wait_all(first)
    add_into(passed, [taken.at[0]])
    waits.append(lines.push(passed, taken.at[2], me.at(zl=1 - me.zl)))
    yield from rest(turns)
    wait_all(waits)


def team_total(own, taken, rows):
    return own[rows].astype(F32) + taken[1, rows].astype(F32) + taken[2, rows].astype(F32)


def by_rows(count, body):
    def step(at, carry):
        body(pl.ds(pl.multiple_of(at * ROWS, ROWS), ROWS))
        return carry

    lax.fori_loop(0, count // ROWS, step, 0)


def row_pieces(size, parts):
    tiles, pieces, start = size // ROWS, [], 0
    for part in range(parts):
        count = (tiles * (part + 1) // parts - tiles * part // parts) * ROWS
        pieces.append((start, count))
        start += count
    return pieces


def column_pieces(columns, parts):
    lanes, pieces, start = columns // 128, [], 0
    for part in range(parts):
        size = (lanes * (part + 1) // parts - lanes * part // parts) * 128
        pieces.append((start, size))
        start += size
    return [(other, *piece) for other in (False, True) for piece in pieces]


def turn_pairs(values, tables, sign):
    return (
        values * tables[0]
        + pltpu.roll(values, 128 - ROTARY // 2, 1) * (tables[1] * sign)
        + pltpu.roll(values, ROTARY // 2, 1) * (tables[2] * sign)
    )


def rotary_tables(length):
    lane = np.arange(128) % HEAD_DIM
    halves = ROTARY // 2
    frequency = np.float32(10000.0) ** (np.float32(-2.0) * np.arange(halves, dtype=np.float32) / np.float32(ROTARY))
    angles = np.arange(length, dtype=np.float32)[:, None] * frequency[lane % halves][None, :]
    rotated = lane < ROTARY
    return np.stack([
        np.where(rotated, np.cos(angles), 1.0),
        np.where(lane < halves, -np.sin(angles), 0.0),
        np.where(rotated & (lane >= halves), np.sin(angles), 0.0),
    ]).astype(np.float32)


def lane_masks():
    lane = lax.broadcasted_iota(jnp.int32, (1, 128), 1)
    return [(lane < HEAD_DIM).astype(F32).astype(BF), (lane >= HEAD_DIM).astype(F32).astype(BF)], lane < HEAD_DIM


def softmax_rows(query, key):
    length = query.shape[0]
    scores = dot_nt(query, key) * 0.125
    below = lax.broadcasted_iota(jnp.int32, (length, length), 0) >= lax.broadcasted_iota(
        jnp.int32, (length, length), 1
    )
    scores = jnp.where(below, scores, -1e30)
    exponent = jnp.exp(scores - jnp.max(scores, axis=-1, keepdims=True))
    return exponent / jnp.sum(exponent, axis=-1, keepdims=True)


def pairs_of(seq, length, part, body):
    def step(at, carry):
        body(pl.ds(seq * length, length), pl.ds(pl.multiple_of(at * 128, 128), 128))
        return carry

    lax.fori_loop(0, part // 128, step, 0)


def forward_attention(first, weight, offset, tables, queries, keys, values, mixed):
    length, part = tables.shape[1], queries.shape[1]
    seqs = queries.shape[0] // length
    for number, target in enumerate((queries, keys, values)):
        for start in range(0, part, 256):
            at = number * part + start
            block = dot(first[...], weight[:, at : at + 256]) + offset[:, at : at + 256]
            if target is values:
                target[:, start : start + 256] = block.astype(BF)
                continue
            for seq in range(seqs):
                for lanes in range(0, 256, 128):
                    rows = slice(seq * length, (seq + 1) * length)
                    turned = turn_pairs(block[rows, lanes : lanes + 128], tables, 1.0)
                    target[rows, start + lanes : start + lanes + 128] = turned.astype(BF)
        yield

    masks, left = lane_masks()
    for seq in range(seqs):

        def body(rows, lanes):
            query, key, value = queries[rows, lanes], keys[rows, lanes], values[rows, lanes]
            sides = [dot(softmax_rows(query * mask, key).astype(BF), value) for mask in masks]
            mixed[rows, lanes] = jnp.where(left, *sides).astype(BF)

        pairs_of(seq, length, part, body)
        yield


def backward_attention(grad_mixed, tables, queries, keys, values, grad_projected):
    length, part = tables.shape[1], queries.shape[1]
    seqs = queries.shape[0] // length
    masks, left = lane_masks()
    for seq in range(seqs):

        def body(rows, lanes):
            query, key, value = queries[rows, lanes], keys[rows, lanes], values[rows, lanes]
            grad = grad_mixed[rows, lanes]
            sides = []
            for mask in masks:
                probs = softmax_rows(query * mask, key)
                grad_probs = dot_nt(grad * mask, value)
                grad_scores = (
                    probs * (grad_probs - jnp.sum(probs * grad_probs, axis=-1, keepdims=True))
                ).astype(BF)
                sides.append((
                    dot(grad_scores, key) * 0.125,
                    dot_tn(grad_scores, query) * 0.125,
                    dot_tn(probs.astype(BF), grad),
                ))
            grads = [jnp.where(left, *pair).astype(BF) for pair in zip(*sides)]
            start = lanes.start
            for number, found in enumerate(grads):
                if number < 2:
                    found = turn_pairs(found.astype(F32), tables, -1.0).astype(BF)
                grad_projected[rows, pl.ds(pl.multiple_of(start + number * part, 128), 128)] = found

        pairs_of(seq, length, part, body)
        yield


def enter_kernel(zhs, tokens, small, qkv_cut, out, tokens_all, small_all, qkv_all, out_all, send, recv, local):
    me, lines = Place(zhs), Lines(send, recv, local)
    me.greet()
    works = [gather_columns(lines, me, qkv_cut, qkv_all, piece) for piece in column_pieces(qkv_cut.shape[2], QKV_PARTS)]
    run(
        *[(0, gather_columns(lines, me, small, small_all, (other, 0, 128))) for other in (False, True)],
        *[(at, work) for at, work in enumerate(works)],
        *[
            (at, gather_rows(lines, me, out, out_all, *piece))
            for at, piece in enumerate(row_pieces(out.shape[0], OUT_PARTS))
        ],
        (1, gather_team(lines, me, tokens, tokens_all, 3)),
    )
    lines.finish()


def middle_kernel(
    zhs, tokens, upstream, tokens_all, qkv_all, out_all, gate_cut, up_cut, down,
    first_gain, first_bias, offset, gain, bias, tables,
    middle, first_out, queries_out, keys_out, values_out, mixed_out,
    upstream_all, input_all, gate_all, up_all, down_all,
    whole, first, weight, out_weight, queries, keys, values, mixed, partial,
    own, passed, taken, second, send, recv, local,
):
    me, lines = Place(zhs), Lines(send, recv, local)
    loads = [lines.copy(tokens_all, whole), lines.copy(qkv_all, weight), lines.copy(out_all, out_weight)]
    me.greet()
    spawned = []

    def tokens_work():
        loads[0]()

        def normed(rows):
            first[rows] = (norm_rows(whole[rows].astype(F32))[0] * first_gain[...] + first_bias[...]).astype(BF)

        by_rows(whole.shape[0], normed)
        loads[1]()
        yield
        yield from forward_attention(first, weight, offset, tables, queries, keys, values, mixed)
        loads[2]()
        for start in range(0, partial.shape[3], 512):
            block = dot(mixed[...], out_weight[:, start : start + 512])
            partial[:, :, :, start : start + 512] = block.astype(BF).reshape(partial.shape[:3] + (512,))
        yield from sum_team(lines, me, partial, own, passed, taken, 2)

        def body(rows):
            values = tokens[rows].astype(F32) + team_total(own, taken, rows)
            middle[rows] = values
            second[rows] = (norm_rows(values)[0] * gain[...] + bias[...]).astype(BF)

        by_rows(middle.shape[0], body)
        kept = [
            lines.copy(source, target)
            for source, target in (
                (first, first_out), (queries, queries_out), (keys, keys_out), (values, values_out), (mixed, mixed_out),
            )
        ]
        yield from gather_team(lines, me, second, input_all, 3)
        wait_all(kept)

    rows = [gather_rows(lines, me, down, down_all, *piece) for piece in row_pieces(down.shape[0], DOWN_PARTS)]
    columns = [
        gather_columns(lines, me, cut, found, piece)
        for piece in column_pieces(gate_cut.shape[2], FF_PARTS)
        for cut, found in ((gate_cut, gate_all), (up_cut, up_all))
    ]
    run(
        *enumerate(rows),
        (0, tokens_work()),
        *[(max(0, len(rows) + at - 1), work) for at, work in enumerate(columns)],
        (1, gather_team(lines, me, upstream, upstream_all, 4)),
    )
    lines.finish()


def back_kernel(
    zhs, middle, upstream, gain, partial_down, partial_second, grad_down, grad_gate, grad_up,
    out_all, queries_in, keys_in, values_in, mixed_in, tables,
    result, grad_middle, sums, down_total, gate_cut, up_cut, out_total, projected_out, bias_sums,
    own_down, passed_down, taken_down, own_second, passed_second, taken_second, attended,
    attended_all, out_weight, queries, keys, values, mixed, grad_mixed, grad_projected, grad_out,
    buffers, send, recv, local,
):
    me, lines = Place(zhs), Lines(send, recv, local)
    loads = [
        lines.copy(source, target)
        for source, target in (
            (out_all, out_weight), (queries_in, queries), (keys_in, keys), (values_in, values), (mixed_in, mixed),
        )
    ]
    me.greet()
    spawned = []
    pieces = column_pieces(gate_cut.shape[2], FF_PARTS)
    works = [
        sum_rows(lines, me, grad_down, down_total, buffers[at], piece[0])
        for at, piece in enumerate(row_pieces(down_total.shape[0], DOWN_PARTS))
    ]
    for piece in pieces:
        for grad, cut in ((grad_gate, gate_cut), (grad_up, up_cut)):
            works.append(sum_columns(lines, me, grad, cut, buffers[len(works)], piece))

    def tokens_work():
        yield from sum_team(lines, me, partial_second, own_second, passed_second, taken_second, 2)
        sums[...] = jnp.zeros_like(sums)

        def body(rows):
            normed, scale_rows = norm_rows(middle[rows])
            grad = team_total(own_second, taken_second, rows)
            sums[0:1] += jnp.sum(grad * normed, axis=0, keepdims=True)
            sums[1:2] += jnp.sum(grad, axis=0, keepdims=True)
            grad = upstream[rows].astype(F32) + norm_back(grad * gain[...], normed, scale_rows)
            grad_middle[rows] = grad
            attended[rows] = grad.astype(BF)

        by_rows(middle.shape[0], body)
        yield from gather_team(lines, me, attended, attended_all, 2)
        wait_all(loads)
        count, width = mixed.shape[0], attended_all.shape[3]
        for start in range(0, width, 512):
            block = dot_tn(mixed[...], attended_all[:, :, :, start : start + 512].reshape(count, 512))
            grad_out[:, :, :, :, start : start + 512] = block.astype(BF).reshape(grad_out.shape[:4] + (512,))
        for at, piece in enumerate(row_pieces(out_total.shape[0], OUT_PARTS)):
            spawned.append(sum_rows(lines, me, grad_out, out_total, buffers[len(works) + at], piece[0]))
        grad_mixed[...] = dot_nt(attended_all[...].reshape(count, width), out_weight[...]).astype(BF)
        yield
        yield from backward_attention(grad_mixed, tables, queries, keys, values, grad_projected)
        wait = lines.copy(grad_projected, projected_out)
        for start in range(0, grad_projected.shape[1], 256):
            block = jnp.sum(grad_projected[:, start : start + 256].astype(F32), axis=0, keepdims=True)
            bias_sums[:, start : start + 256] = block
        yield
        wait()

    def result_work():
        yield from sum_team(lines, me, partial_down, own_down, passed_down, taken_down, 3)

        def body(rows):
            result[rows] = (middle[rows] + team_total(own_down, taken_down, rows)).astype(BF)

        by_rows(middle.shape[0], body)

    run(*enumerate(works), (0, tokens_work()), (7, result_work()), spawned=spawned)
    lines.finish()


def leave_kernel(
    zhs, tokens, grad_middle, gain, second_sums, bias_sums, grad_projected, first_in, qkv_in,
    grad_inputs, sums, qkv_cut,
    first, weight, partial, grad_qkv, own, passed, taken, steps, buffers, send, recv, local,
):
    me, lines = Place(zhs), Lines(send, recv, local)
    loads = [lines.copy(first_in, first), lines.copy(qkv_in, weight)]
    me.greet()

    def tokens_work():
        for at in range(weight.shape[0] // 256):
            block = dot_nt(grad_projected[...], weight[at * 256 : at * 256 + 256])
            partial[:, :, :, at * 256 : at * 256 + 256] = block.astype(BF).reshape(partial.shape[:3] + (256,))
        yield from sum_team(lines, me, partial, own, passed, taken, 2)
        steps[0] = jnp.zeros_like(steps[0])
        steps[0, 2:4] = second_sums[0:2]
        part = bias_sums.shape[1] // 3
        block = part // zhs
        for number in range(3):
            for zh in range(zhs):
                at = ((me.s * zhs + zh) * 2 + me.zl) * block
                steps[0, 4 + number : 5 + number, pl.ds(pl.multiple_of(at, 64), block)] = bias_sums[
                    :, number * part + zh * block : number * part + (zh + 1) * block
                ]

        def body(rows):
            normed, scale_rows = norm_rows(tokens[rows].astype(F32))
            grad = team_total(own, taken, rows)
            steps[0, 0:1] += jnp.sum(grad * normed, axis=0, keepdims=True)
            steps[0, 1:2] += jnp.sum(grad, axis=0, keepdims=True)
            grad_inputs[rows] = grad_middle[rows] + norm_back(grad * gain[...], normed, scale_rows)

        by_rows(tokens.shape[0], body)
        groups = [
            [me.at(s=1 - me.s)], [me.at(zl=1 - me.zl)], [me.at(c=1 - me.c)], [me.at(y=1 - me.y)],
            [me.at(zh=zh) for zh in me.highs()],
        ]
        at = 0
        for group in groups:
            arrived = [
                lines.push(steps.at[at], steps.at[at + 1 + number], device)
                for number, device in enumerate(group)
            ]
            yield
            wait_all(arrived)
            total = steps[at]
            for number in range(len(group)):
                total = total + steps[at + 1 + number]
            at += len(group) + 1
            steps[at] = total
        sums[...] = steps[at]

    wait_all(loads)
    at = 0
    for s in range(grad_qkv.shape[0]):
        for zh in range(zhs):
            for zl in range(grad_qkv.shape[2]):
                block = dot_tn(first[:, at : at + 4 * grad_qkv.shape[5]], grad_projected[...])
                grad_qkv[s, zh, zl] = block.astype(BF).reshape(grad_qkv.shape[3:])
                at += 4 * grad_qkv.shape[5]
    works = [
        sum_columns(lines, me, grad_qkv, qkv_cut, buffers[at], piece)
        for at, piece in enumerate(column_pieces(qkv_cut.shape[2], QKV_PARTS))
    ]
    run(*enumerate(works), (1, tokens_work()))
    lines.finish()


def row_buffers(zhs, size, width):
    return tuple(
        pltpu.VMEM(shape + (size, width), BF) for shape in ((zhs, 2), (zhs, 2), (zhs,), (zhs - 1,))
    ) + (pltpu.VMEM((size, width), F32),)


def column_buffers(zhs, own, columns):
    return tuple(
        pltpu.VMEM(shape + (own, columns), BF)
        for shape in ((zhs, 2, 2), (zhs, 2, 2), (zhs, 2), (zhs - 1, 2))
    )


IN_HBM = pl.BlockSpec(memory_space=pl.ANY)
IN_VMEM = pl.BlockSpec(memory_space=pltpu.VMEM)


def call(kernel, zhs, number, inputs, outputs, scratch, copies, locals_, limit):
    return pl.pallas_call(
        lambda *refs: kernel(zhs, *refs),
        out_shape=[jax.ShapeDtypeStruct(shape, kind) for shape, kind, _ in outputs],
        in_specs=[spec for _, spec in inputs],
        out_specs=[spec for _, _, spec in outputs],
        scratch_shapes=[
            *scratch,
            pltpu.SemaphoreType.DMA((copies,)),
            pltpu.SemaphoreType.DMA((copies,)),
            pltpu.SemaphoreType.DMA((locals_,)),
        ],
        compiler_params=pltpu.CompilerParams(
            collective_id=number, has_side_effects=True, vmem_limit_bytes=limit << 20
        ),
    )(*[array for array, _ in inputs])


def per_device(
    tokens, cotangent, norm1_gain, norm1_bias, qkv_weight, qkv_bias, out_weight,
    norm2_gain, norm2_bias, gate_weight, up_weight, down_weight,
):
    zh = lax.axis_size("zh")
    rows = tokens.shape[1]
    width = tokens.shape[2]
    own = qkv_weight.shape[0]
    ff = gate_weight.shape[1]
    ff_own = down_weight.shape[0]
    half = lax.axis_size("seq")
    length = rows * half
    seqs = lax.axis_size("zl")
    team = half * seqs
    part = width // team
    ff_part = ff // team
    devices = width // own
    tokens, cotangent = tokens[0], cotangent[0]
    index = (lax.axis_index("seq") * (devices // half)
             + ((lax.axis_index("zh") * 2 + lax.axis_index("zl")) * 2 + lax.axis_index("y")) * 2
             + lax.axis_index("c"))

    def cut_columns(shard, parts):
        block = shard.shape[1] // parts // (half * zh * seqs)
        cut = shard.reshape(own, parts, half, zh, seqs, block).transpose(2, 4, 0, 1, 3, 5)
        return cut.reshape(team, own, parts * zh * block)

    def join_columns(cut, parts):
        block = cut.shape[2] // parts // zh
        cut = cut.reshape(half, seqs, own, parts, zh, block).transpose(2, 3, 0, 4, 1, 5)
        return cut.reshape(own, -1).astype(F32)

    def mine_columns(whole, parts):
        block = whole.shape[0] // parts // (half * zh * seqs)
        cut = whole.reshape(parts, half, zh, seqs, block)
        cut = lax.dynamic_index_in_dim(cut, lax.axis_index("seq"), 1, keepdims=False)
        cut = lax.dynamic_index_in_dim(cut, lax.axis_index("zl"), 2, keepdims=False)
        return cut.reshape(-1)

    small = jnp.concatenate([norm1_gain, norm1_bias, norm2_gain, norm2_bias, qkv_bias]).astype(F32)
    small = jnp.pad(small, (0, 1024 - small.shape[0])).reshape(8, 128)
    small = jnp.broadcast_to(small, (team, 8, 128))
    token_shape = (seqs, half, rows, width)
    owners = (half, zh, seqs, 2, 2)
    count = team * rows
    limit = 56
    tables = rotary_tables(length)
    tokens_all, small_all, qkv_all, out_all = call(
        enter_kernel, zh, 0,
        [(tokens, IN_HBM), (small, IN_HBM), (cut_columns(qkv_weight, 3), IN_HBM), (out_weight, IN_HBM)],
        [
            (token_shape, BF, IN_HBM),
            (owners + (8, 128), F32, IN_HBM),
            (owners + (own, 3 * part), BF, IN_HBM),
            ((zh, 2, 2, own, width), BF, IN_HBM),
        ],
        [], 3 + (2 + OUT_PARTS + 2 * QKV_PARTS) * (zh + 4), 24, 16,
    )
    small = small_all.reshape(devices, 1024)
    first_gain = small[:, :own].reshape(1, width)
    first_bias = small[:, own : 2 * own].reshape(1, width)
    second_gain = small[:, 2 * own : 3 * own].reshape(1, width)
    second_bias = small[:, 3 * own : 4 * own].reshape(1, width)
    qkv_offset = mine_columns(small[:, 4 * own : 7 * own].reshape(-1), 3).reshape(1, 3 * part)
    qkv_matrix = qkv_all.reshape(width, 3 * part)
    out_matrix = out_all.reshape(part, width)

    token_scratch = [
        pltpu.VMEM((rows, width), BF), pltpu.VMEM((rows, width), BF), pltpu.VMEM((3, rows, width), BF)
    ]
    head_shape = (count, part)
    heads = [(head_shape, BF, IN_HBM)] * 4
    head_scratch = [pltpu.VMEM(head_shape, BF)] * 4
    (
        middle, first_input, queries, keys, values, mixed, upstream_all, input_all, gate_all, up_all, down_all,
    ) = call(
        middle_kernel, zh, 1,
        [
            (tokens, IN_VMEM), (cotangent, IN_HBM), (tokens_all.reshape(count, width), IN_HBM),
            (qkv_matrix, IN_HBM), (out_matrix, IN_HBM),
            (cut_columns(gate_weight, 1), IN_HBM), (cut_columns(up_weight, 1), IN_HBM), (down_weight, IN_HBM),
            (first_gain, IN_VMEM), (first_bias, IN_VMEM), (qkv_offset, IN_VMEM),
            (second_gain, IN_VMEM), (second_bias, IN_VMEM), (tables, IN_VMEM),
        ],
        [
            ((rows, width), F32, IN_VMEM),
            ((count, width), BF, IN_HBM),
            *heads,
            (token_shape, BF, IN_HBM),
            (token_shape, BF, IN_HBM),
            (owners + (own, ff_part), BF, IN_HBM),
            (owners + (own, ff_part), BF, IN_HBM),
            ((zh, 2, 2, ff_own, width), BF, IN_HBM),
        ],
        [
            pltpu.VMEM((count, width), BF), pltpu.VMEM((count, width), BF),
            pltpu.VMEM((width, 3 * part), BF), pltpu.VMEM((part, width), BF),
            *head_scratch, pltpu.VMEM(token_shape, BF),
            *token_scratch, pltpu.VMEM((rows, width), BF),
        ],
        9 + (DOWN_PARTS + 4 * FF_PARTS) * (zh + 4), 40, limit,
    )
    second_input = input_all.reshape(-1, width)
    upstream = upstream_all.reshape(-1, width)
    gate_matrix = gate_all.reshape(width, ff_part)
    up_matrix = up_all.reshape(width, ff_part)
    down_matrix = down_all.reshape(ff_part, width)
    gate_rows = dot(second_input, gate_matrix)
    up_rows = dot(second_input, up_matrix)
    sigmoid_gate = jax.nn.sigmoid(gate_rows)
    silu_gate = gate_rows * sigmoid_gate
    hidden = (silu_gate * up_rows).astype(BF)
    partial_down = dot(hidden, down_matrix).astype(BF).reshape(token_shape)

    grad_down = dot_tn(hidden, upstream).astype(BF).reshape(down_all.shape)
    grad_hidden = dot_nt(upstream, down_matrix)
    grad_gate = (grad_hidden * up_rows * sigmoid_gate * (1.0 + gate_rows * (1.0 - sigmoid_gate))).astype(BF)
    grad_up = (grad_hidden * silu_gate).astype(BF)
    partial_second = (dot_nt(grad_gate, gate_matrix) + dot_nt(grad_up, up_matrix)).astype(BF).reshape(token_shape)
    result, grad_middle, second_sums, down_total, gate_cut, up_cut, out_total, grad_projected, bias_sums = call(
        back_kernel, zh, 2,
        [
            (middle, IN_VMEM), (cotangent, IN_VMEM), (second_gain, IN_VMEM),
            (partial_down, IN_HBM), (partial_second, IN_HBM), (grad_down, IN_HBM),
            (dot_tn(second_input, grad_gate).astype(BF).reshape(gate_all.shape), IN_HBM),
            (dot_tn(second_input, grad_up).astype(BF).reshape(up_all.shape), IN_HBM),
            (out_matrix, IN_HBM), (queries, IN_HBM), (keys, IN_HBM), (values, IN_HBM), (mixed, IN_HBM),
            (tables, IN_VMEM),
        ],
        [
            ((rows, width), BF, IN_VMEM),
            ((rows, width), F32, IN_VMEM),
            ((8, width), F32, IN_VMEM),
            ((ff_own, width), F32, IN_HBM),
            ((team, own, ff_part), BF, IN_HBM),
            ((team, own, ff_part), BF, IN_HBM),
            ((own, width), F32, IN_HBM),
            ((count, 3 * part), BF, IN_HBM),
            ((1, 3 * part), F32, IN_VMEM),
        ],
        [
            *token_scratch, *token_scratch, pltpu.VMEM((rows, width), BF), pltpu.VMEM(token_shape, BF),
            pltpu.VMEM((part, width), BF), *head_scratch, pltpu.VMEM(head_shape, BF),
            pltpu.VMEM((count, 3 * part), BF), pltpu.VMEM(out_all.shape, BF),
            [row_buffers(zh, size, width) for _, size in row_pieces(ff_own, DOWN_PARTS)]
            + [
                column_buffers(zh, own, size)
                for _, _, size in column_pieces(ff_part, FF_PARTS)
                for _ in range(2)
            ]
            + [row_buffers(zh, size, width) for _, size in row_pieces(own, OUT_PARTS)],
        ],
        9 + (OUT_PARTS + DOWN_PARTS + 4 * FF_PARTS) * (zh + 4), 50, 60,
    )
    grad_inputs, sums, qkv_cut = call(
        leave_kernel, zh, 3,
        [
            (tokens, IN_VMEM), (grad_middle, IN_VMEM), (first_gain, IN_VMEM),
            (second_sums, IN_VMEM), (bias_sums, IN_VMEM), (grad_projected, IN_VMEM),
            (first_input, IN_HBM), (qkv_matrix, IN_HBM),
        ],
        [
            ((rows, width), F32, IN_VMEM),
            ((8, width), F32, IN_VMEM),
            ((team, own, 3 * part), BF, IN_HBM),
        ],
        [
            pltpu.VMEM((count, width), BF), pltpu.VMEM((width, 3 * part), BF), pltpu.VMEM(token_shape, BF),
            pltpu.VMEM(qkv_all.shape, BF),
            *token_scratch, pltpu.VMEM((zh + 9, 8, width), F32),
            [column_buffers(zh, own, size) for _, _, size in column_pieces(3 * part, QKV_PARTS)],
        ],
        zh + 6 + (2 * QKV_PARTS) * (zh + 4), 24, limit,
    )

    def mine(vector_row, size):
        return lax.dynamic_slice_in_dim(vector_row, index * size, size, 0)

    return (
        result[None],
        grad_inputs[None],
        mine(sums[0], own),
        mine(sums[1], own),
        join_columns(qkv_cut, 3),
        mine(sums[4:7].reshape(-1), 3 * own),
        out_total,
        mine(sums[2], own),
        mine(sums[3], own),
        join_columns(gate_cut, 1),
        join_columns(up_cut, 1),
        down_total,
    )


def solution(mesh):
    half, shards = mesh.shape["seq"], mesh.shape["shard"]
    fine = jax.sharding.Mesh(mesh.devices.reshape(half, shards // 8, 2, 2, 2), ALL)
    token = P(("zh", "zl", "y", "c"), "seq", None)
    row = P(ALL)

    def program(*arguments):
        whole_tiles = arguments[-1].shape[0] // (half * shards) % ROWS == 0
        return jax.shard_map(
            per_device if whole_tiles else plain_device,
            mesh=fine,
            in_specs=(token, token) + (row,) * 10,
            out_specs=(token, token) + (row,) * 10,
            check_vma=False,
        )(*arguments)

    return program
```

```python
import jax
import jax.numpy as jnp
import numpy as np
from jax import lax
from jax.experimental import pallas as pl
from jax.experimental.pallas import tpu as pltpu
from jax.sharding import PartitionSpec as P

HEADS = 32
HEAD_DIM = 64
ROTARY = 16
TEAM = ("seq", "zl")
PEERS = ("zh", "y", "c")
ALL = ("seq", "zh", "zl", "y", "c")
BF = jnp.bfloat16
F32 = jnp.float32


def norm_rows(values):
    centre = jnp.mean(values, axis=-1, keepdims=True)
    centred = values - centre
    spread = jnp.mean(centred * centred, axis=-1, keepdims=True)
    scale_rows = lax.rsqrt(spread + 1e-05)
    return (centred * scale_rows, scale_rows)


def norm_back(grad_normed, normed, scale_rows):
    return scale_rows * (
        grad_normed
        - jnp.mean(grad_normed, axis=-1, keepdims=True)
        - normed * jnp.mean(grad_normed * normed, axis=-1, keepdims=True)
    )


def rotate(values, positions, direction):
    halves = ROTARY // 2
    frequency = 10000.0 ** (-2.0 * jnp.arange(halves, dtype=F32) / ROTARY)
    angles = positions.astype(F32)[:, None] * frequency[None, :]
    cosine_table = jnp.cos(angles)[:, None, :]
    sine_table = jnp.sin(angles)[:, None, :] * direction
    first_half = values[..., :halves]
    second_half = values[..., halves:ROTARY]
    return jnp.concatenate(
        [
            first_half * cosine_table - second_half * sine_table,
            second_half * cosine_table + first_half * sine_table,
            values[..., ROTARY:],
        ],
        axis=-1,
    )


def dot(left, right):
    return jnp.dot(left, right, preferred_element_type=F32)


def dot_nt(left, right):
    return lax.dot_general(left, right, (((1,), (1,)), ((), ())), preferred_element_type=F32)


def dot_tn(left, right):
    return lax.dot_general(left, right, (((0,), (0,)), ((), ())), preferred_element_type=F32)


def plain_device(
    tokens, cotangent, norm1_gain, norm1_bias, qkv_weight, qkv_bias, out_weight,
    norm2_gain, norm2_bias, gate_weight, up_weight, down_weight,
):
    zh = lax.axis_size("zh")
    rows = tokens.shape[1]
    width = tokens.shape[2]
    own = qkv_weight.shape[0]
    ff = gate_weight.shape[1]
    half = lax.axis_size("seq")
    length = rows * half
    team = half * lax.axis_size("zl")
    seqs = lax.axis_size("zl")

    def cut_columns(shard, parts):
        block = shard.shape[1] // parts // (half * zh * seqs)
        cut = shard.reshape(own, parts, half, zh, seqs, block).transpose(2, 4, 0, 1, 3, 5)
        return cut.reshape(team, own, parts * zh * block)

    def join_columns(cut, parts):
        block = cut.shape[2] // parts // zh
        cut = cut.reshape(half, seqs, own, parts, zh, block).transpose(2, 3, 0, 4, 1, 5)
        return cut.reshape(own, -1)

    def mine_columns(whole, parts):
        block = whole.shape[0] // parts // (half * zh * seqs)
        cut = whole.reshape(parts, half, zh, seqs, block)
        cut = lax.dynamic_index_in_dim(cut, lax.axis_index("seq"), 1, keepdims=False)
        cut = lax.dynamic_index_in_dim(cut, lax.axis_index("zl"), 2, keepdims=False)
        return cut.reshape(-1)

    def to_owner_order(values):
        n = values.shape[0]
        return values.reshape(n, half, zh, seqs, 4, own).transpose(0, 2, 4, 1, 3, 5).reshape(n, width)

    def from_owner_order(values):
        n = values.shape[0]
        return values.reshape(n, zh, 4, half, seqs, own).transpose(0, 3, 1, 4, 2, 5).reshape(n, width)

    def gather_columns(shard, parts):
        cut = cut_columns(shard, parts)
        cut = lax.all_to_all(cut, TEAM, split_axis=0, concat_axis=0, tiled=True)
        return lax.all_gather(cut.reshape(team * own, -1), PEERS, axis=0, tiled=True)

    def gather_rows(shard):
        return lax.all_gather(shard, PEERS, axis=0, tiled=True)

    def gather_tokens(values):
        return lax.all_gather(values, ("zl", "seq"), axis=0, tiled=True)

    def sum_tokens(values):
        return lax.psum_scatter(values.astype(BF), ("zl", "seq"), scatter_dimension=0, tiled=True).astype(F32)

    def sum_rows(values):
        return lax.psum_scatter(values.astype(BF), PEERS, scatter_dimension=0, tiled=True)

    def sum_columns(values, parts):
        part = sum_rows(values).reshape(team, own, -1)
        part = lax.all_to_all(part, TEAM, split_axis=0, concat_axis=0, tiled=True)
        return join_columns(part, parts).astype(F32)

    small = jnp.concatenate([norm1_gain, norm1_bias, norm2_gain, norm2_bias, qkv_bias])
    small = lax.all_gather(small, ALL, axis=0, tiled=False)
    first_gain = small[:, :own].reshape(-1).astype(F32)
    first_bias = small[:, own : 2 * own].reshape(-1).astype(F32)
    second_gain = small[:, 2 * own : 3 * own].reshape(-1).astype(F32)
    second_bias = small[:, 3 * own : 4 * own].reshape(-1).astype(F32)
    qkv_offset = mine_columns(small[:, 4 * own :].reshape(-1), 3).astype(F32)

    inputs = tokens[0].astype(F32)
    first_normed, first_scale = norm_rows(inputs)
    first_own = to_owner_order((first_normed * first_gain + first_bias).astype(BF))
    first_input = gather_tokens(first_own)
    qkv_matrix = gather_columns(qkv_weight, 3)
    out_matrix = gather_rows(out_weight)
    gate_matrix = gather_columns(gate_weight, 1)
    up_matrix = gather_columns(up_weight, 1)
    down_matrix = gather_rows(down_weight)
    upstream = gather_tokens(cotangent[0])

    projected = dot(first_input, qkv_matrix) + qkv_offset
    part = width // team
    group_heads = part // HEAD_DIM
    positions = jnp.tile(jnp.arange(length, dtype=jnp.int32), seqs)

    def heads_of(values):
        return values.reshape(seqs, length, group_heads, HEAD_DIM).transpose(0, 2, 1, 3)

    def unheads(values):
        return values.transpose(0, 2, 1, 3).reshape(seqs * length, part)

    queries = heads_of(rotate(projected[:, :part].reshape(-1, group_heads, HEAD_DIM), positions, 1.0).astype(BF))
    keys = heads_of(rotate(projected[:, part : 2 * part].reshape(-1, group_heads, HEAD_DIM), positions, 1.0).astype(BF))
    values = heads_of(projected[:, 2 * part :].astype(BF))
    causal = jnp.arange(length)[:, None] >= jnp.arange(length)[None, :]
    scores = jnp.einsum("shqd,shkd->shqk", queries, keys, preferred_element_type=F32) * 0.125
    scores = jnp.where(causal, scores, -1e30)
    highest = jnp.max(scores, axis=-1, keepdims=True)
    exponent = jnp.exp(scores - highest)
    probs = exponent / jnp.sum(exponent, axis=-1, keepdims=True)
    probs_low = probs.astype(BF)
    mixed = unheads(jnp.einsum("shqk,shkd->shqd", probs_low, values, preferred_element_type=F32).astype(BF))
    middle = inputs + sum_tokens(dot(mixed, out_matrix))

    second_normed, second_scale = norm_rows(middle)
    second_own = to_owner_order((second_normed * second_gain + second_bias).astype(BF))
    second_input = gather_tokens(second_own)
    gate_rows = dot(second_input, gate_matrix)
    up_rows = dot(second_input, up_matrix)
    sigmoid_gate = jax.nn.sigmoid(gate_rows)
    silu_gate = gate_rows * sigmoid_gate
    hidden = (silu_gate * up_rows).astype(BF)
    result = middle + sum_tokens(dot(hidden, down_matrix))

    down_total = sum_rows(dot_tn(hidden, upstream)).astype(F32)
    grad_hidden = dot_nt(upstream, down_matrix)
    grad_gate = (grad_hidden * up_rows * sigmoid_gate * (1.0 + gate_rows * (1.0 - sigmoid_gate))).astype(BF)
    grad_up = (grad_hidden * silu_gate).astype(BF)
    gate_total = sum_columns(dot_tn(second_input, grad_gate), 1)
    up_total = sum_columns(dot_tn(second_input, grad_up), 1)
    grad_second = from_owner_order(sum_tokens(dot_nt(grad_gate, gate_matrix) + dot_nt(grad_up, up_matrix)))
    grad_middle = cotangent[0].astype(F32) + norm_back(grad_second * second_gain, second_normed, second_scale)
    grad_attended = gather_tokens(grad_middle.astype(BF))
    out_total = sum_rows(dot_tn(mixed, grad_attended)).astype(F32)
    grad_mixed = heads_of(dot_nt(grad_attended, out_matrix).astype(BF))
    grad_probs = jnp.einsum("shqd,shkd->shqk", grad_mixed, values, preferred_element_type=F32)
    grad_scores = (probs * (grad_probs - jnp.sum(probs * grad_probs, axis=-1, keepdims=True))).astype(BF)
    grad_queries = (jnp.einsum("shqk,shkd->shqd", grad_scores, keys, preferred_element_type=F32) * 0.125).astype(BF)
    grad_keys = (jnp.einsum("shqk,shqd->shkd", grad_scores, queries, preferred_element_type=F32) * 0.125).astype(BF)
    grad_values = jnp.einsum("shqk,shqd->shkd", probs_low, grad_mixed, preferred_element_type=F32).astype(BF)
    grad_queries = rotate(unheads(grad_queries).astype(F32).reshape(-1, group_heads, HEAD_DIM), positions, -1.0)
    grad_keys = rotate(unheads(grad_keys).astype(F32).reshape(-1, group_heads, HEAD_DIM), positions, -1.0)
    grad_projected = jnp.concatenate(
        [grad_queries.reshape(-1, part).astype(BF), grad_keys.reshape(-1, part).astype(BF), unheads(grad_values)],
        axis=1,
    )
    qkv_total = sum_columns(dot_tn(first_input, grad_projected), 3)
    grad_first = from_owner_order(sum_tokens(dot_nt(grad_projected, qkv_matrix)))
    grad_inputs = grad_middle + norm_back(grad_first * first_gain, first_normed, first_scale)

    bias_part = jnp.sum(grad_projected.astype(F32), axis=0).reshape(3, zh, -1)
    bias_whole = jnp.zeros((3, half, zh, seqs, bias_part.shape[2]), F32)
    bias_whole = lax.dynamic_update_slice(
        bias_whole, bias_part[:, None, :, None], (0, lax.axis_index("seq"), 0, lax.axis_index("zl"), 0)
    ).reshape(-1)
    count = width // own
    sums = jnp.concatenate(
        [
            jnp.sum(grad_first * first_normed, axis=0).reshape(count, own),
            jnp.sum(grad_first, axis=0).reshape(count, own),
            jnp.sum(grad_second * second_normed, axis=0).reshape(count, own),
            jnp.sum(grad_second, axis=0).reshape(count, own),
            bias_whole.reshape(count, 3 * own),
        ],
        axis=1,
    )
    sums = lax.psum_scatter(sums, ALL, scatter_dimension=0, tiled=True)[0]
    return (
        result.astype(BF)[None],
        grad_inputs[None],
        sums[:own],
        sums[own : 2 * own],
        qkv_total,
        sums[4 * own :],
        out_total,
        sums[2 * own : 3 * own],
        sums[3 * own : 4 * own],
        gate_total,
        up_total,
        down_total,
    )


MESH = pl.DeviceIdType.MESH
ROWS = 16
QKV_PARTS, OUT_PARTS, FF_PARTS, DOWN_PARTS = 2, 2, 2, 4


class Place:
    def __init__(self, zhs):
        self.s, self.zh, self.zl, self.y, self.c = (lax.axis_index(axis) for axis in ALL)
        self.zhs = zhs

    def at(self, **changed):
        return tuple(changed.get(name, getattr(self, name)) for name in ("s", "zh", "zl", "y", "c"))

    def mates(self):
        for flip_s, flip_z in ((0, 1), (1, 0), (1, 1)):
            yield (1 - self.s if flip_s else self.s), (1 - self.zl if flip_z else self.zl)

    def highs(self):
        for step in range(1, self.zhs):
            yield (self.zh + step) % self.zhs

    def greet(self):
        partners = [self.at(s=s, zl=zl) for s, zl in self.mates()]
        partners += [self.at(zh=zh) for zh in self.highs()]
        partners += [self.at(y=1 - self.y), self.at(c=1 - self.c)]
        barrier = pltpu.get_barrier_semaphore()
        for partner in partners:
            pl.semaphore_signal(barrier, inc=1, device_id=partner, device_id_type=MESH)
        pl.semaphore_wait(barrier, len(partners))


class Traffic:
    def __init__(self):
        self.now, self.active = 0.0, []

    def start(self, demands):
        transfer = {"left": {link: time for link, time in demands.items()}, "done": None}
        self.active.append(transfer)
        return transfer

    def backlog(self, link):
        return sum(transfer["left"].get(link, 0.0) for transfer in self.active)

    def advance(self, until):
        while self.now < until:
            shares = {}
            for transfer in self.active:
                for link in transfer["left"]:
                    shares[link] = shares.get(link, 0) + 1
            step = until - self.now
            for transfer in self.active:
                for link, left in transfer["left"].items():
                    step = min(step, left * shares[link])
            self.now += step
            for transfer in list(self.active):
                transfer["left"] = {
                    link: left - step / shares[link]
                    for link, left in transfer["left"].items()
                    if left - step / shares[link] > 1e-6
                }
                if not transfer["left"]:
                    transfer["done"] = self.now + LATENCY
                    self.active.remove(transfer)


LATENCY = 2.0
ENTER_PLAN = ((5.6, 57), (8.2, 57), (7.8, 21), (3.3, 0), (2.3, 33), (5.3, 10), (1.3, 7), (3, 0), (2.7, 10))
MIDDLE_PLAN = ((0, 0), (1, 0), (3, 0), (4, 0), (5, 0), (6, 0), (7, 0), (8, 0), (9, 0), (2, 0), (10, 0), (11, 0), (12, 0), (13, 0))
FEED_PLAN = ((4.7, 15), (4.7, 0), (3.3, 39), (2.5, 34), (1.8, 21))
BACK_PLAN = ((15.2, 0), (4.1, 1), (5.4, 4), (11.1, 9), (8.1, 19), (2.1, 0), (9.7, 36), (9.5, 0), (5.8, 0), (14.6, 4), (7.3, 25), (1.1, 18), (3.7, 0), (14.2, 21), (0.3, 49), (13.7, 26), (5.5, 0))
LEAVE_PLAN = ((3.5, 0), (3.2, 55), (1.3, 24), (4.2, 47), (2.1, 0))
BACKLOG = 12.0
LINK_TIME = {
    "s": {"s": 2 / 92e3},
    "zl": {"zl": 2 / 92e3},
    "y": {"y": 2 / 92e3},
    "zh": {"zh": 4 / 92e3, "zl": 2 / 92e3},
    "c": {"c": 1 / 300e3},
    "diagonal": {"s": 2 / 92e3, "zl": 2 / 92e3},
    "local": {"local": 1 / 1500e3},
}


class Lines:
    def __init__(self, send, recv, local):
        self.send, self.recv, self.local = send, recv, local
        self.sent, self.copied, self.traffic = [], 0, Traffic()

    def track(self, wait, source, link):
        size = int(np.prod(source.shape)) * jnp.dtype(source.dtype).itemsize
        return wait, self.traffic.start({name: time * size for name, time in LINK_TIME[link].items()})

    def push(self, source, target, device, link):
        at = len(self.sent)
        copy = pltpu.make_async_remote_copy(
            src_ref=source, dst_ref=target, send_sem=self.send.at[at], recv_sem=self.recv.at[at],
            device_id=device, device_id_type=MESH,
        )
        copy.start()
        self.sent.append(copy)
        return self.track(copy.wait_recv, source, link)

    def copy(self, source, target):
        copy = pltpu.make_async_copy(source, target, self.local.at[self.copied])
        copy.start()
        self.copied += 1
        return self.track(copy.wait, source, "local")

    def finish(self):
        for copy in self.sent:
            copy.wait_send()


def run(lines, works, plan, start=3.0):
    traffic, now = lines.traffic, start
    open_works, late, plan = [], None, iter(plan)

    def add(work):
        rank, begin = next(plan, (0.0, 0.0))
        open_works.append([rank, begin, work, next(work)])
        open_works.sort(key=lambda entry: entry[0])

    for work in works:
        if isinstance(work, list):
            late = work
        else:
            add(work)
    while open_works:
        traffic.advance(now)
        for entry in open_works:
            waits, cost, link = entry[3]
            arrived = all(transfer["done"] is not None and transfer["done"] <= now for _, transfer in waits)
            if arrived and now >= entry[1] and (link is None or traffic.backlog(link) < BACKLOG):
                break
        else:
            now += 0.25
            continue
        for wait, _ in waits:
            wait()
        entry[1], entry[3] = 0.0, next(entry[2], None)
        now += cost + 0.15
        if entry[3] is None:
            open_works.remove(entry)
        while late:
            add(late.pop(0))


def gather_team(lines, me, source, whole):
    yield [], 0, None
    mine, other = whole.at[me.zl, me.s], whole.at[1 - me.zl, me.s]
    across = lines.push(source, mine, me.at(zl=1 - me.zl), "zl")
    waits = [lines.copy(source, mine), lines.push(source, mine, me.at(s=1 - me.s), "s")]
    yield [across], 0, None
    waits.append(lines.push(other, other, me.at(s=1 - me.s), "s"))
    yield waits, 0, None


def gather_columns(lines, me, cut, whole, piece):
    other, start, size = piece
    s, columns = 1 - me.s if other else me.s, pl.ds(start, size)
    yield [], 0, "s"
    mine = whole.at[me.s, me.zh, me.zl, me.y, me.c, :, columns]
    waits = []
    for flip in (0, 1):
        zl = 1 - me.zl if flip else me.zl
        if other or flip:
            link = "diagonal" if other and flip else "s" if other else "zl"
            waits.append(lines.push(cut.at[s * 2 + zl, :, columns], mine, me.at(s=s, zl=zl), link))
        else:
            waits.append(lines.copy(cut.at[s * 2 + zl, :, columns], mine))
    yield waits, 0, "zh"
    part = whole.at[s, me.zh, :, me.y, me.c, :, columns]
    waits = [lines.push(part, part, me.at(zh=zh), "zh") for zh in me.highs()]
    yield waits, 0, "y"
    part = whole.at[s, :, :, me.y, me.c, :, columns]
    wait = lines.push(part, part, me.at(y=1 - me.y), "y")
    yield [wait], 0, None
    part = whole.at[s, :, :, :, me.c, :, columns]
    wait = lines.push(part, part, me.at(c=1 - me.c), "c")
    yield [wait], 0, None


def gather_rows(lines, me, source, whole, start, size):
    rows = pl.ds(start, size)
    yield [], 0, "zh"
    mine = whole.at[me.zh, me.y, me.c, rows]
    waits = [lines.copy(source.at[rows], mine)]
    waits += [lines.push(source.at[rows], mine, me.at(zh=zh), "zh") for zh in me.highs()]
    yield waits, 0, "y"
    part = whole.at[:, me.y, me.c, rows]
    wait = lines.push(part, part, me.at(y=1 - me.y), "y")
    yield [wait], 0, None
    part = whole.at[:, :, me.c, rows]
    wait = lines.push(part, part, me.at(c=1 - me.c), "c")
    yield [wait], 0, None


def add_into(target, sources, result=None):
    result = target if result is None else result

    def step(at, carry):
        rows = pl.ds(pl.multiple_of(at * ROWS, ROWS), ROWS)
        total = target[rows].astype(F32)
        for source in sources:
            total = total + source[rows].astype(F32)
        result[rows] = total.astype(result.dtype)
        return carry

    lax.fori_loop(0, target.shape[0] // ROWS, step, 0)


def add_time(*refs):
    return sum(int(np.prod(ref.shape)) for ref in refs) * ADD_TIME


ADD_TIME = 1.6e-6


def sum_columns(lines, me, grad, cut, buffers, piece):
    first, second, third = buffers
    other, start, size = piece
    s, columns = 1 - me.s if other else me.s, pl.ds(start, size)
    mine = grad.at[s, :, :, :, me.c, :, columns]
    yield [], 0, "c"
    wait = lines.push(grad.at[s, :, :, :, 1 - me.c, :, columns], first, me.at(c=1 - me.c), "c")
    yield [wait], add_time(first) / 2, "y"

    def fold(y):
        for zh in range(me.zhs):
            for zl in range(2):
                add_into(mine.at[zh, zl, y], [first.at[zh, zl, y]])

    fold(1 - me.y)
    wait = lines.push(mine.at[:, :, 1 - me.y], second, me.at(y=1 - me.y), "y")
    yield [], add_time(first) / 2, None
    fold(me.y)
    yield [wait], add_time(second), "zh"
    waits = []
    for step, zh in enumerate([*me.highs(), me.zh]):
        for zl in range(2):
            add_into(mine.at[zh, zl, me.y], [second.at[zh, zl]])
        if step < me.zhs - 1:
            waits.append(lines.push(mine.at[zh, :, me.y], third.at[step], me.at(zh=zh), "zh"))
    yield waits, add_time(third), None
    for zl in range(2):
        add_into(mine.at[me.zh, zl, me.y], [third.at[step, zl] for step in range(me.zhs - 1)])
    waits = []
    for flip in (0, 1):
        zl = 1 - me.zl if flip else me.zl
        source, target = mine.at[me.zh, zl, me.y], cut.at[me.s * 2 + me.zl, :, columns]
        if other or flip:
            link = "diagonal" if other and flip else "s" if other else "zl"
            waits.append(lines.push(source, target, me.at(s=s, zl=zl), link))
        else:
            waits.append(lines.copy(source, target))
    yield waits, 0, None


def sum_near(lines, me, grad, buffers, piece):
    first, second = buffers
    rows = pl.ds(*piece)
    mine = grad.at[:, :, me.c, rows]
    yield [], 0, "c"
    wait = lines.push(grad.at[:, :, 1 - me.c, rows], first, me.at(c=1 - me.c), "c")
    yield [wait], add_time(first) / 2, "y"
    for zh in range(me.zhs):
        add_into(mine.at[zh, 1 - me.y], [first.at[zh, 1 - me.y]])
    wait = lines.push(mine.at[:, 1 - me.y], second, me.at(y=1 - me.y), "y")
    yield [], add_time(first) / 2, None
    for zh in range(me.zhs):
        add_into(mine.at[zh, me.y], [first.at[zh, me.y]])
    yield [wait], add_time(second), None
    for zh in range(me.zhs):
        add_into(mine.at[zh, me.y], [second.at[zh]])


def sum_far(lines, me, part, total, buffers, piece):
    mine, third, final = buffers
    rows = pl.ds(*piece)
    yield [], 0, "zh"
    waits = [lines.copy(part.at[me.zh, rows], mine)]
    for step, zh in enumerate(me.highs()):
        waits.append(lines.push(part.at[zh, rows], third.at[step], me.at(zh=zh), "zh"))
    yield waits, add_time(third), None
    add_into(mine, [third.at[step] for step in range(me.zhs - 1)], final)
    wait = lines.copy(final, total.at[rows])
    yield [wait], 0, None


def sum_rows(lines, me, grad, total, near, far, piece):
    yield from sum_near(lines, me, grad, near, piece)
    yield from sum_far(lines, me, grad.at[:, me.y, me.c], total, far, piece)


def sum_team(lines, me, partial, own, passed, taken):
    first = [
        lines.copy(partial.at[1 - me.zl, me.s], passed),
        lines.push(partial.at[1 - me.zl, 1 - me.s], taken.at[0], me.at(s=1 - me.s), "s"),
    ]
    waits = [
        lines.push(partial.at[me.zl, 1 - me.s], taken.at[1], me.at(s=1 - me.s), "s"),
        lines.copy(partial.at[me.zl, me.s], own),
    ]
    yield first, add_time(passed), None
    add_into(passed, [taken.at[0]])
    waits.append(lines.push(passed, taken.at[2], me.at(zl=1 - me.zl), "zl"))
    yield waits, 3, None


def team_total(own, taken, rows):
    return own[rows].astype(F32) + taken[1, rows].astype(F32) + taken[2, rows].astype(F32)


def by_rows(count, body):
    def step(at, carry):
        body(pl.ds(pl.multiple_of(at * ROWS, ROWS), ROWS))
        return carry

    lax.fori_loop(0, count // ROWS, step, 0)


def row_pieces(size, parts):
    tiles, pieces, start = size // ROWS, [], 0
    for part in range(parts):
        count = (tiles * (part + 1) // parts - tiles * part // parts) * ROWS
        pieces.append((start, count))
        start += count
    return pieces


def column_pieces(columns, parts):
    lanes, pieces, start = columns // 128, [], 0
    for part in range(parts):
        size = (lanes * (part + 1) // parts - lanes * part // parts) * 128
        pieces.append((start, size))
        start += size
    return [(other, *piece) for other in (False, True) for piece in pieces]


def turn_pairs(values, tables, sign):
    return (
        values * tables[0]
        + pltpu.roll(values, 128 - ROTARY // 2, 1) * (tables[1] * sign)
        + pltpu.roll(values, ROTARY // 2, 1) * (tables[2] * sign)
    )


def rotary_tables(length):
    lane = np.arange(128) % HEAD_DIM
    halves = ROTARY // 2
    frequency = np.float32(10000.0) ** (np.float32(-2.0) * np.arange(halves, dtype=np.float32) / np.float32(ROTARY))
    angles = np.arange(length, dtype=np.float32)[:, None] * frequency[lane % halves][None, :]
    rotated = lane < ROTARY
    return np.stack([
        np.where(rotated, np.cos(angles), 1.0),
        np.where(lane < halves, -np.sin(angles), 0.0),
        np.where(rotated & (lane >= halves), np.sin(angles), 0.0),
    ]).astype(np.float32)


def lane_masks():
    lane = lax.broadcasted_iota(jnp.int32, (1, 128), 1)
    return [(lane < HEAD_DIM).astype(F32).astype(BF), (lane >= HEAD_DIM).astype(F32).astype(BF)], lane < HEAD_DIM


def softmax_rows(query, key):
    length = query.shape[0]
    scores = dot_nt(query, key) * 0.125
    below = lax.broadcasted_iota(jnp.int32, (length, length), 0) >= lax.broadcasted_iota(
        jnp.int32, (length, length), 1
    )
    scores = jnp.where(below, scores, -1e30)
    exponent = jnp.exp(scores - jnp.max(scores, axis=-1, keepdims=True))
    return exponent / jnp.sum(exponent, axis=-1, keepdims=True)


def pairs_of(seq, length, part, body):
    def step(at, carry):
        body(pl.ds(seq * length, length), pl.ds(pl.multiple_of(at * 128, 128), 128))
        return carry

    lax.fori_loop(0, part // 128, step, 0)


def forward_attention(first, weight, offset, tables, queries, keys, values, mixed):
    length, part = tables.shape[1], queries.shape[1]
    seqs = queries.shape[0] // length
    for number, target in enumerate((queries, keys, values)):
        for start in range(0, part, 256):
            at = number * part + start
            block = dot(first[...], weight[:, at : at + 256]) + offset[:, at : at + 256]
            if target is values:
                target[:, start : start + 256] = block.astype(BF)
                continue
            for seq in range(seqs):
                for lanes in range(0, 256, 128):
                    rows = slice(seq * length, (seq + 1) * length)
                    turned = turn_pairs(block[rows, lanes : lanes + 128], tables, 1.0)
                    target[rows, start + lanes : start + lanes + 128] = turned.astype(BF)
        yield [], 2.5 if number < 2 else 6, None

    masks, left = lane_masks()
    for seq in range(seqs):

        def body(rows, lanes):
            query, key, value = queries[rows, lanes], keys[rows, lanes], values[rows, lanes]
            sides = [dot(softmax_rows(query * mask, key).astype(BF), value) for mask in masks]
            mixed[rows, lanes] = jnp.where(left, *sides).astype(BF)

        pairs_of(seq, length, part, body)
        yield [], 6 if seq < seqs - 1 else 2, None


def backward_attention(grad_mixed, tables, queries, keys, values, grad_projected):
    length, part = tables.shape[1], queries.shape[1]
    seqs = queries.shape[0] // length
    masks, left = lane_masks()
    for seq in range(seqs):

        def body(rows, lanes):
            query, key, value = queries[rows, lanes], keys[rows, lanes], values[rows, lanes]
            grad = grad_mixed[rows, lanes]
            sides = []
            for mask in masks:
                probs = softmax_rows(query * mask, key)
                grad_probs = dot_nt(grad * mask, value)
                grad_scores = (
                    probs * (grad_probs - jnp.sum(probs * grad_probs, axis=-1, keepdims=True))
                ).astype(BF)
                sides.append((
                    dot(grad_scores, key) * 0.125,
                    dot_tn(grad_scores, query) * 0.125,
                    dot_tn(probs.astype(BF), grad),
                ))
            grads = [jnp.where(left, *pair).astype(BF) for pair in zip(*sides)]
            start = lanes.start
            for number, found in enumerate(grads):
                if number < 2:
                    found = turn_pairs(found.astype(F32), tables, -1.0).astype(BF)
                grad_projected[rows, pl.ds(pl.multiple_of(start + number * part, 128), 128)] = found

        pairs_of(seq, length, part, body)
        yield [], 9 if seq < seqs - 1 else 1, None


def enter_kernel(zhs, tokens, small, qkv_cut, out, tokens_all, small_all, qkv_all, out_all, send, recv, local):
    me, lines = Place(zhs), Lines(send, recv, local)
    me.greet()
    run(lines, [
        *[gather_columns(lines, me, small, small_all, (other, 0, 128)) for other in (False, True)],
        *[gather_columns(lines, me, qkv_cut, qkv_all, piece) for piece in column_pieces(qkv_cut.shape[2], QKV_PARTS)],
        *[gather_rows(lines, me, out, out_all, *piece) for piece in row_pieces(out.shape[0], OUT_PARTS)],
        gather_team(lines, me, tokens, tokens_all),
    ], ENTER_PLAN)
    lines.finish()


def middle_kernel(
    zhs, tokens, upstream, tokens_all, qkv_all, out_all, gate_cut, up_cut, down,
    first_gain, first_bias, offset, gain, bias, tables,
    middle, first_out, queries_out, keys_out, values_out, mixed_out,
    upstream_all, input_all, gate_all, up_all, down_all,
    whole, first, weight, out_weight, queries, keys, values, mixed, partial,
    own, passed, taken, second, send, recv, local,
):
    me, lines = Place(zhs), Lines(send, recv, local)
    loads = [lines.copy(tokens_all, whole), lines.copy(qkv_all, weight), lines.copy(out_all, out_weight)]
    me.greet()

    def tokens_work():
        yield loads[:1], 4, None

        def normed(rows):
            first[rows] = (norm_rows(whole[rows].astype(F32))[0] * first_gain[...] + first_bias[...]).astype(BF)

        by_rows(whole.shape[0], normed)
        yield loads[1:], 2.5, None
        yield from forward_attention(first, weight, offset, tables, queries, keys, values, mixed)
        for start in range(0, partial.shape[3], 512):
            block = dot(mixed[...], out_weight[:, start : start + 512])
            partial[:, :, :, start : start + 512] = block.astype(BF).reshape(partial.shape[:3] + (512,))
        yield from sum_team(lines, me, partial, own, passed, taken)

        def body(rows):
            values = tokens[rows].astype(F32) + team_total(own, taken, rows)
            middle[rows] = values
            second[rows] = (norm_rows(values)[0] * gain[...] + bias[...]).astype(BF)

        by_rows(middle.shape[0], body)
        kept = [
            lines.copy(source, target)
            for source, target in (
                (first, first_out), (queries, queries_out), (keys, keys_out), (values, values_out), (mixed, mixed_out),
            )
        ]
        yield from gather_team(lines, me, second, input_all)
        yield kept, 0, None

    rows = [gather_rows(lines, me, down, down_all, *piece) for piece in row_pieces(down.shape[0], DOWN_PARTS)]
    columns = [
        gather_columns(lines, me, cut, found, piece)
        for piece in column_pieces(gate_cut.shape[2], FF_PARTS)
        for cut, found in ((gate_cut, gate_all), (up_cut, up_all))
    ]
    run(lines, [tokens_work(), *columns, *rows, gather_team(lines, me, upstream, upstream_all)], MIDDLE_PLAN)
    lines.finish()


def feed_kernel(
    zhs, input_all, upstream_all, gate_all, up_all, down_all,
    partial_down_out, partial_second_out, grad_gate_out, grad_up_out, down_part,
    second, upstream, gate_weight, up_weight, down_weight, gate, up, hidden, grad_gate, grad_up,
    partial_down, partial_second, grad_down, buffers, send, recv, local,
):
    me, lines = Place(zhs), Lines(send, recv, local)
    loads = [
        lines.copy(source, target)
        for source, target in (
            (input_all, second), (gate_all, gate_weight), (up_all, up_weight),
            (upstream_all, upstream), (down_all, down_weight),
        )
    ]
    me.greet()
    spawned, pieces = [], row_pieces(grad_down.shape[3], DOWN_PARTS)
    width, ff = gate_weight.shape
    tiles = [(start, min(256, ff - start)) for start in range(0, ff, 256)]

    def sums(piece, near):
        yield from sum_near(lines, me, grad_down, near, piece)
        rows = pl.ds(*piece)
        wait = lines.copy(grad_down.at[:, me.y, me.c, rows], down_part.at[:, rows])
        yield [wait], 0, None

    def work():
        yield loads[:3], 9, None
        for start, size in tiles:
            at = slice(start, start + size)
            gate_rows = dot(second[...], gate_weight[:, at])
            up_rows = dot(second[...], up_weight[:, at])
            gate[:, at], up[:, at] = gate_rows, up_rows
            hidden[:, at] = (gate_rows * jax.nn.sigmoid(gate_rows) * up_rows).astype(BF)
        yield loads[3:], 4.5, None
        for start in range(0, width, 512):
            block = dot_tn(hidden[...], upstream[:, start : start + 512]).astype(BF)
            grad_down[:, :, :, :, start : start + 512] = block.reshape(grad_down.shape[:4] + (512,))
        spawned.extend(sums(piece, near) for piece, near in zip(pieces, buffers))
        yield [], 5, None
        for start, size in tiles:
            at = slice(start, start + size)
            grad_hidden = dot_nt(upstream[...], down_weight[at])
            gate_rows = gate[:, at]
            sigmoid_gate = jax.nn.sigmoid(gate_rows)
            grad_gate[:, at] = (
                grad_hidden * up[:, at] * sigmoid_gate * (1.0 + gate_rows * (1.0 - sigmoid_gate))
            ).astype(BF)
            grad_up[:, at] = (grad_hidden * gate_rows * sigmoid_gate).astype(BF)
        waits = [lines.copy(grad_gate, grad_gate_out), lines.copy(grad_up, grad_up_out)]
        for start in range(0, width, 512):
            yield [], 2.5, None
            block = dot_nt(grad_gate[...], gate_weight[start : start + 512]) + dot_nt(
                grad_up[...], up_weight[start : start + 512]
            )
            partial_second[:, start : start + 512] = block.astype(BF)
        waits.append(lines.copy(partial_second, partial_second_out))
        for start in range(0, width, 1024):
            yield [], 2.5, None
            block = dot(hidden[...], down_weight[:, start : start + 1024])
            partial_down[:, start : start + 1024] = block.astype(BF)
        waits.append(lines.copy(partial_down, partial_down_out))
        yield waits, 0, None

    run(lines, [work(), spawned], FEED_PLAN)
    lines.finish()


def back_kernel(
    zhs, middle, upstream, gain, partial_down, partial_second, down_part, input_all, gate_in, up_in,
    out_all, queries_in, keys_in, values_in, mixed_in, tables,
    result, grad_middle, sums, down_total, gate_cut, up_cut, out_total, projected_out, bias_sums,
    own_down, passed_down, taken_down, own_second, passed_second, taken_second, attended,
    attended_all, out_weight, queries, keys, values, mixed, grad_mixed, grad_projected, grad_out,
    second, grad_side, grad_gate, grad_up, down_buffers, out_buffers, buffers, send, recv, local,
):
    me, lines = Place(zhs), Lines(send, recv, local)
    near_loads = [lines.copy(input_all, second), lines.copy(gate_in, grad_side)]
    loads = [
        lines.copy(source, target)
        for source, target in (
            (out_all, out_weight), (queries_in, queries), (keys_in, keys), (values_in, values), (mixed_in, mixed),
        )
    ]
    me.greet()
    spawned = []
    pieces = column_pieces(gate_cut.shape[2], FF_PARTS)

    def weights_work():
        number = 0
        for grad, cut in ((grad_gate, gate_cut), (grad_up, up_cut)):
            yield near_loads if grad is grad_gate else [lines.copy(up_in, grad_side)], 4.5, None
            ff = grad_side.shape[1]
            for start in range(0, ff, 256):
                size = min(256, ff - start)
                block = dot_tn(second[...], grad_side[:, start : start + size]).astype(BF)
                grad[:, :, :, :, :, :, start : start + size] = block.reshape(grad.shape[:6] + (size,))
            for piece in pieces:
                spawned.append(sum_columns(lines, me, grad, cut, buffers[number], piece))
                number += 1

    def tokens_work():
        yield [], 0, None
        yield from sum_team(lines, me, partial_second, own_second, passed_second, taken_second)
        sums[...] = jnp.zeros_like(sums)

        def body(rows):
            normed, scale_rows = norm_rows(middle[rows])
            grad = team_total(own_second, taken_second, rows)
            sums[0:1] += jnp.sum(grad * normed, axis=0, keepdims=True)
            sums[1:2] += jnp.sum(grad, axis=0, keepdims=True)
            grad = upstream[rows].astype(F32) + norm_back(grad * gain[...], normed, scale_rows)
            grad_middle[rows] = grad
            attended[rows] = grad.astype(BF)

        by_rows(middle.shape[0], body)
        yield from gather_team(lines, me, attended, attended_all)
        yield loads, 4, None
        count, width = mixed.shape[0], attended_all.shape[3]
        for start in range(0, width, 512):
            block = dot_tn(mixed[...], attended_all[:, :, :, start : start + 512].reshape(count, 512))
            grad_out[:, :, :, :, start : start + 512] = block.astype(BF).reshape(grad_out.shape[:4] + (512,))
        for at, piece in enumerate(row_pieces(out_total.shape[0], OUT_PARTS)):
            spawned.append(sum_rows(lines, me, grad_out, out_total, *out_buffers[at], piece))
        grad_mixed[...] = dot_nt(attended_all[...].reshape(count, width), out_weight[...]).astype(BF)
        yield [], 9, None
        yield from backward_attention(grad_mixed, tables, queries, keys, values, grad_projected)
        wait = lines.copy(grad_projected, projected_out)
        for start in range(0, grad_projected.shape[1], 256):
            block = jnp.sum(grad_projected[:, start : start + 256].astype(F32), axis=0, keepdims=True)
            bias_sums[:, start : start + 256] = block
        yield [wait], 0, None

    def result_work():
        yield [], 0, "s"
        yield from sum_team(lines, me, partial_down, own_down, passed_down, taken_down)

        def body(rows):
            result[rows] = (middle[rows] + team_total(own_down, taken_down, rows)).astype(BF)

        by_rows(middle.shape[0], body)

    far = [
        sum_far(lines, me, down_part, down_total, found, piece)
        for found, piece in zip(down_buffers, row_pieces(down_total.shape[0], DOWN_PARTS))
    ]
    run(lines, [tokens_work(), weights_work(), *far, result_work(), spawned], BACK_PLAN)
    lines.finish()


def leave_kernel(
    zhs, tokens, grad_middle, gain, second_sums, bias_sums, grad_projected, first_in, qkv_in,
    grad_inputs, sums, qkv_cut,
    first, weight, partial, grad_qkv, own, passed, taken, steps, buffers, send, recv, local,
):
    me, lines = Place(zhs), Lines(send, recv, local)
    loads = [lines.copy(first_in, first), lines.copy(qkv_in, weight)]
    me.greet()

    spawned = []
    pieces = column_pieces(qkv_cut.shape[2], QKV_PARTS)

    def tokens_work():
        yield loads, 3, None
        columns = grad_qkv.shape[6]
        for number in range(QKV_PARTS):
            _, start, size = pieces[number]
            for at in range(start, start + size, 256):
                block = dot_tn(first[...], grad_projected[:, at : at + 256]).astype(BF)
                grad_qkv[:, :, :, :, :, :, at : at + 256] = block.reshape(grad_qkv.shape[:6] + (256,))
            for at in (number, number + QKV_PARTS):
                spawned.append(sum_columns(lines, me, grad_qkv, qkv_cut, buffers[at], pieces[at]))
            yield [], 3 if number < QKV_PARTS - 1 else 7, None
        for at in range(weight.shape[0] // 256):
            block = dot_nt(grad_projected[...], weight[at * 256 : at * 256 + 256])
            partial[:, :, :, at * 256 : at * 256 + 256] = block.astype(BF).reshape(partial.shape[:3] + (256,))
        yield from sum_team(lines, me, partial, own, passed, taken)
        steps[0] = jnp.zeros_like(steps[0])
        steps[0, 2:4] = second_sums[0:2]
        part = bias_sums.shape[1] // 3
        block = part // zhs
        for number in range(3):
            for zh in range(zhs):
                at = ((me.s * zhs + zh) * 2 + me.zl) * block
                steps[0, 4 + number : 5 + number, pl.ds(pl.multiple_of(at, 64), block)] = bias_sums[
                    :, number * part + zh * block : number * part + (zh + 1) * block
                ]

        def body(rows):
            normed, scale_rows = norm_rows(tokens[rows].astype(F32))
            grad = team_total(own, taken, rows)
            steps[0, 0:1] += jnp.sum(grad * normed, axis=0, keepdims=True)
            steps[0, 1:2] += jnp.sum(grad, axis=0, keepdims=True)
            grad_inputs[rows] = grad_middle[rows] + norm_back(grad * gain[...], normed, scale_rows)

        by_rows(tokens.shape[0], body)
        groups = [
            [me.at(s=1 - me.s)], [me.at(zl=1 - me.zl)], [me.at(c=1 - me.c)], [me.at(y=1 - me.y)],
            [me.at(zh=zh) for zh in me.highs()],
        ]
        at = 0
        for group, link in zip(groups, ("s", "zl", "c", "y", "zh")):
            arrived = [
                lines.push(steps.at[at], steps.at[at + 1 + number], device, link)
                for number, device in enumerate(group)
            ]
            yield arrived, 0.3, None
            total = steps[at]
            for number in range(len(group)):
                total = total + steps[at + 1 + number]
            at += len(group) + 1
            steps[at] = total
        sums[...] = steps[at]

    run(lines, [tokens_work(), spawned], LEAVE_PLAN)
    lines.finish()


def near_buffers(zhs, size, width):
    return tuple(pltpu.VMEM(shape + (size, width), BF) for shape in ((zhs, 2), (zhs,)))


def far_buffers(zhs, size, width):
    return (
        pltpu.VMEM((size, width), BF), pltpu.VMEM((zhs - 1, size, width), BF), pltpu.VMEM((size, width), F32)
    )


def column_buffers(zhs, own, columns):
    return tuple(
        pltpu.VMEM(shape + (own, columns), BF) for shape in ((zhs, 2, 2), (zhs, 2), (zhs - 1, 2))
    )


IN_HBM = pl.BlockSpec(memory_space=pl.ANY)
IN_VMEM = pl.BlockSpec(memory_space=pltpu.VMEM)


def call(kernel, zhs, number, inputs, outputs, scratch, copies, locals_, limit):
    return pl.pallas_call(
        lambda *refs: kernel(zhs, *refs),
        out_shape=[jax.ShapeDtypeStruct(shape, kind) for shape, kind, _ in outputs],
        in_specs=[spec for _, spec in inputs],
        out_specs=[spec for _, _, spec in outputs],
        scratch_shapes=[
            *scratch,
            pltpu.SemaphoreType.DMA((copies,)),
            pltpu.SemaphoreType.DMA((copies,)),
            pltpu.SemaphoreType.DMA((locals_,)),
        ],
        compiler_params=pltpu.CompilerParams(
            collective_id=number, has_side_effects=True, vmem_limit_bytes=limit << 20
        ),
    )(*[array for array, _ in inputs])


def per_device(
    tokens, cotangent, norm1_gain, norm1_bias, qkv_weight, qkv_bias, out_weight,
    norm2_gain, norm2_bias, gate_weight, up_weight, down_weight,
):
    zh = lax.axis_size("zh")
    rows = tokens.shape[1]
    width = tokens.shape[2]
    own = qkv_weight.shape[0]
    ff = gate_weight.shape[1]
    ff_own = down_weight.shape[0]
    half = lax.axis_size("seq")
    length = rows * half
    seqs = lax.axis_size("zl")
    team = half * seqs
    part = width // team
    ff_part = ff // team
    devices = width // own
    tokens, cotangent = tokens[0], cotangent[0]
    index = (lax.axis_index("seq") * (devices // half)
             + ((lax.axis_index("zh") * 2 + lax.axis_index("zl")) * 2 + lax.axis_index("y")) * 2
             + lax.axis_index("c"))

    def cut_columns(shard, parts):
        block = shard.shape[1] // parts // (half * zh * seqs)
        cut = shard.reshape(own, parts, half, zh, seqs, block).transpose(2, 4, 0, 1, 3, 5)
        return cut.reshape(team, own, parts * zh * block)

    def join_columns(cut, parts):
        block = cut.shape[2] // parts // zh
        cut = cut.reshape(half, seqs, own, parts, zh, block).transpose(2, 3, 0, 4, 1, 5)
        return cut.reshape(own, -1).astype(F32)

    def mine_columns(whole, parts):
        block = whole.shape[0] // parts // (half * zh * seqs)
        cut = whole.reshape(parts, half, zh, seqs, block)
        cut = lax.dynamic_index_in_dim(cut, lax.axis_index("seq"), 1, keepdims=False)
        cut = lax.dynamic_index_in_dim(cut, lax.axis_index("zl"), 2, keepdims=False)
        return cut.reshape(-1)

    small = jnp.concatenate([norm1_gain, norm1_bias, norm2_gain, norm2_bias, qkv_bias]).astype(F32)
    small = jnp.pad(small, (0, 1024 - small.shape[0])).reshape(8, 128)
    small = jnp.broadcast_to(small, (team, 8, 128))
    token_shape = (seqs, half, rows, width)
    owners = (half, zh, seqs, 2, 2)
    count = team * rows
    limit = 56
    tables = rotary_tables(length)
    tokens_all, small_all, qkv_all, out_all = call(
        enter_kernel, zh, 0,
        [(tokens, IN_HBM), (small, IN_HBM), (cut_columns(qkv_weight, 3), IN_HBM), (out_weight, IN_HBM)],
        [
            (token_shape, BF, IN_HBM),
            (owners + (8, 128), F32, IN_HBM),
            (owners + (own, 3 * part), BF, IN_HBM),
            ((zh, 2, 2, own, width), BF, IN_HBM),
        ],
        [], 3 + (2 + OUT_PARTS + 2 * QKV_PARTS) * (zh + 4), 24, 16,
    )
    small = small_all.reshape(devices, 1024)
    first_gain = small[:, :own].reshape(1, width)
    first_bias = small[:, own : 2 * own].reshape(1, width)
    second_gain = small[:, 2 * own : 3 * own].reshape(1, width)
    second_bias = small[:, 3 * own : 4 * own].reshape(1, width)
    qkv_offset = mine_columns(small[:, 4 * own : 7 * own].reshape(-1), 3).reshape(1, 3 * part)
    qkv_matrix = qkv_all.reshape(width, 3 * part)
    out_matrix = out_all.reshape(part, width)

    token_scratch = [
        pltpu.VMEM((rows, width), BF), pltpu.VMEM((rows, width), BF), pltpu.VMEM((3, rows, width), BF)
    ]
    head_shape = (count, part)
    heads = [(head_shape, BF, IN_HBM)] * 4
    head_scratch = [pltpu.VMEM(head_shape, BF)] * 4
    (
        middle, first_input, queries, keys, values, mixed, upstream_all, input_all, gate_all, up_all, down_all,
    ) = call(
        middle_kernel, zh, 1,
        [
            (tokens, IN_VMEM), (cotangent, IN_HBM), (tokens_all.reshape(count, width), IN_HBM),
            (qkv_matrix, IN_HBM), (out_matrix, IN_HBM),
            (cut_columns(gate_weight, 1), IN_HBM), (cut_columns(up_weight, 1), IN_HBM), (down_weight, IN_HBM),
            (first_gain, IN_VMEM), (first_bias, IN_VMEM), (qkv_offset, IN_VMEM),
            (second_gain, IN_VMEM), (second_bias, IN_VMEM), (tables, IN_VMEM),
        ],
        [
            ((rows, width), F32, IN_VMEM),
            ((count, width), BF, IN_HBM),
            *heads,
            (token_shape, BF, IN_HBM),
            (token_shape, BF, IN_HBM),
            (owners + (own, ff_part), BF, IN_HBM),
            (owners + (own, ff_part), BF, IN_HBM),
            ((zh, 2, 2, ff_own, width), BF, IN_HBM),
        ],
        [
            pltpu.VMEM((count, width), BF), pltpu.VMEM((count, width), BF),
            pltpu.VMEM((width, 3 * part), BF), pltpu.VMEM((part, width), BF),
            *head_scratch, pltpu.VMEM(token_shape, BF),
            *token_scratch, pltpu.VMEM((rows, width), BF),
        ],
        9 + (DOWN_PARTS + 4 * FF_PARTS) * (zh + 4), 40, limit,
    )
    second_input = input_all.reshape(count, width)
    ff_shape = (count, ff_part)
    down_pieces = [size for _, size in row_pieces(ff_own, DOWN_PARTS)]
    partial_down, partial_second, grad_gate, grad_up, down_part = call(
        feed_kernel, zh, 4,
        [
            (second_input, IN_HBM), (upstream_all.reshape(count, width), IN_HBM),
            (gate_all.reshape(width, ff_part), IN_HBM), (up_all.reshape(width, ff_part), IN_HBM),
            (down_all.reshape(ff_part, width), IN_HBM),
        ],
        [
            ((count, width), BF, IN_HBM),
            ((count, width), BF, IN_HBM),
            (ff_shape, BF, IN_HBM),
            (ff_shape, BF, IN_HBM),
            ((zh, ff_own, width), BF, IN_HBM),
        ],
        [
            pltpu.VMEM((count, width), BF), pltpu.VMEM((count, width), BF),
            pltpu.VMEM((width, ff_part), BF), pltpu.VMEM((width, ff_part), BF), pltpu.VMEM((ff_part, width), BF),
            pltpu.VMEM(ff_shape, F32), pltpu.VMEM(ff_shape, F32),
            *[pltpu.VMEM(ff_shape, BF)] * 3,
            pltpu.VMEM((count, width), BF), pltpu.VMEM((count, width), BF), pltpu.VMEM(down_all.shape, BF),
            [near_buffers(zh, size, width) for size in down_pieces],
        ],
        DOWN_PARTS * 2, 32, 60,
    )
    result, grad_middle, second_sums, down_total, gate_cut, up_cut, out_total, grad_projected, bias_sums = call(
        back_kernel, zh, 2,
        [
            (middle, IN_VMEM), (cotangent, IN_VMEM), (second_gain, IN_VMEM),
            (partial_down.reshape(token_shape), IN_HBM), (partial_second.reshape(token_shape), IN_HBM),
            (down_part, IN_HBM), (second_input, IN_HBM), (grad_gate, IN_HBM), (grad_up, IN_HBM),
            (out_matrix, IN_HBM), (queries, IN_HBM), (keys, IN_HBM), (values, IN_HBM), (mixed, IN_HBM),
            (tables, IN_VMEM),
        ],
        [
            ((rows, width), BF, IN_VMEM),
            ((rows, width), F32, IN_VMEM),
            ((8, width), F32, IN_VMEM),
            ((ff_own, width), F32, IN_HBM),
            ((team, own, ff_part), BF, IN_HBM),
            ((team, own, ff_part), BF, IN_HBM),
            ((own, width), F32, IN_HBM),
            ((count, 3 * part), BF, IN_HBM),
            ((1, 3 * part), F32, IN_VMEM),
        ],
        [
            *token_scratch, *token_scratch, pltpu.VMEM((rows, width), BF), pltpu.VMEM(token_shape, BF),
            pltpu.VMEM((part, width), BF), *head_scratch, pltpu.VMEM(head_shape, BF),
            pltpu.VMEM((count, 3 * part), BF), pltpu.VMEM(out_all.shape, BF),
            pltpu.VMEM((count, width), BF), pltpu.VMEM(ff_shape, BF),
            pltpu.VMEM(gate_all.shape, BF), pltpu.VMEM(gate_all.shape, BF),
            [far_buffers(zh, size, width) for size in down_pieces],
            [
                (near_buffers(zh, size, width), far_buffers(zh, size, width))
                for _, size in row_pieces(own, OUT_PARTS)
            ],
            [
                column_buffers(zh, own, size)
                for _ in range(2)
                for _, _, size in column_pieces(ff_part, FF_PARTS)
            ],
        ],
        9 + (OUT_PARTS + DOWN_PARTS + 4 * FF_PARTS) * (zh + 4), 50, 60,
    )
    grad_inputs, sums, qkv_cut = call(
        leave_kernel, zh, 3,
        [
            (tokens, IN_VMEM), (grad_middle, IN_VMEM), (first_gain, IN_VMEM),
            (second_sums, IN_VMEM), (bias_sums, IN_VMEM), (grad_projected, IN_VMEM),
            (first_input, IN_HBM), (qkv_matrix, IN_HBM),
        ],
        [
            ((rows, width), F32, IN_VMEM),
            ((8, width), F32, IN_VMEM),
            ((team, own, 3 * part), BF, IN_HBM),
        ],
        [
            pltpu.VMEM((count, width), BF), pltpu.VMEM((width, 3 * part), BF), pltpu.VMEM(token_shape, BF),
            pltpu.VMEM(qkv_all.shape, BF),
            *token_scratch, pltpu.VMEM((zh + 9, 8, width), F32),
            [column_buffers(zh, own, size) for _, _, size in column_pieces(3 * part, QKV_PARTS)],
        ],
        zh + 6 + (2 * QKV_PARTS) * (zh + 4), 24, limit,
    )

    def mine(vector_row, size):
        return lax.dynamic_slice_in_dim(vector_row, index * size, size, 0)

    return (
        result[None],
        grad_inputs[None],
        mine(sums[0], own),
        mine(sums[1], own),
        join_columns(qkv_cut, 3),
        mine(sums[4:7].reshape(-1), 3 * own),
        out_total,
        mine(sums[2], own),
        mine(sums[3], own),
        join_columns(gate_cut, 1),
        join_columns(up_cut, 1),
        down_total,
    )


def solution(mesh):
    half, shards = mesh.shape["seq"], mesh.shape["shard"]
    fine = jax.sharding.Mesh(mesh.devices.reshape(half, shards // 8, 2, 2, 2), ALL)
    token = P(("zh", "zl", "y", "c"), "seq", None)
    row = P(ALL)

    def program(*arguments):
        whole_tiles = arguments[-1].shape[0] // (half * shards) % ROWS == 0
        return jax.shard_map(
            per_device if whole_tiles else plain_device,
            mesh=fine,
            in_specs=(token, token) + (row,) * 10,
            out_specs=(token, token) + (row,) * 10,
            check_vma=False,
        )(*arguments)

    return program
```

```python
import jax
import jax.numpy as jnp
import numpy as np
from jax import lax
from jax.experimental import pallas as pl
from jax.experimental.pallas import tpu as pltpu
from jax.sharding import PartitionSpec as P

HEADS = 32
HEAD_DIM = 64
ROTARY = 16
TEAM = ("seq", "zl")
PEERS = ("zh", "y", "c")
ALL = ("seq", "zh", "zl", "y", "c")
BF = jnp.bfloat16
F32 = jnp.float32


def norm_rows(values):
    centre = jnp.mean(values, axis=-1, keepdims=True)
    centred = values - centre
    spread = jnp.mean(centred * centred, axis=-1, keepdims=True)
    scale_rows = lax.rsqrt(spread + 1e-05)
    return (centred * scale_rows, scale_rows)


def norm_back(grad_normed, normed, scale_rows):
    return scale_rows * (
        grad_normed
        - jnp.mean(grad_normed, axis=-1, keepdims=True)
        - normed * jnp.mean(grad_normed * normed, axis=-1, keepdims=True)
    )


def rotate(values, positions, direction):
    halves = ROTARY // 2
    frequency = 10000.0 ** (-2.0 * jnp.arange(halves, dtype=F32) / ROTARY)
    angles = positions.astype(F32)[:, None] * frequency[None, :]
    cosine_table = jnp.cos(angles)[:, None, :]
    sine_table = jnp.sin(angles)[:, None, :] * direction
    first_half = values[..., :halves]
    second_half = values[..., halves:ROTARY]
    return jnp.concatenate(
        [
            first_half * cosine_table - second_half * sine_table,
            second_half * cosine_table + first_half * sine_table,
            values[..., ROTARY:],
        ],
        axis=-1,
    )


def dot(left, right):
    return jnp.dot(left, right, preferred_element_type=F32)


def dot_nt(left, right):
    return lax.dot_general(left, right, (((1,), (1,)), ((), ())), preferred_element_type=F32)


def dot_tn(left, right):
    return lax.dot_general(left, right, (((0,), (0,)), ((), ())), preferred_element_type=F32)


def plain_device(
    tokens, cotangent, norm1_gain, norm1_bias, qkv_weight, qkv_bias, out_weight,
    norm2_gain, norm2_bias, gate_weight, up_weight, down_weight,
):
    zh = lax.axis_size("zh")
    rows = tokens.shape[1]
    width = tokens.shape[2]
    own = qkv_weight.shape[0]
    ff = gate_weight.shape[1]
    half = lax.axis_size("seq")
    length = rows * half
    team = half * lax.axis_size("zl")
    seqs = lax.axis_size("zl")

    def cut_columns(shard, parts):
        block = shard.shape[1] // parts // (half * zh * seqs)
        cut = shard.reshape(own, parts, half, zh, seqs, block).transpose(2, 4, 0, 1, 3, 5)
        return cut.reshape(team, own, parts * zh * block)

    def join_columns(cut, parts):
        block = cut.shape[2] // parts // zh
        cut = cut.reshape(half, seqs, own, parts, zh, block).transpose(2, 3, 0, 4, 1, 5)
        return cut.reshape(own, -1)

    def mine_columns(whole, parts):
        block = whole.shape[0] // parts // (half * zh * seqs)
        cut = whole.reshape(parts, half, zh, seqs, block)
        cut = lax.dynamic_index_in_dim(cut, lax.axis_index("seq"), 1, keepdims=False)
        cut = lax.dynamic_index_in_dim(cut, lax.axis_index("zl"), 2, keepdims=False)
        return cut.reshape(-1)

    def to_owner_order(values):
        n = values.shape[0]
        return values.reshape(n, half, zh, seqs, 4, own).transpose(0, 2, 4, 1, 3, 5).reshape(n, width)

    def from_owner_order(values):
        n = values.shape[0]
        return values.reshape(n, zh, 4, half, seqs, own).transpose(0, 3, 1, 4, 2, 5).reshape(n, width)

    def gather_columns(shard, parts):
        cut = cut_columns(shard, parts)
        cut = lax.all_to_all(cut, TEAM, split_axis=0, concat_axis=0, tiled=True)
        return lax.all_gather(cut.reshape(team * own, -1), PEERS, axis=0, tiled=True)

    def gather_rows(shard):
        return lax.all_gather(shard, PEERS, axis=0, tiled=True)

    def gather_tokens(values):
        return lax.all_gather(values, ("zl", "seq"), axis=0, tiled=True)

    def sum_tokens(values):
        return lax.psum_scatter(values.astype(BF), ("zl", "seq"), scatter_dimension=0, tiled=True).astype(F32)

    def sum_rows(values):
        return lax.psum_scatter(values.astype(BF), PEERS, scatter_dimension=0, tiled=True)

    def sum_columns(values, parts):
        part = sum_rows(values).reshape(team, own, -1)
        part = lax.all_to_all(part, TEAM, split_axis=0, concat_axis=0, tiled=True)
        return join_columns(part, parts).astype(F32)

    small = jnp.concatenate([norm1_gain, norm1_bias, norm2_gain, norm2_bias, qkv_bias])
    small = lax.all_gather(small, ALL, axis=0, tiled=False)
    first_gain = small[:, :own].reshape(-1).astype(F32)
    first_bias = small[:, own : 2 * own].reshape(-1).astype(F32)
    second_gain = small[:, 2 * own : 3 * own].reshape(-1).astype(F32)
    second_bias = small[:, 3 * own : 4 * own].reshape(-1).astype(F32)
    qkv_offset = mine_columns(small[:, 4 * own :].reshape(-1), 3).astype(F32)

    inputs = tokens[0].astype(F32)
    first_normed, first_scale = norm_rows(inputs)
    first_own = to_owner_order((first_normed * first_gain + first_bias).astype(BF))
    first_input = gather_tokens(first_own)
    qkv_matrix = gather_columns(qkv_weight, 3)
    out_matrix = gather_rows(out_weight)
    gate_matrix = gather_columns(gate_weight, 1)
    up_matrix = gather_columns(up_weight, 1)
    down_matrix = gather_rows(down_weight)
    upstream = gather_tokens(cotangent[0])

    projected = dot(first_input, qkv_matrix) + qkv_offset
    part = width // team
    group_heads = part // HEAD_DIM
    positions = jnp.tile(jnp.arange(length, dtype=jnp.int32), seqs)

    def heads_of(values):
        return values.reshape(seqs, length, group_heads, HEAD_DIM).transpose(0, 2, 1, 3)

    def unheads(values):
        return values.transpose(0, 2, 1, 3).reshape(seqs * length, part)

    queries = heads_of(rotate(projected[:, :part].reshape(-1, group_heads, HEAD_DIM), positions, 1.0).astype(BF))
    keys = heads_of(rotate(projected[:, part : 2 * part].reshape(-1, group_heads, HEAD_DIM), positions, 1.0).astype(BF))
    values = heads_of(projected[:, 2 * part :].astype(BF))
    causal = jnp.arange(length)[:, None] >= jnp.arange(length)[None, :]
    scores = jnp.einsum("shqd,shkd->shqk", queries, keys, preferred_element_type=F32) * 0.125
    scores = jnp.where(causal, scores, -1e30)
    highest = jnp.max(scores, axis=-1, keepdims=True)
    exponent = jnp.exp(scores - highest)
    probs = exponent / jnp.sum(exponent, axis=-1, keepdims=True)
    probs_low = probs.astype(BF)
    mixed = unheads(jnp.einsum("shqk,shkd->shqd", probs_low, values, preferred_element_type=F32).astype(BF))
    middle = inputs + sum_tokens(dot(mixed, out_matrix))

    second_normed, second_scale = norm_rows(middle)
    second_own = to_owner_order((second_normed * second_gain + second_bias).astype(BF))
    second_input = gather_tokens(second_own)
    gate_rows = dot(second_input, gate_matrix)
    up_rows = dot(second_input, up_matrix)
    sigmoid_gate = jax.nn.sigmoid(gate_rows)
    silu_gate = gate_rows * sigmoid_gate
    hidden = (silu_gate * up_rows).astype(BF)
    result = middle + sum_tokens(dot(hidden, down_matrix))

    down_total = sum_rows(dot_tn(hidden, upstream)).astype(F32)
    grad_hidden = dot_nt(upstream, down_matrix)
    grad_gate = (grad_hidden * up_rows * sigmoid_gate * (1.0 + gate_rows * (1.0 - sigmoid_gate))).astype(BF)
    grad_up = (grad_hidden * silu_gate).astype(BF)
    gate_total = sum_columns(dot_tn(second_input, grad_gate), 1)
    up_total = sum_columns(dot_tn(second_input, grad_up), 1)
    grad_second = from_owner_order(sum_tokens(dot_nt(grad_gate, gate_matrix) + dot_nt(grad_up, up_matrix)))
    grad_middle = cotangent[0].astype(F32) + norm_back(grad_second * second_gain, second_normed, second_scale)
    grad_attended = gather_tokens(grad_middle.astype(BF))
    out_total = sum_rows(dot_tn(mixed, grad_attended)).astype(F32)
    grad_mixed = heads_of(dot_nt(grad_attended, out_matrix).astype(BF))
    grad_probs = jnp.einsum("shqd,shkd->shqk", grad_mixed, values, preferred_element_type=F32)
    grad_scores = (probs * (grad_probs - jnp.sum(probs * grad_probs, axis=-1, keepdims=True))).astype(BF)
    grad_queries = (jnp.einsum("shqk,shkd->shqd", grad_scores, keys, preferred_element_type=F32) * 0.125).astype(BF)
    grad_keys = (jnp.einsum("shqk,shqd->shkd", grad_scores, queries, preferred_element_type=F32) * 0.125).astype(BF)
    grad_values = jnp.einsum("shqk,shqd->shkd", probs_low, grad_mixed, preferred_element_type=F32).astype(BF)
    grad_queries = rotate(unheads(grad_queries).astype(F32).reshape(-1, group_heads, HEAD_DIM), positions, -1.0)
    grad_keys = rotate(unheads(grad_keys).astype(F32).reshape(-1, group_heads, HEAD_DIM), positions, -1.0)
    grad_projected = jnp.concatenate(
        [grad_queries.reshape(-1, part).astype(BF), grad_keys.reshape(-1, part).astype(BF), unheads(grad_values)],
        axis=1,
    )
    qkv_total = sum_columns(dot_tn(first_input, grad_projected), 3)
    grad_first = from_owner_order(sum_tokens(dot_nt(grad_projected, qkv_matrix)))
    grad_inputs = grad_middle + norm_back(grad_first * first_gain, first_normed, first_scale)

    bias_part = jnp.sum(grad_projected.astype(F32), axis=0).reshape(3, zh, -1)
    bias_whole = jnp.zeros((3, half, zh, seqs, bias_part.shape[2]), F32)
    bias_whole = lax.dynamic_update_slice(
        bias_whole, bias_part[:, None, :, None], (0, lax.axis_index("seq"), 0, lax.axis_index("zl"), 0)
    ).reshape(-1)
    count = width // own
    sums = jnp.concatenate(
        [
            jnp.sum(grad_first * first_normed, axis=0).reshape(count, own),
            jnp.sum(grad_first, axis=0).reshape(count, own),
            jnp.sum(grad_second * second_normed, axis=0).reshape(count, own),
            jnp.sum(grad_second, axis=0).reshape(count, own),
            bias_whole.reshape(count, 3 * own),
        ],
        axis=1,
    )
    sums = lax.psum_scatter(sums, ALL, scatter_dimension=0, tiled=True)[0]
    return (
        result.astype(BF)[None],
        grad_inputs[None],
        sums[:own],
        sums[own : 2 * own],
        qkv_total,
        sums[4 * own :],
        out_total,
        sums[2 * own : 3 * own],
        sums[3 * own : 4 * own],
        gate_total,
        up_total,
        down_total,
    )


MESH = pl.DeviceIdType.MESH
ROWS = 16
QKV_PARTS, QKV_GATHERS, OUT_PARTS, FF_PARTS, DOWN_PARTS = 2, 3, 2, 2, 4


class Place:
    def __init__(self, zhs):
        self.s, self.zh, self.zl, self.y, self.c = (lax.axis_index(axis) for axis in ALL)
        self.zhs = zhs

    def at(self, **changed):
        return tuple(changed.get(name, getattr(self, name)) for name in ("s", "zh", "zl", "y", "c"))

    def mates(self):
        for flip_s, flip_z in ((0, 1), (1, 0), (1, 1)):
            yield (1 - self.s if flip_s else self.s), (1 - self.zl if flip_z else self.zl)

    def highs(self):
        for step in range(1, self.zhs):
            yield (self.zh + step) % self.zhs

    def greet(self):
        partners = [self.at(s=s, zl=zl) for s, zl in self.mates()]
        partners += [self.at(zh=zh) for zh in self.highs()]
        partners += [self.at(y=1 - self.y), self.at(c=1 - self.c)]
        barrier = pltpu.get_barrier_semaphore()
        for partner in partners:
            pl.semaphore_signal(barrier, inc=1, device_id=partner, device_id_type=MESH)
        pl.semaphore_wait(barrier, len(partners))


class Traffic:
    def __init__(self):
        self.now, self.active = 0.0, []

    def start(self, demands):
        transfer = {"left": {link: time for link, time in demands.items()}, "done": None}
        self.active.append(transfer)
        return transfer

    def backlog(self, link):
        return sum(transfer["left"].get(link, 0.0) for transfer in self.active)

    def advance(self, until):
        while self.now < until:
            shares = {}
            for transfer in self.active:
                for link in transfer["left"]:
                    shares[link] = shares.get(link, 0) + 1
            step = until - self.now
            for transfer in self.active:
                for link, left in transfer["left"].items():
                    step = min(step, left * shares[link])
            self.now += step
            for transfer in list(self.active):
                transfer["left"] = {
                    link: left - step / shares[link]
                    for link, left in transfer["left"].items()
                    if left - step / shares[link] > 1e-6
                }
                if not transfer["left"]:
                    transfer["done"] = self.now + LATENCY
                    self.active.remove(transfer)


LATENCY = 2.0
ENTER_PLAN = {"small": (7.8, 43), "qkv0": (4.3, 33), "qkv1": (10.8, 0), "qkv2": (6.1, 1), "qkv3": (10.6, 19), "qkv4": (3.8, 13), "qkv5": (11.5, 41), "out0": (2.2, 0), "out1": (2.6, 32), "tokens": (5.8, 13), "cut": (7, 0)}
MIDDLE_PLAN = {"tokens": (0, 0), "ff0": (1, 0), "ff1": (3, 0), "ff2": (4, 0), "ff3": (5, 0), "ff4": (6, 0), "ff5": (7, 0), "ff6": (8, 0), "ff7": (9, 0), "down0": (2, 0), "down1": (10, 0), "down2": (11, 0), "down3": (12, 0), "upstream": (13, 0)}
FEED_PLAN = {"work": (4.9, 13), "down0": (4.9, 36), "down1": (1.5, 25), "down2": (1.8, 33), "down3": (1.2, 40)}
BACK_PLAN = {"tokens": (15.2, 0), "weights": (4.1, 1), "down0": (5.4, 4), "down1": (11.1, 9), "down2": (8.1, 19), "down3": (2.1, 0), "result": (9.7, 36), "ff0": (9.5, 0), "ff1": (5.8, 0), "ff2": (14.6, 4), "ff3": (7.3, 25), "ff4": (1.1, 18), "ff5": (3.7, 0), "ff6": (14.2, 21), "ff7": (0.3, 49), "out0": (13.7, 26), "out1": (5.5, 0)}
LEAVE_PLAN = {"tokens": (1.5, 0), "qkv0": (0.6, 55), "qkv2": (2, 24), "qkv1": (4.6, 47), "qkv3": (1.2, 9)}
BACKLOG = 12.0
LINK_TIME = {
    "s": {"s": 2 / 92e3},
    "zl": {"zl": 2 / 92e3},
    "y": {"y": 2 / 92e3},
    "zh": {"zh": 4 / 92e3, "zl": 2 / 92e3},
    "c": {"c": 1 / 300e3},
    "diagonal": {"s": 2 / 92e3, "zl": 2 / 92e3},
    "local": {"local": 1 / 1500e3},
}


class Lines:
    def __init__(self, send, recv, local):
        self.send, self.recv, self.local = send, recv, local
        self.sent, self.copied, self.traffic = [], 0, Traffic()

    def track(self, wait, source, link):
        size = int(np.prod(source.shape)) * jnp.dtype(source.dtype).itemsize
        return wait, self.traffic.start({name: time * size for name, time in LINK_TIME[link].items()})

    def push(self, source, target, device, link):
        at = len(self.sent)
        copy = pltpu.make_async_remote_copy(
            src_ref=source, dst_ref=target, send_sem=self.send.at[at], recv_sem=self.recv.at[at],
            device_id=device, device_id_type=MESH,
        )
        copy.start()
        self.sent.append(copy)
        return self.track(copy.wait_recv, source, link)

    def copy(self, source, target):
        copy = pltpu.make_async_copy(source, target, self.local.at[self.copied])
        copy.start()
        self.copied += 1
        return self.track(copy.wait, source, "local")

    def finish(self):
        for copy in self.sent:
            copy.wait_send()


def run(lines, works, plan, start=3.0):
    traffic, now = lines.traffic, start
    open_works, late, plan = [], None, dict(plan)

    def add(label, work):
        rank, begin = plan.get(label, (0.0, 0.0))
        open_works.append([rank, begin, work, next(work)])
        open_works.sort(key=lambda entry: entry[0])

    for work in works:
        if isinstance(work, list):
            late = work
        else:
            add(*work)
    while open_works:
        traffic.advance(now)
        for entry in open_works:
            waits, cost, link = entry[3]
            arrived = all(transfer["done"] is not None and transfer["done"] <= now for _, transfer in waits)
            if arrived and now >= entry[1] and (link is None or traffic.backlog(link) < BACKLOG):
                break
        else:
            now += 0.25
            continue
        for wait, _ in waits:
            wait()
        entry[1], entry[3] = 0.0, next(entry[2], None)
        now += cost + 0.15
        if entry[3] is None:
            open_works.remove(entry)
        while late:
            add(*late.pop(0))


def gather_team(lines, me, source, whole):
    yield [], 0, None
    mine, other = whole.at[me.zl, me.s], whole.at[1 - me.zl, me.s]
    across = lines.push(source, mine, me.at(zl=1 - me.zl), "zl")
    waits = [lines.copy(source, mine), lines.push(source, mine, me.at(s=1 - me.s), "s")]
    yield [across], 0, None
    waits.append(lines.push(other, other, me.at(s=1 - me.s), "s"))
    yield waits, 0, None


def gather_columns(lines, me, cut, whole, piece):
    other, start, size = piece
    s, columns = 1 - me.s if other else me.s, pl.ds(start, size)
    yield [], 0, "s"
    waits = []
    for flip in (0, 1):
        zl = 1 - me.zl if flip else me.zl
        for source, at in cut(s, zl, start, size):
            mine = whole.at[me.s, me.zh, me.zl, me.y, me.c, :, pl.ds(at, source.shape[1])]
            if other or flip:
                link = "diagonal" if other and flip else "s" if other else "zl"
                waits.append(lines.push(source, mine, me.at(s=s, zl=zl), link))
            else:
                waits.append(lines.copy(source, mine))
    yield waits, 0, "zh"
    part = whole.at[s, me.zh, :, me.y, me.c, :, columns]
    waits = [lines.push(part, part, me.at(zh=zh), "zh") for zh in me.highs()]
    yield waits, 0, "y"
    part = whole.at[s, :, :, me.y, me.c, :, columns]
    wait = lines.push(part, part, me.at(y=1 - me.y), "y")
    yield [wait], 0, None
    part = whole.at[s, :, :, :, me.c, :, columns]
    wait = lines.push(part, part, me.at(c=1 - me.c), "c")
    yield [wait], 0, None


def ready_cut(cut):
    return lambda s, zl, start, size: [(cut.at[s * 2 + zl, :, pl.ds(start, size)], start)]


def block_cut(zhs, shard, block):
    def cut(s, zl, start, size):
        found = []
        for at in range(start, start + size, block):
            number, zh = at // (zhs * block), at // block % zhs
            column = (number * 4 * zhs + (s * zhs + zh) * 2 + zl) * block
            found.append((shard.at[:, pl.ds(pl.multiple_of(column, block), block)], at))
        return found

    return cut


def swap_halves(left, right):
    width = left.shape[1]
    first = lax.broadcasted_iota(jnp.int32, (1, width), 1) < width // 2
    return (
        jnp.where(first, left, pltpu.roll(right, width // 2, 1)),
        jnp.where(first, pltpu.roll(left, width // 2, 1), right),
    )


def gather_rows(lines, me, source, whole, start, size):
    rows = pl.ds(start, size)
    yield [], 0, "zh"
    mine = whole.at[me.zh, me.y, me.c, rows]
    waits = [lines.copy(source.at[rows], mine)]
    waits += [lines.push(source.at[rows], mine, me.at(zh=zh), "zh") for zh in me.highs()]
    yield waits, 0, "y"
    part = whole.at[:, me.y, me.c, rows]
    wait = lines.push(part, part, me.at(y=1 - me.y), "y")
    yield [wait], 0, None
    part = whole.at[:, :, me.c, rows]
    wait = lines.push(part, part, me.at(c=1 - me.c), "c")
    yield [wait], 0, None


def add_into(target, sources, result=None):
    result = target if result is None else result

    def step(at, carry):
        rows = pl.ds(pl.multiple_of(at * ROWS, ROWS), ROWS)
        total = target[rows].astype(F32)
        for source in sources:
            total = total + source[rows].astype(F32)
        result[rows] = total.astype(result.dtype)
        return carry

    lax.fori_loop(0, target.shape[0] // ROWS, step, 0)


def add_time(*refs):
    return sum(int(np.prod(ref.shape)) for ref in refs) * ADD_TIME


ADD_TIME = 1.6e-6


def sum_columns(lines, me, grad, cut, buffers, piece):
    first, second, third = buffers
    other, start, size = piece
    s, columns = 1 - me.s if other else me.s, pl.ds(start, size)
    mine = grad.at[s, :, :, :, me.c, :, columns]
    yield [], 0, "c"
    wait = lines.push(grad.at[s, :, :, :, 1 - me.c, :, columns], first, me.at(c=1 - me.c), "c")
    yield [wait], add_time(first) / 2, "y"

    def fold(y):
        for zh in range(me.zhs):
            for zl in range(2):
                add_into(mine.at[zh, zl, y], [first.at[zh, zl, y]])

    fold(1 - me.y)
    wait = lines.push(mine.at[:, :, 1 - me.y], second, me.at(y=1 - me.y), "y")
    yield [], add_time(first) / 2, None
    fold(me.y)
    yield [wait], add_time(second), "zh"
    waits = []
    for step, zh in enumerate([*me.highs(), me.zh]):
        for zl in range(2):
            add_into(mine.at[zh, zl, me.y], [second.at[zh, zl]])
        if step < me.zhs - 1:
            waits.append(lines.push(mine.at[zh, :, me.y], third.at[step], me.at(zh=zh), "zh"))
    yield waits, add_time(third), None
    for zl in range(2):
        add_into(mine.at[me.zh, zl, me.y], [third.at[step, zl] for step in range(me.zhs - 1)])
    waits = []
    for flip in (0, 1):
        zl = 1 - me.zl if flip else me.zl
        source, target = mine.at[me.zh, zl, me.y], cut.at[me.s * 2 + me.zl, :, columns]
        if other or flip:
            link = "diagonal" if other and flip else "s" if other else "zl"
            waits.append(lines.push(source, target, me.at(s=s, zl=zl), link))
        else:
            waits.append(lines.copy(source, target))
    yield waits, 0, None


def sum_near(lines, me, grad, buffers, piece):
    first, second = buffers
    rows = pl.ds(*piece)
    mine = grad.at[:, :, me.c, rows]
    yield [], 0, "c"
    wait = lines.push(grad.at[:, :, 1 - me.c, rows], first, me.at(c=1 - me.c), "c")
    yield [wait], add_time(first) / 2, "y"
    for zh in range(me.zhs):
        add_into(mine.at[zh, 1 - me.y], [first.at[zh, 1 - me.y]])
    wait = lines.push(mine.at[:, 1 - me.y], second, me.at(y=1 - me.y), "y")
    yield [], add_time(first) / 2, None
    for zh in range(me.zhs):
        add_into(mine.at[zh, me.y], [first.at[zh, me.y]])
    yield [wait], add_time(second), None
    for zh in range(me.zhs):
        add_into(mine.at[zh, me.y], [second.at[zh]])


def sum_far(lines, me, part, total, buffers, piece):
    mine, third, final = buffers
    rows = pl.ds(*piece)
    yield [], 0, "zh"
    waits = [lines.copy(part.at[me.zh, rows], mine)]
    for step, zh in enumerate(me.highs()):
        waits.append(lines.push(part.at[zh, rows], third.at[step], me.at(zh=zh), "zh"))
    yield waits, add_time(third), None
    add_into(mine, [third.at[step] for step in range(me.zhs - 1)], final)
    wait = lines.copy(final, total.at[rows])
    yield [wait], 0, None


def sum_rows(lines, me, grad, total, near, far, piece):
    yield from sum_near(lines, me, grad, near, piece)
    yield from sum_far(lines, me, grad.at[:, me.y, me.c], total, far, piece)


def sum_team(lines, me, partial, own, passed, taken):
    first = [
        lines.copy(partial.at[1 - me.zl, me.s], passed),
        lines.push(partial.at[1 - me.zl, 1 - me.s], taken.at[0], me.at(s=1 - me.s), "s"),
    ]
    waits = [
        lines.push(partial.at[me.zl, 1 - me.s], taken.at[1], me.at(s=1 - me.s), "s"),
        lines.copy(partial.at[me.zl, me.s], own),
    ]
    yield first, add_time(passed), None
    add_into(passed, [taken.at[0]])
    waits.append(lines.push(passed, taken.at[2], me.at(zl=1 - me.zl), "zl"))
    yield waits, 3, None


def team_total(own, taken, rows):
    return own[rows].astype(F32) + taken[1, rows].astype(F32) + taken[2, rows].astype(F32)


def by_rows(count, body):
    def step(at, carry):
        body(pl.ds(pl.multiple_of(at * ROWS, ROWS), ROWS))
        return carry

    lax.fori_loop(0, count // ROWS, step, 0)


def row_pieces(size, parts):
    tiles, pieces, start = size // ROWS, [], 0
    for part in range(parts):
        count = (tiles * (part + 1) // parts - tiles * part // parts) * ROWS
        pieces.append((start, count))
        start += count
    return pieces


def column_pieces(columns, parts):
    lanes, pieces, start = columns // 128, [], 0
    for part in range(parts):
        size = (lanes * (part + 1) // parts - lanes * part // parts) * 128
        pieces.append((start, size))
        start += size
    return [(other, *piece) for other in (False, True) for piece in pieces]


def turn_pairs(values, tables, sign):
    return (
        values * tables[0]
        + pltpu.roll(values, 128 - ROTARY // 2, 1) * (tables[1] * sign)
        + pltpu.roll(values, ROTARY // 2, 1) * (tables[2] * sign)
    )


def rotary_tables(length):
    lane = np.arange(128) % HEAD_DIM
    halves = ROTARY // 2
    frequency = np.float32(10000.0) ** (np.float32(-2.0) * np.arange(halves, dtype=np.float32) / np.float32(ROTARY))
    angles = np.arange(length, dtype=np.float32)[:, None] * frequency[lane % halves][None, :]
    rotated = lane < ROTARY
    return np.stack([
        np.where(rotated, np.cos(angles), 1.0),
        np.where(lane < halves, -np.sin(angles), 0.0),
        np.where(rotated & (lane >= halves), np.sin(angles), 0.0),
    ]).astype(np.float32)


def lane_masks():
    lane = lax.broadcasted_iota(jnp.int32, (1, 128), 1)
    return [(lane < HEAD_DIM).astype(F32).astype(BF), (lane >= HEAD_DIM).astype(F32).astype(BF)], lane < HEAD_DIM


def softmax_rows(query, key):
    length = query.shape[0]
    scores = dot_nt(query, key) * 0.125
    below = lax.broadcasted_iota(jnp.int32, (length, length), 0) >= lax.broadcasted_iota(
        jnp.int32, (length, length), 1
    )
    scores = jnp.where(below, scores, -1e30)
    exponent = jnp.exp(scores - jnp.max(scores, axis=-1, keepdims=True))
    return exponent / jnp.sum(exponent, axis=-1, keepdims=True)


def pairs_of(seq, length, part, body):
    def step(at, carry):
        body(pl.ds(seq * length, length), pl.ds(pl.multiple_of(at * 128, 128), 128))
        return carry

    lax.fori_loop(0, part // 128, step, 0)


def forward_attention(first, weight, offset, tables, queries, keys, values, mixed):
    length, part = tables.shape[1], queries.shape[1]
    seqs = queries.shape[0] // length
    for number, target in enumerate((queries, keys, values)):
        for start in range(0, part, 256):
            at = number * part + start
            block = dot(first[...], weight[:, at : at + 256]) + offset[:, at : at + 256]
            if target is values:
                target[:, start : start + 256] = block.astype(BF)
                continue
            for seq in range(seqs):
                for lanes in range(0, 256, 128):
                    rows = slice(seq * length, (seq + 1) * length)
                    turned = turn_pairs(block[rows, lanes : lanes + 128], tables, 1.0)
                    target[rows, start + lanes : start + lanes + 128] = turned.astype(BF)
        yield [], 2.5 if number < 2 else 6, None

    masks, left = lane_masks()
    for seq in range(seqs):

        def body(rows, lanes):
            query, key, value = queries[rows, lanes], keys[rows, lanes], values[rows, lanes]
            sides = [dot(softmax_rows(query * mask, key).astype(BF), value) for mask in masks]
            mixed[rows, lanes] = jnp.where(left, *sides).astype(BF)

        pairs_of(seq, length, part, body)
        yield [], 6 if seq < seqs - 1 else 2, None


def backward_attention(grad_mixed, tables, queries, keys, values, grad_projected):
    length, part = tables.shape[1], queries.shape[1]
    seqs = queries.shape[0] // length
    masks, left = lane_masks()
    for seq in range(seqs):

        def body(rows, lanes):
            query, key, value = queries[rows, lanes], keys[rows, lanes], values[rows, lanes]
            grad = grad_mixed[rows, lanes]
            sides = []
            for mask in masks:
                probs = softmax_rows(query * mask, key)
                grad_probs = dot_nt(grad * mask, value)
                grad_scores = (
                    probs * (grad_probs - jnp.sum(probs * grad_probs, axis=-1, keepdims=True))
                ).astype(BF)
                sides.append((
                    dot(grad_scores, key) * 0.125,
                    dot_tn(grad_scores, query) * 0.125,
                    dot_tn(probs.astype(BF), grad),
                ))
            grads = [jnp.where(left, *pair).astype(BF) for pair in zip(*sides)]
            start = lanes.start
            for number, found in enumerate(grads):
                if number < 2:
                    found = turn_pairs(found.astype(F32), tables, -1.0).astype(BF)
                grad_projected[rows, pl.ds(pl.multiple_of(start + number * part, 128), 128)] = found

        pairs_of(seq, length, part, body)
        yield [], 9 if seq < seqs - 1 else 1, None


def enter_kernel(
    zhs, tokens, small, qkv, out, gate, up,
    tokens_all, small_all, qkv_all, out_all, gate_cut, up_cut, shard, cuts, send, recv, local,
):
    me, lines = Place(zhs), Lines(send, recv, local)
    loads = [lines.copy(gate, shard.at[0]), lines.copy(up, shard.at[1])]
    me.greet()
    block = qkv_all.shape[6] // 3 // zhs

    def cut_work():
        width = cuts.shape[3]
        kept = []
        for number, target in enumerate((gate_cut, up_cut)):
            yield loads if number == 0 else [], 2, None
            for s in range(2):
                at = 2 * s * width
                left = shard[number, :, at : at + width].astype(F32)
                right = shard[number, :, at + width : at + 2 * width].astype(F32)
                for zl, found in enumerate(swap_halves(left, right)):
                    cuts[number, s * 2 + zl] = found.astype(BF)
            kept.append(lines.copy(cuts.at[number], target))
        yield kept, 0, None

    run(lines, [
        *[("small", gather_columns(lines, me, ready_cut(small), small_all, (other, 0, 128))) for other in (False, True)],
        *[
            (f"qkv{at}", gather_columns(lines, me, block_cut(zhs, qkv, block), qkv_all, piece))
            for at, piece in enumerate(column_pieces(qkv_all.shape[6], QKV_GATHERS))
        ],
        *[
            (f"out{at}", gather_rows(lines, me, out, out_all, *piece))
            for at, piece in enumerate(row_pieces(out.shape[0], OUT_PARTS))
        ],
        ("tokens", gather_team(lines, me, tokens, tokens_all)),
        ("cut", cut_work()),
    ], ENTER_PLAN)
    lines.finish()


def middle_kernel(
    zhs, tokens, upstream, tokens_all, qkv_all, out_all, gate_cut, up_cut, down,
    first_gain, first_bias, offset, gain, bias, tables,
    middle, first_out, queries_out, keys_out, values_out, mixed_out,
    upstream_all, input_all, gate_all, up_all, down_all,
    whole, first, weight, out_weight, queries, keys, values, mixed, partial,
    own, passed, taken, second, send, recv, local,
):
    me, lines = Place(zhs), Lines(send, recv, local)
    loads = [lines.copy(tokens_all, whole), lines.copy(qkv_all, weight), lines.copy(out_all, out_weight)]
    me.greet()

    def tokens_work():
        yield loads[:1], 4, None

        def normed(rows):
            first[rows] = (norm_rows(whole[rows].astype(F32))[0] * first_gain[...] + first_bias[...]).astype(BF)

        by_rows(whole.shape[0], normed)
        yield loads[1:], 2.5, None
        yield from forward_attention(first, weight, offset, tables, queries, keys, values, mixed)
        for start in range(0, partial.shape[3], 512):
            block = dot(mixed[...], out_weight[:, start : start + 512])
            partial[:, :, :, start : start + 512] = block.astype(BF).reshape(partial.shape[:3] + (512,))
        yield from sum_team(lines, me, partial, own, passed, taken)

        def body(rows):
            values = tokens[rows].astype(F32) + team_total(own, taken, rows)
            middle[rows] = values
            second[rows] = (norm_rows(values)[0] * gain[...] + bias[...]).astype(BF)

        by_rows(middle.shape[0], body)
        kept = [
            lines.copy(source, target)
            for source, target in (
                (first, first_out), (queries, queries_out), (keys, keys_out), (values, values_out), (mixed, mixed_out),
            )
        ]
        yield from gather_team(lines, me, second, input_all)
        yield kept, 0, None

    rows = [gather_rows(lines, me, down, down_all, *piece) for piece in row_pieces(down.shape[0], DOWN_PARTS)]
    columns = [
        gather_columns(lines, me, ready_cut(cut), found, piece)
        for piece in column_pieces(gate_cut.shape[2], FF_PARTS)
        for cut, found in ((gate_cut, gate_all), (up_cut, up_all))
    ]
    run(lines, [
        ("tokens", tokens_work()),
        *[(f"ff{at}", work) for at, work in enumerate(columns)],
        *[(f"down{at}", work) for at, work in enumerate(rows)],
        ("upstream", gather_team(lines, me, upstream, upstream_all)),
    ], MIDDLE_PLAN)
    lines.finish()


def feed_kernel(
    zhs, input_all, upstream_all, gate_all, up_all, down_all,
    partial_down_out, partial_second_out, grad_gate_out, grad_up_out, down_part,
    second, upstream, gate_weight, up_weight, down_weight, gate, up, hidden, grad_gate, grad_up,
    partial_down, partial_second, grad_down, buffers, send, recv, local,
):
    me, lines = Place(zhs), Lines(send, recv, local)
    loads = [
        lines.copy(source, target)
        for source, target in (
            (input_all, second), (gate_all, gate_weight), (up_all, up_weight),
            (upstream_all, upstream), (down_all, down_weight),
        )
    ]
    me.greet()
    spawned, pieces = [], row_pieces(grad_down.shape[3], DOWN_PARTS)
    width, ff = gate_weight.shape
    tiles = [(start, min(256, ff - start)) for start in range(0, ff, 256)]

    def sums(piece, near):
        yield from sum_near(lines, me, grad_down, near, piece)
        rows = pl.ds(*piece)
        wait = lines.copy(grad_down.at[:, me.y, me.c, rows], down_part.at[:, rows])
        yield [wait], 0, None

    def work():
        yield loads[:3], 9, None
        for start, size in tiles:
            at = slice(start, start + size)
            gate_rows = dot(second[...], gate_weight[:, at])
            up_rows = dot(second[...], up_weight[:, at])
            gate[:, at], up[:, at] = gate_rows, up_rows
            hidden[:, at] = (gate_rows * jax.nn.sigmoid(gate_rows) * up_rows).astype(BF)
        yield loads[3:], 4.5, None
        for start in range(0, width, 512):
            block = dot_tn(hidden[...], upstream[:, start : start + 512]).astype(BF)
            grad_down[:, :, :, :, start : start + 512] = block.reshape(grad_down.shape[:4] + (512,))
        spawned.extend((f"down{at}", sums(piece, near)) for at, (piece, near) in enumerate(zip(pieces, buffers)))
        yield [], 5, None
        for start, size in tiles:
            at = slice(start, start + size)
            grad_hidden = dot_nt(upstream[...], down_weight[at])
            gate_rows = gate[:, at]
            sigmoid_gate = jax.nn.sigmoid(gate_rows)
            grad_gate[:, at] = (
                grad_hidden * up[:, at] * sigmoid_gate * (1.0 + gate_rows * (1.0 - sigmoid_gate))
            ).astype(BF)
            grad_up[:, at] = (grad_hidden * gate_rows * sigmoid_gate).astype(BF)
        waits = [lines.copy(grad_gate, grad_gate_out), lines.copy(grad_up, grad_up_out)]
        for start in range(0, width, 512):
            yield [], 2.5, None
            block = dot_nt(grad_gate[...], gate_weight[start : start + 512]) + dot_nt(
                grad_up[...], up_weight[start : start + 512]
            )
            partial_second[:, start : start + 512] = block.astype(BF)
        waits.append(lines.copy(partial_second, partial_second_out))
        for start in range(0, width, 1024):
            yield [], 2.5, None
            block = dot(hidden[...], down_weight[:, start : start + 1024])
            partial_down[:, start : start + 1024] = block.astype(BF)
        waits.append(lines.copy(partial_down, partial_down_out))
        yield waits, 0, None

    run(lines, [("work", work()), spawned], FEED_PLAN)
    lines.finish()


def back_kernel(
    zhs, middle, upstream, gain, partial_down, partial_second, down_part, input_all, gate_in, up_in,
    out_all, queries_in, keys_in, values_in, mixed_in, tables,
    result, grad_middle, sums, down_total, gate_total, up_total, out_total, projected_out, bias_sums,
    own_down, passed_down, taken_down, own_second, passed_second, taken_second, attended,
    attended_all, out_weight, queries, keys, values, mixed, grad_mixed, grad_projected, grad_out,
    second, grad_side, grad_gate, grad_up, cuts, joined, down_buffers, out_buffers, buffers, send, recv, local,
):
    me, lines = Place(zhs), Lines(send, recv, local)
    near_loads = [lines.copy(input_all, second), lines.copy(gate_in, grad_side)]
    loads = [
        lines.copy(source, target)
        for source, target in (
            (out_all, out_weight), (queries_in, queries), (keys_in, keys), (values_in, values), (mixed_in, mixed),
        )
    ]
    me.greet()
    spawned = []
    pieces = column_pieces(cuts.shape[3], FF_PARTS)

    def weights_work():
        number = 0
        for which, (grad, total) in enumerate(((grad_gate, gate_total), (grad_up, up_total))):
            yield near_loads if grad is grad_gate else [lines.copy(up_in, grad_side)], 4.5, None
            ff = grad_side.shape[1]
            for start in range(0, ff, 256):
                size = min(256, ff - start)
                block = dot_tn(second[...], grad_side[:, start : start + size]).astype(BF)
                grad[:, :, :, :, :, :, start : start + size] = block.reshape(grad.shape[:6] + (size,))
            left = list(pieces)
            for piece in pieces:
                work = piece_work(grad, which, total, buffers[number], piece, left)
                spawned.append((f"ff{number}", work))
                number += 1

    def piece_work(grad, which, total, found, piece, left):
        yield from sum_columns(lines, me, grad, cuts.at[which], found, piece)
        left.remove(piece)
        if not left:
            spawned.append(("join", join_work(which, total)))

    def join_work(which, total):
        yield [], 2, None
        width, kept = cuts.shape[3], []
        for s in range(2):
            sides = [cuts[which, s * 2 + zl].astype(F32) for zl in range(2)]
            for zh, found in enumerate(swap_halves(*sides)):
                joined[which, s * 2 + zh] = found
                at = (s * 2 + zh) * width
                kept.append(lines.copy(joined.at[which, s * 2 + zh], total.at[:, at : at + width]))
        yield kept, 0, None

    def tokens_work():
        yield [], 0, None
        yield from sum_team(lines, me, partial_second, own_second, passed_second, taken_second)
        sums[...] = jnp.zeros_like(sums)

        def body(rows):
            normed, scale_rows = norm_rows(middle[rows])
            grad = team_total(own_second, taken_second, rows)
            sums[0:1] += jnp.sum(grad * normed, axis=0, keepdims=True)
            sums[1:2] += jnp.sum(grad, axis=0, keepdims=True)
            grad = upstream[rows].astype(F32) + norm_back(grad * gain[...], normed, scale_rows)
            grad_middle[rows] = grad
            attended[rows] = grad.astype(BF)

        by_rows(middle.shape[0], body)
        yield from gather_team(lines, me, attended, attended_all)
        yield loads, 4, None
        count, width = mixed.shape[0], attended_all.shape[3]
        for start in range(0, width, 512):
            block = dot_tn(mixed[...], attended_all[:, :, :, start : start + 512].reshape(count, 512))
            grad_out[:, :, :, :, start : start + 512] = block.astype(BF).reshape(grad_out.shape[:4] + (512,))
        for at, piece in enumerate(row_pieces(out_total.shape[0], OUT_PARTS)):
            spawned.append((f"out{at}", sum_rows(lines, me, grad_out, out_total, *out_buffers[at], piece)))
        grad_mixed[...] = dot_nt(attended_all[...].reshape(count, width), out_weight[...]).astype(BF)
        yield [], 9, None
        yield from backward_attention(grad_mixed, tables, queries, keys, values, grad_projected)
        wait = lines.copy(grad_projected, projected_out)
        for start in range(0, grad_projected.shape[1], 256):
            block = jnp.sum(grad_projected[:, start : start + 256].astype(F32), axis=0, keepdims=True)
            bias_sums[:, start : start + 256] = block
        yield [wait], 0, None

    def result_work():
        yield [], 0, "s"
        yield from sum_team(lines, me, partial_down, own_down, passed_down, taken_down)

        def body(rows):
            result[rows] = (middle[rows] + team_total(own_down, taken_down, rows)).astype(BF)

        by_rows(middle.shape[0], body)

    far = [
        sum_far(lines, me, down_part, down_total, found, piece)
        for found, piece in zip(down_buffers, row_pieces(down_total.shape[0], DOWN_PARTS))
    ]
    run(lines, [
        ("tokens", tokens_work()),
        ("weights", weights_work()),
        *[(f"down{at}", work) for at, work in enumerate(far)],
        ("result", result_work()),
        spawned,
    ], BACK_PLAN)
    lines.finish()


def leave_kernel(
    zhs, tokens, grad_middle, gain, second_sums, bias_sums, grad_projected, first_in, qkv_in,
    grad_inputs, sums, qkv_total,
    first, weight, partial, grad_qkv, cut, own, passed, taken, steps, buffers, send, recv, local,
):
    me, lines = Place(zhs), Lines(send, recv, local)
    loads = [lines.copy(first_in, first), lines.copy(qkv_in, weight)]
    me.greet()

    spawned = []
    pieces = column_pieces(cut.shape[2], QKV_PARTS)
    left = list(pieces)

    def piece_work(at):
        yield from sum_columns(lines, me, grad_qkv, cut, buffers[at], pieces[at])
        left.remove(pieces[at])
        if not left:
            block = cut.shape[2] // 3 // zhs
            for s in range(2):
                for zl in range(2):
                    for start in range(0, cut.shape[2], block):
                        number, zh = start // (zhs * block), start // block % zhs
                        column = (number * 4 * zhs + (s * zhs + zh) * 2 + zl) * block
                        found = cut[s * 2 + zl, :, start : start + block]
                        qkv_total[:, column : column + block] = found.astype(F32)

    def tokens_work():
        yield loads, 3, None
        columns = grad_qkv.shape[6]
        for number in range(QKV_PARTS):
            _, start, size = pieces[number]
            for at in range(start, start + size, 256):
                block = dot_tn(first[...], grad_projected[:, at : at + 256]).astype(BF)
                grad_qkv[:, :, :, :, :, :, at : at + 256] = block.reshape(grad_qkv.shape[:6] + (256,))
            for at in (number, number + QKV_PARTS):
                spawned.append((f"qkv{at}", piece_work(at)))
            yield [], 3 if number < QKV_PARTS - 1 else 7, None
        for at in range(weight.shape[0] // 256):
            block = dot_nt(grad_projected[...], weight[at * 256 : at * 256 + 256])
            partial[:, :, :, at * 256 : at * 256 + 256] = block.astype(BF).reshape(partial.shape[:3] + (256,))
        yield from sum_team(lines, me, partial, own, passed, taken)
        steps[0] = jnp.zeros_like(steps[0])
        steps[0, 2:4] = second_sums[0:2]
        part = bias_sums.shape[1] // 3
        block = part // zhs
        for number in range(3):
            for zh in range(zhs):
                at = ((me.s * zhs + zh) * 2 + me.zl) * block
                steps[0, 4 + number : 5 + number, pl.ds(pl.multiple_of(at, 64), block)] = bias_sums[
                    :, number * part + zh * block : number * part + (zh + 1) * block
                ]

        def body(rows):
            normed, scale_rows = norm_rows(tokens[rows].astype(F32))
            grad = team_total(own, taken, rows)
            steps[0, 0:1] += jnp.sum(grad * normed, axis=0, keepdims=True)
            steps[0, 1:2] += jnp.sum(grad, axis=0, keepdims=True)
            grad_inputs[rows] = grad_middle[rows] + norm_back(grad * gain[...], normed, scale_rows)

        by_rows(tokens.shape[0], body)
        groups = [
            [me.at(s=1 - me.s)], [me.at(zl=1 - me.zl)], [me.at(c=1 - me.c)], [me.at(y=1 - me.y)],
            [me.at(zh=zh) for zh in me.highs()],
        ]
        at = 0
        for group, link in zip(groups, ("s", "zl", "c", "y", "zh")):
            arrived = [
                lines.push(steps.at[at], steps.at[at + 1 + number], device, link)
                for number, device in enumerate(group)
            ]
            yield arrived, 0.3, None
            total = steps[at]
            for number in range(len(group)):
                total = total + steps[at + 1 + number]
            at += len(group) + 1
            steps[at] = total
        sums[...] = steps[at]

    run(lines, [("tokens", tokens_work()), spawned], LEAVE_PLAN)
    lines.finish()


def near_buffers(zhs, size, width):
    return tuple(pltpu.VMEM(shape + (size, width), BF) for shape in ((zhs, 2), (zhs,)))


def far_buffers(zhs, size, width):
    return (
        pltpu.VMEM((size, width), BF), pltpu.VMEM((zhs - 1, size, width), BF), pltpu.VMEM((size, width), F32)
    )


def column_buffers(zhs, own, columns):
    return tuple(
        pltpu.VMEM(shape + (own, columns), BF) for shape in ((zhs, 2, 2), (zhs, 2), (zhs - 1, 2))
    )


IN_HBM = pl.BlockSpec(memory_space=pl.ANY)
IN_VMEM = pl.BlockSpec(memory_space=pltpu.VMEM)


def call(kernel, zhs, number, inputs, outputs, scratch, copies, locals_, limit):
    return pl.pallas_call(
        lambda *refs: kernel(zhs, *refs),
        out_shape=[jax.ShapeDtypeStruct(shape, kind) for shape, kind, _ in outputs],
        in_specs=[spec for _, spec in inputs],
        out_specs=[spec for _, _, spec in outputs],
        scratch_shapes=[
            *scratch,
            pltpu.SemaphoreType.DMA((copies,)),
            pltpu.SemaphoreType.DMA((copies,)),
            pltpu.SemaphoreType.DMA((locals_,)),
        ],
        compiler_params=pltpu.CompilerParams(
            collective_id=number, has_side_effects=True, vmem_limit_bytes=limit << 20
        ),
    )(*[array for array, _ in inputs])


def per_device(
    tokens, cotangent, norm1_gain, norm1_bias, qkv_weight, qkv_bias, out_weight,
    norm2_gain, norm2_bias, gate_weight, up_weight, down_weight,
):
    zh = lax.axis_size("zh")
    rows = tokens.shape[1]
    width = tokens.shape[2]
    own = qkv_weight.shape[0]
    ff = gate_weight.shape[1]
    ff_own = down_weight.shape[0]
    half = lax.axis_size("seq")
    length = rows * half
    seqs = lax.axis_size("zl")
    team = half * seqs
    part = width // team
    ff_part = ff // team
    devices = width // own
    tokens, cotangent = tokens[0], cotangent[0]
    index = (lax.axis_index("seq") * (devices // half)
             + ((lax.axis_index("zh") * 2 + lax.axis_index("zl")) * 2 + lax.axis_index("y")) * 2
             + lax.axis_index("c"))

    def mine_columns(whole, parts):
        block = whole.shape[0] // parts // (half * zh * seqs)
        cut = whole.reshape(parts, half, zh, seqs, block)
        cut = lax.dynamic_index_in_dim(cut, lax.axis_index("seq"), 1, keepdims=False)
        cut = lax.dynamic_index_in_dim(cut, lax.axis_index("zl"), 2, keepdims=False)
        return cut.reshape(-1)

    small = jnp.concatenate([norm1_gain, norm1_bias, norm2_gain, norm2_bias, qkv_bias]).astype(F32)
    small = jnp.pad(small, (0, 1024 - small.shape[0])).reshape(8, 128)
    small = jnp.broadcast_to(small, (team, 8, 128))
    token_shape = (seqs, half, rows, width)
    owners = (half, zh, seqs, 2, 2)
    count = team * rows
    limit = 60
    tables = rotary_tables(length)
    tokens_all, small_all, qkv_all, out_all, gate_cut, up_cut = call(
        enter_kernel, zh, 0,
        [
            (tokens, IN_HBM), (small, IN_HBM), (qkv_weight, IN_HBM), (out_weight, IN_HBM),
            (gate_weight, IN_HBM), (up_weight, IN_HBM),
        ],
        [
            (token_shape, BF, IN_HBM),
            (owners + (8, 128), F32, IN_HBM),
            (owners + (own, 3 * part), BF, IN_HBM),
            ((zh, 2, 2, own, width), BF, IN_HBM),
            ((team, own, ff_part), BF, IN_HBM),
            ((team, own, ff_part), BF, IN_HBM),
        ],
        [pltpu.VMEM((2, own, ff), BF), pltpu.VMEM((2, team, own, ff_part), BF)],
        3 + (2 + OUT_PARTS) * (zh + 4) + 2 * QKV_GATHERS * (3 * zh + 2), 32, 60,
    )
    small = small_all.reshape(devices, 1024)
    first_gain = small[:, :own].reshape(1, width)
    first_bias = small[:, own : 2 * own].reshape(1, width)
    second_gain = small[:, 2 * own : 3 * own].reshape(1, width)
    second_bias = small[:, 3 * own : 4 * own].reshape(1, width)
    qkv_offset = mine_columns(small[:, 4 * own : 7 * own].reshape(-1), 3).reshape(1, 3 * part)
    qkv_matrix = qkv_all.reshape(width, 3 * part)
    out_matrix = out_all.reshape(part, width)

    token_scratch = [
        pltpu.VMEM((rows, width), BF), pltpu.VMEM((rows, width), BF), pltpu.VMEM((3, rows, width), BF)
    ]
    head_shape = (count, part)
    heads = [(head_shape, BF, IN_HBM)] * 4
    head_scratch = [pltpu.VMEM(head_shape, BF)] * 4
    (
        middle, first_input, queries, keys, values, mixed, upstream_all, input_all, gate_all, up_all, down_all,
    ) = call(
        middle_kernel, zh, 1,
        [
            (tokens, IN_VMEM), (cotangent, IN_HBM), (tokens_all.reshape(count, width), IN_HBM),
            (qkv_matrix, IN_HBM), (out_matrix, IN_HBM),
            (gate_cut, IN_HBM), (up_cut, IN_HBM), (down_weight, IN_HBM),
            (first_gain, IN_VMEM), (first_bias, IN_VMEM), (qkv_offset, IN_VMEM),
            (second_gain, IN_VMEM), (second_bias, IN_VMEM), (tables, IN_VMEM),
        ],
        [
            ((rows, width), F32, IN_VMEM),
            ((count, width), BF, IN_HBM),
            *heads,
            (token_shape, BF, IN_HBM),
            (token_shape, BF, IN_HBM),
            (owners + (own, ff_part), BF, IN_HBM),
            (owners + (own, ff_part), BF, IN_HBM),
            ((zh, 2, 2, ff_own, width), BF, IN_HBM),
        ],
        [
            pltpu.VMEM((count, width), BF), pltpu.VMEM((count, width), BF),
            pltpu.VMEM((width, 3 * part), BF), pltpu.VMEM((part, width), BF),
            *head_scratch, pltpu.VMEM(token_shape, BF),
            *token_scratch, pltpu.VMEM((rows, width), BF),
        ],
        9 + (DOWN_PARTS + 4 * FF_PARTS) * (zh + 4), 40, limit,
    )
    second_input = input_all.reshape(count, width)
    ff_shape = (count, ff_part)
    down_pieces = [size for _, size in row_pieces(ff_own, DOWN_PARTS)]
    partial_down, partial_second, grad_gate, grad_up, down_part = call(
        feed_kernel, zh, 4,
        [
            (second_input, IN_HBM), (upstream_all.reshape(count, width), IN_HBM),
            (gate_all.reshape(width, ff_part), IN_HBM), (up_all.reshape(width, ff_part), IN_HBM),
            (down_all.reshape(ff_part, width), IN_HBM),
        ],
        [
            ((count, width), BF, IN_HBM),
            ((count, width), BF, IN_HBM),
            (ff_shape, BF, IN_HBM),
            (ff_shape, BF, IN_HBM),
            ((zh, ff_own, width), BF, IN_HBM),
        ],
        [
            pltpu.VMEM((count, width), BF), pltpu.VMEM((count, width), BF),
            pltpu.VMEM((width, ff_part), BF), pltpu.VMEM((width, ff_part), BF), pltpu.VMEM((ff_part, width), BF),
            pltpu.VMEM(ff_shape, F32), pltpu.VMEM(ff_shape, F32),
            *[pltpu.VMEM(ff_shape, BF)] * 3,
            pltpu.VMEM((count, width), BF), pltpu.VMEM((count, width), BF), pltpu.VMEM(down_all.shape, BF),
            [near_buffers(zh, size, width) for size in down_pieces],
        ],
        DOWN_PARTS * 2, 32, 60,
    )
    result, grad_middle, second_sums, down_total, gate_total, up_total, out_total, grad_projected, bias_sums = call(
        back_kernel, zh, 2,
        [
            (middle, IN_VMEM), (cotangent, IN_VMEM), (second_gain, IN_VMEM),
            (partial_down.reshape(token_shape), IN_HBM), (partial_second.reshape(token_shape), IN_HBM),
            (down_part, IN_HBM), (second_input, IN_HBM), (grad_gate, IN_HBM), (grad_up, IN_HBM),
            (out_matrix, IN_HBM), (queries, IN_HBM), (keys, IN_HBM), (values, IN_HBM), (mixed, IN_HBM),
            (tables, IN_VMEM),
        ],
        [
            ((rows, width), BF, IN_VMEM),
            ((rows, width), F32, IN_VMEM),
            ((8, width), F32, IN_VMEM),
            ((ff_own, width), F32, IN_HBM),
            ((own, ff), F32, IN_HBM),
            ((own, ff), F32, IN_HBM),
            ((own, width), F32, IN_HBM),
            ((count, 3 * part), BF, IN_HBM),
            ((1, 3 * part), F32, IN_VMEM),
        ],
        [
            *token_scratch, *token_scratch, pltpu.VMEM((rows, width), BF), pltpu.VMEM(token_shape, BF),
            pltpu.VMEM((part, width), BF), *head_scratch, pltpu.VMEM(head_shape, BF),
            pltpu.VMEM((count, 3 * part), BF), pltpu.VMEM(out_all.shape, BF),
            pltpu.VMEM((count, width), BF), pltpu.VMEM(ff_shape, BF),
            pltpu.VMEM(gate_all.shape, BF), pltpu.VMEM(gate_all.shape, BF),
            pltpu.VMEM((2, team, own, ff_part), BF), pltpu.VMEM((2, team, own, ff_part), F32),
            [far_buffers(zh, size, width) for size in down_pieces],
            [
                (near_buffers(zh, size, width), far_buffers(zh, size, width))
                for _, size in row_pieces(own, OUT_PARTS)
            ],
            [
                column_buffers(zh, own, size)
                for _ in range(2)
                for _, _, size in column_pieces(ff_part, FF_PARTS)
            ],
        ],
        9 + (OUT_PARTS + DOWN_PARTS + 4 * FF_PARTS) * (zh + 4), 60, 62,
    )
    grad_inputs, sums, qkv_total = call(
        leave_kernel, zh, 3,
        [
            (tokens, IN_VMEM), (grad_middle, IN_VMEM), (first_gain, IN_VMEM),
            (second_sums, IN_VMEM), (bias_sums, IN_VMEM), (grad_projected, IN_VMEM),
            (first_input, IN_HBM), (qkv_matrix, IN_HBM),
        ],
        [
            ((rows, width), F32, IN_VMEM),
            ((8, width), F32, IN_VMEM),
            ((own, 3 * width), F32, IN_VMEM),
        ],
        [
            pltpu.VMEM((count, width), BF), pltpu.VMEM((width, 3 * part), BF), pltpu.VMEM(token_shape, BF),
            pltpu.VMEM(qkv_all.shape, BF), pltpu.VMEM((team, own, 3 * part), BF),
            *token_scratch, pltpu.VMEM((zh + 9, 8, width), F32),
            [column_buffers(zh, own, size) for _, _, size in column_pieces(3 * part, QKV_PARTS)],
        ],
        zh + 6 + (2 * QKV_PARTS) * (zh + 4), 24, limit,
    )

    def mine(vector_row, size):
        return lax.dynamic_slice_in_dim(vector_row, index * size, size, 0)

    return (
        result[None],
        grad_inputs[None],
        mine(sums[0], own),
        mine(sums[1], own),
        qkv_total,
        mine(sums[4:7].reshape(-1), 3 * own),
        out_total,
        mine(sums[2], own),
        mine(sums[3], own),
        gate_total,
        up_total,
        down_total,
    )


def solution(mesh):
    half, shards = mesh.shape["seq"], mesh.shape["shard"]
    fine = jax.sharding.Mesh(mesh.devices.reshape(half, shards // 8, 2, 2, 2), ALL)
    token = P(("zh", "zl", "y", "c"), "seq", None)
    row = P(ALL)

    def program(*arguments):
        whole_tiles = shards == 16 and arguments[-1].shape[0] // (half * shards) % ROWS == 0
        return jax.shard_map(
            per_device if whole_tiles else plain_device,
            mesh=fine,
            in_specs=(token, token) + (row,) * 10,
            out_specs=(token, token) + (row,) * 10,
            check_vma=False,
        )(*arguments)

    return program
```

```python
import jax
import jax.numpy as jnp
import numpy as np
from jax import lax
from jax.experimental import pallas as pl
from jax.experimental.pallas import tpu as pltpu
from jax.sharding import PartitionSpec as P

HEADS = 32
HEAD_DIM = 64
ROTARY = 16
TEAM = ("seq", "zl")
PEERS = ("zh", "y", "c")
ALL = ("seq", "zh", "zl", "y", "c")
BF = jnp.bfloat16
F32 = jnp.float32


def norm_rows(values):
    centre = jnp.mean(values, axis=-1, keepdims=True)
    centred = values - centre
    spread = jnp.mean(centred * centred, axis=-1, keepdims=True)
    scale_rows = lax.rsqrt(spread + 1e-05)
    return (centred * scale_rows, scale_rows)


def norm_back(grad_normed, normed, scale_rows):
    return scale_rows * (
        grad_normed
        - jnp.mean(grad_normed, axis=-1, keepdims=True)
        - normed * jnp.mean(grad_normed * normed, axis=-1, keepdims=True)
    )


def rotate(values, positions, direction):
    halves = ROTARY // 2
    frequency = 10000.0 ** (-2.0 * jnp.arange(halves, dtype=F32) / ROTARY)
    angles = positions.astype(F32)[:, None] * frequency[None, :]
    cosine_table = jnp.cos(angles)[:, None, :]
    sine_table = jnp.sin(angles)[:, None, :] * direction
    first_half = values[..., :halves]
    second_half = values[..., halves:ROTARY]
    return jnp.concatenate(
        [
            first_half * cosine_table - second_half * sine_table,
            second_half * cosine_table + first_half * sine_table,
            values[..., ROTARY:],
        ],
        axis=-1,
    )


def dot(left, right):
    return jnp.dot(left, right, preferred_element_type=F32)


def dot_nt(left, right):
    return lax.dot_general(left, right, (((1,), (1,)), ((), ())), preferred_element_type=F32)


def dot_tn(left, right):
    return lax.dot_general(left, right, (((0,), (0,)), ((), ())), preferred_element_type=F32)


def plain_device(
    tokens, cotangent, norm1_gain, norm1_bias, qkv_weight, qkv_bias, out_weight,
    norm2_gain, norm2_bias, gate_weight, up_weight, down_weight,
):
    zh = lax.axis_size("zh")
    rows = tokens.shape[1]
    width = tokens.shape[2]
    own = qkv_weight.shape[0]
    ff = gate_weight.shape[1]
    half = lax.axis_size("seq")
    length = rows * half
    team = half * lax.axis_size("zl")
    seqs = lax.axis_size("zl")

    def cut_columns(shard, parts):
        block = shard.shape[1] // parts // (half * zh * seqs)
        cut = shard.reshape(own, parts, half, zh, seqs, block).transpose(2, 4, 0, 1, 3, 5)
        return cut.reshape(team, own, parts * zh * block)

    def join_columns(cut, parts):
        block = cut.shape[2] // parts // zh
        cut = cut.reshape(half, seqs, own, parts, zh, block).transpose(2, 3, 0, 4, 1, 5)
        return cut.reshape(own, -1)

    def mine_columns(whole, parts):
        block = whole.shape[0] // parts // (half * zh * seqs)
        cut = whole.reshape(parts, half, zh, seqs, block)
        cut = lax.dynamic_index_in_dim(cut, lax.axis_index("seq"), 1, keepdims=False)
        cut = lax.dynamic_index_in_dim(cut, lax.axis_index("zl"), 2, keepdims=False)
        return cut.reshape(-1)

    def to_owner_order(values):
        n = values.shape[0]
        return values.reshape(n, half, zh, seqs, 4, own).transpose(0, 2, 4, 1, 3, 5).reshape(n, width)

    def from_owner_order(values):
        n = values.shape[0]
        return values.reshape(n, zh, 4, half, seqs, own).transpose(0, 3, 1, 4, 2, 5).reshape(n, width)

    def gather_columns(shard, parts):
        cut = cut_columns(shard, parts)
        cut = lax.all_to_all(cut, TEAM, split_axis=0, concat_axis=0, tiled=True)
        return lax.all_gather(cut.reshape(team * own, -1), PEERS, axis=0, tiled=True)

    def gather_rows(shard):
        return lax.all_gather(shard, PEERS, axis=0, tiled=True)

    def gather_tokens(values):
        return lax.all_gather(values, ("zl", "seq"), axis=0, tiled=True)

    def sum_tokens(values):
        return lax.psum_scatter(values.astype(BF), ("zl", "seq"), scatter_dimension=0, tiled=True).astype(F32)

    def sum_rows(values):
        return lax.psum_scatter(values.astype(BF), PEERS, scatter_dimension=0, tiled=True)

    def sum_columns(values, parts):
        part = sum_rows(values).reshape(team, own, -1)
        part = lax.all_to_all(part, TEAM, split_axis=0, concat_axis=0, tiled=True)
        return join_columns(part, parts).astype(F32)

    small = jnp.concatenate([norm1_gain, norm1_bias, norm2_gain, norm2_bias, qkv_bias])
    small = lax.all_gather(small, ALL, axis=0, tiled=False)
    first_gain = small[:, :own].reshape(-1).astype(F32)
    first_bias = small[:, own : 2 * own].reshape(-1).astype(F32)
    second_gain = small[:, 2 * own : 3 * own].reshape(-1).astype(F32)
    second_bias = small[:, 3 * own : 4 * own].reshape(-1).astype(F32)
    qkv_offset = mine_columns(small[:, 4 * own :].reshape(-1), 3).astype(F32)

    inputs = tokens[0].astype(F32)
    first_normed, first_scale = norm_rows(inputs)
    first_own = to_owner_order((first_normed * first_gain + first_bias).astype(BF))
    first_input = gather_tokens(first_own)
    qkv_matrix = gather_columns(qkv_weight, 3)
    out_matrix = gather_rows(out_weight)
    gate_matrix = gather_columns(gate_weight, 1)
    up_matrix = gather_columns(up_weight, 1)
    down_matrix = gather_rows(down_weight)
    upstream = gather_tokens(cotangent[0])

    projected = dot(first_input, qkv_matrix) + qkv_offset
    part = width // team
    group_heads = part // HEAD_DIM
    positions = jnp.tile(jnp.arange(length, dtype=jnp.int32), seqs)

    def heads_of(values):
        return values.reshape(seqs, length, group_heads, HEAD_DIM).transpose(0, 2, 1, 3)

    def unheads(values):
        return values.transpose(0, 2, 1, 3).reshape(seqs * length, part)

    queries = heads_of(rotate(projected[:, :part].reshape(-1, group_heads, HEAD_DIM), positions, 1.0).astype(BF))
    keys = heads_of(rotate(projected[:, part : 2 * part].reshape(-1, group_heads, HEAD_DIM), positions, 1.0).astype(BF))
    values = heads_of(projected[:, 2 * part :].astype(BF))
    causal = jnp.arange(length)[:, None] >= jnp.arange(length)[None, :]
    scores = jnp.einsum("shqd,shkd->shqk", queries, keys, preferred_element_type=F32) * 0.125
    scores = jnp.where(causal, scores, -1e30)
    highest = jnp.max(scores, axis=-1, keepdims=True)
    exponent = jnp.exp(scores - highest)
    probs = exponent / jnp.sum(exponent, axis=-1, keepdims=True)
    probs_low = probs.astype(BF)
    mixed = unheads(jnp.einsum("shqk,shkd->shqd", probs_low, values, preferred_element_type=F32).astype(BF))
    middle = inputs + sum_tokens(dot(mixed, out_matrix))

    second_normed, second_scale = norm_rows(middle)
    second_own = to_owner_order((second_normed * second_gain + second_bias).astype(BF))
    second_input = gather_tokens(second_own)
    gate_rows = dot(second_input, gate_matrix)
    up_rows = dot(second_input, up_matrix)
    sigmoid_gate = jax.nn.sigmoid(gate_rows)
    silu_gate = gate_rows * sigmoid_gate
    hidden = (silu_gate * up_rows).astype(BF)
    result = middle + sum_tokens(dot(hidden, down_matrix))

    down_total = sum_rows(dot_tn(hidden, upstream)).astype(F32)
    grad_hidden = dot_nt(upstream, down_matrix)
    grad_gate = (grad_hidden * up_rows * sigmoid_gate * (1.0 + gate_rows * (1.0 - sigmoid_gate))).astype(BF)
    grad_up = (grad_hidden * silu_gate).astype(BF)
    gate_total = sum_columns(dot_tn(second_input, grad_gate), 1)
    up_total = sum_columns(dot_tn(second_input, grad_up), 1)
    grad_second = from_owner_order(sum_tokens(dot_nt(grad_gate, gate_matrix) + dot_nt(grad_up, up_matrix)))
    grad_middle = cotangent[0].astype(F32) + norm_back(grad_second * second_gain, second_normed, second_scale)
    grad_attended = gather_tokens(grad_middle.astype(BF))
    out_total = sum_rows(dot_tn(mixed, grad_attended)).astype(F32)
    grad_mixed = heads_of(dot_nt(grad_attended, out_matrix).astype(BF))
    grad_probs = jnp.einsum("shqd,shkd->shqk", grad_mixed, values, preferred_element_type=F32)
    grad_scores = (probs * (grad_probs - jnp.sum(probs * grad_probs, axis=-1, keepdims=True))).astype(BF)
    grad_queries = (jnp.einsum("shqk,shkd->shqd", grad_scores, keys, preferred_element_type=F32) * 0.125).astype(BF)
    grad_keys = (jnp.einsum("shqk,shqd->shkd", grad_scores, queries, preferred_element_type=F32) * 0.125).astype(BF)
    grad_values = jnp.einsum("shqk,shqd->shkd", probs_low, grad_mixed, preferred_element_type=F32).astype(BF)
    grad_queries = rotate(unheads(grad_queries).astype(F32).reshape(-1, group_heads, HEAD_DIM), positions, -1.0)
    grad_keys = rotate(unheads(grad_keys).astype(F32).reshape(-1, group_heads, HEAD_DIM), positions, -1.0)
    grad_projected = jnp.concatenate(
        [grad_queries.reshape(-1, part).astype(BF), grad_keys.reshape(-1, part).astype(BF), unheads(grad_values)],
        axis=1,
    )
    qkv_total = sum_columns(dot_tn(first_input, grad_projected), 3)
    grad_first = from_owner_order(sum_tokens(dot_nt(grad_projected, qkv_matrix)))
    grad_inputs = grad_middle + norm_back(grad_first * first_gain, first_normed, first_scale)

    bias_part = jnp.sum(grad_projected.astype(F32), axis=0).reshape(3, zh, -1)
    bias_whole = jnp.zeros((3, half, zh, seqs, bias_part.shape[2]), F32)
    bias_whole = lax.dynamic_update_slice(
        bias_whole, bias_part[:, None, :, None], (0, lax.axis_index("seq"), 0, lax.axis_index("zl"), 0)
    ).reshape(-1)
    count = width // own
    sums = jnp.concatenate(
        [
            jnp.sum(grad_first * first_normed, axis=0).reshape(count, own),
            jnp.sum(grad_first, axis=0).reshape(count, own),
            jnp.sum(grad_second * second_normed, axis=0).reshape(count, own),
            jnp.sum(grad_second, axis=0).reshape(count, own),
            bias_whole.reshape(count, 3 * own),
        ],
        axis=1,
    )
    sums = lax.psum_scatter(sums, ALL, scatter_dimension=0, tiled=True)[0]
    return (
        result.astype(BF)[None],
        grad_inputs[None],
        sums[:own],
        sums[own : 2 * own],
        qkv_total,
        sums[4 * own :],
        out_total,
        sums[2 * own : 3 * own],
        sums[3 * own : 4 * own],
        gate_total,
        up_total,
        down_total,
    )


MESH = pl.DeviceIdType.MESH
ROWS = 16
QKV_PARTS, QKV_GATHERS, OUT_PARTS, FF_PARTS, DOWN_PARTS = 2, 3, 2, 2, 4


class Place:
    def __init__(self, zhs):
        self.s, self.zh, self.zl, self.y, self.c = (lax.axis_index(axis) for axis in ALL)
        self.zhs = zhs

    def at(self, **changed):
        return tuple(changed.get(name, getattr(self, name)) for name in ("s", "zh", "zl", "y", "c"))

    def mates(self):
        for flip_s, flip_z in ((0, 1), (1, 0), (1, 1)):
            yield (1 - self.s if flip_s else self.s), (1 - self.zl if flip_z else self.zl)

    def highs(self):
        for step in range(1, self.zhs):
            yield (self.zh + step) % self.zhs

    def greet(self, corners=False):
        partners = [self.at(s=s, zl=zl) for s, zl in self.mates()]
        partners += [self.at(zh=zh) for zh in self.highs()]
        partners += [self.at(y=1 - self.y), self.at(c=1 - self.c)]
        if corners:
            partners += [self.at(zh=zh, y=1 - self.y) for zh in self.highs()]
        barrier = pltpu.get_barrier_semaphore()
        for partner in partners:
            pl.semaphore_signal(barrier, inc=1, device_id=partner, device_id_type=MESH)
        pl.semaphore_wait(barrier, len(partners))


class Traffic:
    def __init__(self):
        self.now, self.active = 0.0, []

    def start(self, demands):
        transfer = {"left": {link: time for link, time in demands.items()}, "done": None}
        self.active.append(transfer)
        return transfer

    def backlog(self, link):
        return sum(transfer["left"].get(link, 0.0) for transfer in self.active)

    def advance(self, until):
        while self.now < until:
            shares = {}
            for transfer in self.active:
                for link in transfer["left"]:
                    shares[link] = shares.get(link, 0) + 1
            step = until - self.now
            for transfer in self.active:
                for link, left in transfer["left"].items():
                    step = min(step, left * shares[link])
            self.now += step
            for transfer in list(self.active):
                transfer["left"] = {
                    link: left - step / shares[link]
                    for link, left in transfer["left"].items()
                    if left - step / shares[link] > 1e-6
                }
                if not transfer["left"]:
                    transfer["done"] = self.now + LATENCY
                    self.active.remove(transfer)


LATENCY = 2.0
ENTER_PLAN = {"small": (7.8, 43), "qkv0": (4.9, 33), "qkv1": (10.8, 0), "qkv2": (6.1, 1), "qkv3": (10.6, 19), "qkv4": (3.8, 13), "qkv5": (11.5, 41), "out0": (2.2, 0), "out1": (2.6, 32), "tokens": (5.8, 13), "cut": (2.3, 40), "backlog": 12}
MIDDLE_PLAN = {"tokens": (0, 0), "ff0": (1, 0), "ff1": (3, 0), "ff2": (4, 0), "ff3": (5, 0), "ff4": (6, 0), "ff5": (7, 0), "ff6": (8, 0), "ff7": (9, 0), "down0": (2, 0), "down1": (10, 0), "down2": (11, 0), "down3": (12, 0), "upstream": (13, 8)}
FEED_PLAN = {"work": (4.9, 0), "down0": (5.9, 0), "down1": (1, 0), "down2": (2.3, 35), "down3": (4.1, 43), "result": (1.3, 0)}
BACK_PLAN = {"tokens": (16.9, 0), "weights": (17.1, 0), "down0": (12.9, 0), "down1": (7.6, 0), "down2": (12.3, 11), "down3": (0.2, 34), "ff0": (14.7, 49), "ff1": (12.6, 10), "ff2": (12.3, 29), "ff3": (3.9, 0), "ff4": (16, 0), "ff5": (6, 0), "ff6": (10.6, 61), "ff7": (9.2, 2), "out0": (6.2, 0), "out1": (16.3, 40), "join": (17.7, 21)}
LEAVE_PLAN = {"weights": (4, 0), "tokens": (1.5, 0), "qkv0": (0.8, 24), "qkv2": (0.1, 0), "qkv1": (0.1, 33), "qkv3": (3.9, 19)}
BACKLOG = 12.0
LINK_TIME = {
    "s": {"s": 2 / 92e3},
    "zl": {"zl": 2 / 92e3},
    "y": {"y": 2 / 92e3},
    "zh": {"zh": 4 / 92e3, "zl": 2 / 92e3},
    "c": {"c": 1 / 300e3},
    "diagonal": {"s": 2 / 92e3, "zl": 2 / 92e3},
    "local": {"local": 1 / 1500e3},
}


class Lines:
    def __init__(self, send, recv, local):
        self.send, self.recv, self.local = send, recv, local
        self.sent, self.copied, self.traffic = [], 0, Traffic()

    def track(self, wait, source, link):
        size = int(np.prod(source.shape)) * jnp.dtype(source.dtype).itemsize
        return wait, self.traffic.start({name: time * size for name, time in LINK_TIME[link].items()})

    def push(self, source, target, device, link):
        at = len(self.sent)
        copy = pltpu.make_async_remote_copy(
            src_ref=source, dst_ref=target, send_sem=self.send.at[at], recv_sem=self.recv.at[at],
            device_id=device, device_id_type=MESH,
        )
        copy.start()
        self.sent.append(copy)
        return self.track(copy.wait_recv, source, link)

    def copy(self, source, target):
        copy = pltpu.make_async_copy(source, target, self.local.at[self.copied])
        copy.start()
        self.copied += 1
        return self.track(copy.wait, source, "local")

    def finish(self):
        for copy in self.sent:
            copy.wait_send()


def run(lines, works, plan, start=3.0):
    traffic, now = lines.traffic, start
    open_works, late, plan = [], None, dict(plan)
    limit = plan.get("backlog", BACKLOG)

    def add(label, work):
        rank, begin = plan.get(label, (0.0, 0.0))
        open_works.append([rank, begin, work, next(work)])
        open_works.sort(key=lambda entry: entry[0])

    for work in works:
        if isinstance(work, list):
            late = work
        else:
            add(*work)
    while open_works:
        traffic.advance(now)
        for entry in open_works:
            waits, cost, link = entry[3]
            arrived = all(transfer["done"] is not None and transfer["done"] <= now for _, transfer in waits)
            if arrived and now >= entry[1] and (link is None or traffic.backlog(link) < limit):
                break
        else:
            now += 0.25
            continue
        for wait, _ in waits:
            wait()
        entry[1], entry[3] = 0.0, next(entry[2], None)
        now += cost + 0.15
        if entry[3] is None:
            open_works.remove(entry)
        while late:
            add(*late.pop(0))


def gather_team(lines, me, source, whole):
    yield [], 0, None
    mine, other = whole.at[me.zl, me.s], whole.at[1 - me.zl, me.s]
    across = lines.push(source, mine, me.at(zl=1 - me.zl), "zl")
    waits = [lines.copy(source, mine), lines.push(source, mine, me.at(s=1 - me.s), "s")]
    yield [across], 0, None
    waits.append(lines.push(other, other, me.at(s=1 - me.s), "s"))
    yield waits, 0, None


def gather_columns(lines, me, cut, whole, piece):
    other, start, size = piece
    s, columns = 1 - me.s if other else me.s, pl.ds(start, size)
    yield [], 0, "s"
    waits = []
    for flip in (0, 1):
        zl = 1 - me.zl if flip else me.zl
        for source, at in cut(s, zl, start, size):
            mine = whole.at[me.s, me.zh, me.zl, me.y, me.c, :, pl.ds(at, source.shape[1])]
            if other or flip:
                link = "diagonal" if other and flip else "s" if other else "zl"
                waits.append(lines.push(source, mine, me.at(s=s, zl=zl), link))
            else:
                waits.append(lines.copy(source, mine))
    yield waits, 0, "zh"
    part = whole.at[s, me.zh, :, me.y, me.c, :, columns]
    waits = [lines.push(part, part, me.at(zh=zh), "zh") for zh in me.highs()]
    yield waits, 0, "y"
    part = whole.at[s, :, :, me.y, me.c, :, columns]
    wait = lines.push(part, part, me.at(y=1 - me.y), "y")
    yield [wait], 0, None
    part = whole.at[s, :, :, :, me.c, :, columns]
    wait = lines.push(part, part, me.at(c=1 - me.c), "c")
    yield [wait], 0, None


def ready_cut(cut):
    return lambda s, zl, start, size: [(cut.at[s * 2 + zl, :, pl.ds(start, size)], start)]


def block_cut(zhs, shard, block):
    def cut(s, zl, start, size):
        found = []
        for at in range(start, start + size, block):
            number, zh = at // (zhs * block), at // block % zhs
            column = (number * 4 * zhs + (s * zhs + zh) * 2 + zl) * block
            found.append((shard.at[:, pl.ds(pl.multiple_of(column, block), block)], at))
        return found

    return cut


def swap_halves(left, right):
    width = left.shape[1]
    first = lax.broadcasted_iota(jnp.int32, (1, width), 1) < width // 2
    return (
        jnp.where(first, left, pltpu.roll(right, width // 2, 1)),
        jnp.where(first, pltpu.roll(left, width // 2, 1), right),
    )


def gather_rows(lines, me, source, whole, start, size):
    rows = pl.ds(start, size)
    yield [], 0, "zh"
    mine = whole.at[me.zh, me.y, me.c, rows]
    waits = [lines.copy(source.at[rows], mine)]
    waits += [lines.push(source.at[rows], mine, me.at(zh=zh), "zh") for zh in me.highs()]
    yield waits, 0, "y"
    part = whole.at[:, me.y, me.c, rows]
    wait = lines.push(part, part, me.at(y=1 - me.y), "y")
    yield [wait], 0, None
    part = whole.at[:, :, me.c, rows]
    wait = lines.push(part, part, me.at(c=1 - me.c), "c")
    yield [wait], 0, None


def add_into(target, sources, result=None):
    result = target if result is None else result

    def step(at, carry):
        rows = pl.ds(pl.multiple_of(at * ROWS, ROWS), ROWS)
        total = target[rows].astype(F32)
        for source in sources:
            total = total + source[rows].astype(F32)
        result[rows] = total.astype(result.dtype)
        return carry

    lax.fori_loop(0, target.shape[0] // ROWS, step, 0)


def add_time(*refs):
    return sum(int(np.prod(ref.shape)) for ref in refs) * ADD_TIME


ADD_TIME = 1.6e-6


def sum_columns(lines, me, grad, cut, buffers, piece):
    first, second, third = buffers
    other, start, size = piece
    s, columns = 1 - me.s if other else me.s, pl.ds(start, size)
    mine = grad.at[s, :, :, :, me.c, :, columns]
    yield [], 0, "c"
    wait = lines.push(grad.at[s, :, :, :, 1 - me.c, :, columns], first, me.at(c=1 - me.c), "c")
    yield [wait], add_time(first) / 2, "y"

    def fold(y):
        for zh in range(me.zhs):
            for zl in range(2):
                add_into(mine.at[zh, zl, y], [first.at[zh, zl, y]])

    fold(1 - me.y)
    wait = lines.push(mine.at[:, :, 1 - me.y], second, me.at(y=1 - me.y), "y")
    yield [], add_time(first) / 2, None
    fold(me.y)
    yield [wait], add_time(second), "zh"
    waits = []
    for step, zh in enumerate([*me.highs(), me.zh]):
        for zl in range(2):
            add_into(mine.at[zh, zl, me.y], [second.at[zh, zl]])
        if step < me.zhs - 1:
            waits.append(lines.push(mine.at[zh, :, me.y], third.at[step], me.at(zh=zh), "zh"))
    yield waits, add_time(third), None
    for zl in range(2):
        add_into(mine.at[me.zh, zl, me.y], [third.at[step, zl] for step in range(me.zhs - 1)])
    waits = []
    for flip in (0, 1):
        zl = 1 - me.zl if flip else me.zl
        source, target = mine.at[me.zh, zl, me.y], cut.at[me.s * 2 + me.zl, :, columns]
        if other or flip:
            link = "diagonal" if other and flip else "s" if other else "zl"
            waits.append(lines.push(source, target, me.at(s=s, zl=zl), link))
        else:
            waits.append(lines.copy(source, target))
    yield waits, 0, None


def sum_near(lines, me, grad, buffers, piece):
    first, second = buffers
    rows = pl.ds(*piece)
    mine = grad.at[:, :, me.c, rows]
    yield [], 0, "c"
    wait = lines.push(grad.at[:, :, 1 - me.c, rows], first, me.at(c=1 - me.c), "c")
    yield [wait], add_time(first) / 2, "y"
    for zh in range(me.zhs):
        add_into(mine.at[zh, 1 - me.y], [first.at[zh, 1 - me.y]])
    wait = lines.push(mine.at[:, 1 - me.y], second, me.at(y=1 - me.y), "y")
    yield [], add_time(first) / 2, None
    for zh in range(me.zhs):
        add_into(mine.at[zh, me.y], [first.at[zh, me.y]])
    yield [wait], add_time(second), None
    for zh in range(me.zhs):
        add_into(mine.at[zh, me.y], [second.at[zh]])


def sum_far(lines, me, part, total, buffers, piece):
    mine, third, final = buffers
    rows = pl.ds(*piece)
    yield [], 0, "zh"
    waits = [lines.copy(part.at[me.zh, rows], mine)]
    for step, zh in enumerate(me.highs()):
        waits.append(lines.push(part.at[zh, rows], third.at[step], me.at(zh=zh), "zh"))
    yield waits, add_time(third), None
    add_into(mine, [third.at[step] for step in range(me.zhs - 1)], final)
    wait = lines.copy(final, total.at[rows])
    yield [wait], 0, None


def sum_rows(lines, me, grad, total, near, far, piece):
    yield from sum_near(lines, me, grad, near, piece)
    yield from sum_far(lines, me, grad.at[:, me.y, me.c], total, far, piece)


def sum_team(lines, me, partial, own, passed, taken):
    load = lines.copy(partial.at[1 - me.zl, me.s], passed)
    first = send_rows(lines, me, partial, taken, 1 - me.zl)
    yield [load, first], add_time(passed), None
    waits = [lines.copy(partial.at[me.zl, me.s], own), send_rows(lines, me, partial, taken, me.zl)]
    add_into(passed, [taken.at[1 - me.zl]])
    waits.append(lines.push(passed, taken.at[2], me.at(zl=1 - me.zl), "zl"))
    yield waits, 3, None


def send_rows(lines, me, partial, taken, zl):
    return lines.push(partial.at[zl, 1 - me.s], taken.at[zl], me.at(s=1 - me.s), "s")


def end_team(lines, me, partial, own, passed, taken, started):
    load = lines.copy(partial.at[1 - me.zl, me.s], passed)
    keep = lines.copy(partial.at[me.zl, me.s], own)
    yield [load, *started], add_time(passed), None
    add_into(passed, [taken.at[1 - me.zl]])
    wait = lines.push(passed, taken.at[2], me.at(zl=1 - me.zl), "zl")
    yield [keep, wait], 3, None


def team_total(me, own, taken, rows):
    return own[rows].astype(F32) + taken[me.zl, rows].astype(F32) + taken[2, rows].astype(F32)


def by_rows(count, body):
    def step(at, carry):
        body(pl.ds(pl.multiple_of(at * ROWS, ROWS), ROWS))
        return carry

    lax.fori_loop(0, count // ROWS, step, 0)


def row_pieces(size, parts):
    tiles, pieces, start = size // ROWS, [], 0
    for part in range(parts):
        count = (tiles * (part + 1) // parts - tiles * part // parts) * ROWS
        pieces.append((start, count))
        start += count
    return pieces


def column_pieces(columns, parts):
    lanes, pieces, start = columns // 128, [], 0
    for part in range(parts):
        size = (lanes * (part + 1) // parts - lanes * part // parts) * 128
        pieces.append((start, size))
        start += size
    return [(other, *piece) for other in (False, True) for piece in pieces]


def turn_pairs(values, tables, sign):
    return (
        values * tables[0]
        + pltpu.roll(values, 128 - ROTARY // 2, 1) * (tables[1] * sign)
        + pltpu.roll(values, ROTARY // 2, 1) * (tables[2] * sign)
    )


def rotary_tables(length):
    lane = np.arange(128) % HEAD_DIM
    halves = ROTARY // 2
    frequency = np.float32(10000.0) ** (np.float32(-2.0) * np.arange(halves, dtype=np.float32) / np.float32(ROTARY))
    angles = np.arange(length, dtype=np.float32)[:, None] * frequency[lane % halves][None, :]
    rotated = lane < ROTARY
    return np.stack([
        np.where(rotated, np.cos(angles), 1.0),
        np.where(lane < halves, -np.sin(angles), 0.0),
        np.where(rotated & (lane >= halves), np.sin(angles), 0.0),
    ]).astype(np.float32)


def lane_masks():
    lane = lax.broadcasted_iota(jnp.int32, (1, 128), 1)
    return [(lane < HEAD_DIM).astype(F32).astype(BF), (lane >= HEAD_DIM).astype(F32).astype(BF)], lane < HEAD_DIM


def softmax_rows(query, key):
    length = query.shape[0]
    scores = dot_nt(query, key) * 0.125
    below = lax.broadcasted_iota(jnp.int32, (length, length), 0) >= lax.broadcasted_iota(
        jnp.int32, (length, length), 1
    )
    scores = jnp.where(below, scores, -1e30)
    exponent = jnp.exp(scores - jnp.max(scores, axis=-1, keepdims=True))
    return exponent / jnp.sum(exponent, axis=-1, keepdims=True)


def pairs_of(seq, length, part, body):
    def step(at, carry):
        body(pl.ds(seq * length, length), pl.ds(pl.multiple_of(at * 128, 128), 128))
        return carry

    lax.fori_loop(0, part // 128, step, 0)


def forward_attention(first, weight, offset, tables, queries, keys, values, mixed, leave):
    length, part = tables.shape[1], queries.shape[1]
    seqs = queries.shape[0] // length
    for number, target in enumerate((queries, keys, values)):
        for start in range(0, part, 256):
            at = number * part + start
            block = dot(first[...], weight[:, at : at + 256]) + offset[:, at : at + 256]
            if target is values:
                target[:, start : start + 256] = block.astype(BF)
                continue
            for seq in range(seqs):
                for lanes in range(0, 256, 128):
                    rows = slice(seq * length, (seq + 1) * length)
                    turned = turn_pairs(block[rows, lanes : lanes + 128], tables, 1.0)
                    target[rows, start + lanes : start + lanes + 128] = turned.astype(BF)
        yield [], 2.5 if number < 2 else 7, None

    masks, left = lane_masks()
    for seq in range(seqs):

        def body(rows, lanes):
            query, key, value = queries[rows, lanes], keys[rows, lanes], values[rows, lanes]
            sides = [dot(softmax_rows(query * mask, key).astype(BF), value) for mask in masks]
            mixed[rows, lanes] = jnp.where(left, *sides).astype(BF)

        pairs_of(seq, length, part, body)
        leave(seq)
        if seq < seqs - 1:
            yield [], 7, None


def backward_attention(grad_mixed, tables, queries, keys, values, grad_projected):
    length, part = tables.shape[1], queries.shape[1]
    seqs = queries.shape[0] // length
    masks, left = lane_masks()
    for seq in range(seqs):

        def body(rows, lanes):
            query, key, value = queries[rows, lanes], keys[rows, lanes], values[rows, lanes]
            grad = grad_mixed[rows, lanes]
            sides = []
            for mask in masks:
                probs = softmax_rows(query * mask, key)
                grad_probs = dot_nt(grad * mask, value)
                grad_scores = (
                    probs * (grad_probs - jnp.sum(probs * grad_probs, axis=-1, keepdims=True))
                ).astype(BF)
                sides.append((
                    dot(grad_scores, key) * 0.125,
                    dot_tn(grad_scores, query) * 0.125,
                    dot_tn(probs.astype(BF), grad),
                ))
            grads = [jnp.where(left, *pair).astype(BF) for pair in zip(*sides)]
            start = lanes.start
            for number, found in enumerate(grads):
                if number < 2:
                    found = turn_pairs(found.astype(F32), tables, -1.0).astype(BF)
                grad_projected[rows, pl.ds(pl.multiple_of(start + number * part, 128), 128)] = found

        pairs_of(seq, length, part, body)
        yield [], 9 if seq < seqs - 1 else 1, None


def enter_kernel(
    zhs, tokens, small, qkv, out, gate, up,
    tokens_all, small_all, qkv_all, out_all, gate_cut, up_cut, shard, cuts, send, recv, local,
):
    me, lines = Place(zhs), Lines(send, recv, local)
    loads = [lines.copy(gate, shard.at[0]), lines.copy(up, shard.at[1])]
    me.greet()
    block = qkv_all.shape[6] // 3 // zhs

    def cut_work():
        width = cuts.shape[3]
        kept = []
        for number, target in enumerate((gate_cut, up_cut)):
            yield loads if number == 0 else [], 2, None
            for s in range(2):
                at = 2 * s * width
                left = shard[number, :, at : at + width].astype(F32)
                right = shard[number, :, at + width : at + 2 * width].astype(F32)
                for zl, found in enumerate(swap_halves(left, right)):
                    cuts[number, s * 2 + zl] = found.astype(BF)
            kept.append(lines.copy(cuts.at[number], target))
        yield kept, 0, None

    run(lines, [
        *[("small", gather_columns(lines, me, ready_cut(small), small_all, (other, 0, 128))) for other in (False, True)],
        *[
            (f"qkv{at}", gather_columns(lines, me, block_cut(zhs, qkv, block), qkv_all, piece))
            for at, piece in enumerate(column_pieces(qkv_all.shape[6], QKV_GATHERS))
        ],
        *[
            (f"out{at}", gather_rows(lines, me, out, out_all, *piece))
            for at, piece in enumerate(row_pieces(out.shape[0], OUT_PARTS))
        ],
        ("tokens", gather_team(lines, me, tokens, tokens_all)),
        ("cut", cut_work()),
    ], ENTER_PLAN)
    lines.finish()


def middle_kernel(
    zhs, tokens, upstream, tokens_all, qkv_all, out_all, gate_cut, up_cut, down,
    first_gain, first_bias, offset, gain, bias, tables,
    middle, first_out, queries_out, keys_out, values_out, mixed_out,
    upstream_all, input_all, gate_all, up_all, down_all,
    whole, first, weight, out_weight, queries, keys, values, mixed, partial,
    own, passed, taken, second, send, recv, local,
):
    me, lines = Place(zhs), Lines(send, recv, local)
    loads = [lines.copy(tokens_all, whole), lines.copy(qkv_all, weight), lines.copy(out_all, out_weight)]
    me.greet()

    def tokens_work():
        yield loads[:1], 4, None

        def normed(rows):
            first[rows] = (norm_rows(whole[rows].astype(F32))[0] * first_gain[...] + first_bias[...]).astype(BF)

        by_rows(whole.shape[0], normed)
        yield loads[1:], 2.5, None
        started = []

        def leave(seq):
            rows = slice(seq * tables.shape[1], (seq + 1) * tables.shape[1])
            for start in range(0, partial.shape[3], 512):
                block = dot(mixed[rows], out_weight[:, start : start + 512]).astype(BF)
                partial[seq, :, :, start : start + 512] = block.reshape(partial.shape[1:3] + (512,))
            started.append(send_rows(lines, me, partial, taken, seq))

        yield from forward_attention(first, weight, offset, tables, queries, keys, values, mixed, leave)
        yield from end_team(lines, me, partial, own, passed, taken, started)

        def body(rows):
            values = tokens[rows].astype(F32) + team_total(me, own, taken, rows)
            middle[rows] = values
            second[rows] = (norm_rows(values)[0] * gain[...] + bias[...]).astype(BF)

        by_rows(middle.shape[0], body)
        kept = [
            lines.copy(source, target)
            for source, target in (
                (first, first_out), (queries, queries_out), (keys, keys_out), (values, values_out), (mixed, mixed_out),
            )
        ]
        yield from gather_team(lines, me, second, input_all)
        yield kept, 0, None

    rows = [gather_rows(lines, me, down, down_all, *piece) for piece in row_pieces(down.shape[0], DOWN_PARTS)]
    columns = [
        gather_columns(lines, me, ready_cut(cut), found, piece)
        for piece in column_pieces(gate_cut.shape[2], FF_PARTS)
        for cut, found in ((gate_cut, gate_all), (up_cut, up_all))
    ]
    run(lines, [
        ("tokens", tokens_work()),
        *[(f"ff{at}", work) for at, work in enumerate(columns)],
        *[(f"down{at}", work) for at, work in enumerate(rows)],
        ("upstream", gather_team(lines, me, upstream, upstream_all)),
    ], MIDDLE_PLAN)
    lines.finish()


def feed_kernel(
    zhs, middle, input_all, upstream_all, gate_all, up_all, down_all,
    result, partial_second_out, grad_gate_out, grad_up_out, down_part,
    second, upstream, gate_weight, up_weight, down_weight, gate, up, hidden, grad_gate, grad_up,
    partial_down, partial_second, grad_down, own, passed, taken, buffers, send, recv, local,
):
    me, lines = Place(zhs), Lines(send, recv, local)
    loads = [
        lines.copy(source, target)
        for source, target in (
            (input_all, second), (gate_all, gate_weight), (up_all, up_weight),
            (upstream_all, upstream), (down_all, down_weight),
        )
    ]
    me.greet()
    spawned, pieces = [], row_pieces(grad_down.shape[3], DOWN_PARTS)
    width, ff = gate_weight.shape
    tiles = [(start, min(256, ff - start)) for start in range(0, ff, 256)]

    def sums(piece, near):
        yield from sum_near(lines, me, grad_down, near, piece)
        rows = pl.ds(*piece)
        wait = lines.copy(grad_down.at[:, me.y, me.c, rows], down_part.at[:, rows])
        yield [wait], 0, None

    def work():
        yield loads[:3], 9, None
        for start, size in tiles:
            at = slice(start, start + size)
            gate_rows = dot(second[...], gate_weight[:, at])
            up_rows = dot(second[...], up_weight[:, at])
            gate[:, at], up[:, at] = gate_rows, up_rows
            hidden[:, at] = (gate_rows * jax.nn.sigmoid(gate_rows) * up_rows).astype(BF)
        yield loads[3:], 4.5, None
        for start in range(0, width, 512):
            block = dot_tn(hidden[...], upstream[:, start : start + 512]).astype(BF)
            grad_down[:, :, :, :, start : start + 512] = block.reshape(grad_down.shape[:4] + (512,))
        spawned.extend((f"down{at}", sums(piece, near)) for at, (piece, near) in enumerate(zip(pieces, buffers)))
        yield [], 4.5, None
        for start in range(0, width, 512):
            block = dot(hidden[...], down_weight[:, start : start + 512]).astype(BF)
            partial_down[:, :, :, start : start + 512] = block.reshape(partial_down.shape[:3] + (512,))
        spawned.append(("result", result_work()))
        yield [], 5, None
        for start, size in tiles:
            at = slice(start, start + size)
            grad_hidden = dot_nt(upstream[...], down_weight[at])
            gate_rows = gate[:, at]
            sigmoid_gate = jax.nn.sigmoid(gate_rows)
            grad_gate[:, at] = (
                grad_hidden * up[:, at] * sigmoid_gate * (1.0 + gate_rows * (1.0 - sigmoid_gate))
            ).astype(BF)
            grad_up[:, at] = (grad_hidden * gate_rows * sigmoid_gate).astype(BF)
        waits = [lines.copy(grad_gate, grad_gate_out), lines.copy(grad_up, grad_up_out)]
        for start in range(0, width, 512):
            yield [], 2.5, None
            block = dot_nt(grad_gate[...], gate_weight[start : start + 512]) + dot_nt(
                grad_up[...], up_weight[start : start + 512]
            )
            partial_second[:, start : start + 512] = block.astype(BF)
        waits.append(lines.copy(partial_second, partial_second_out))
        yield waits, 0, None

    def result_work():
        yield from sum_team(lines, me, partial_down, own, passed, taken)

        def body(rows):
            result[rows] = (middle[rows] + team_total(me, own, taken, rows)).astype(BF)

        by_rows(middle.shape[0], body)

    run(lines, [("work", work()), spawned], FEED_PLAN)
    lines.finish()


def back_kernel(
    zhs, middle, upstream, gain, partial_second, down_part, input_all, gate_in, up_in,
    out_all, queries_in, keys_in, values_in, mixed_in, tables,
    grad_middle, sums, down_total, gate_total, up_total, out_total, projected_out, bias_sums,
    own_second, passed_second, taken_second, attended,
    attended_all, out_weight, queries, keys, values, mixed, grad_mixed, grad_projected, grad_out,
    second, grad_side, grad_gate, grad_up, cuts, joined, down_buffers, out_buffers, buffers, send, recv, local,
):
    me, lines = Place(zhs), Lines(send, recv, local)
    near_loads = [lines.copy(input_all, second), lines.copy(gate_in, grad_side)]
    loads = [
        lines.copy(source, target)
        for source, target in (
            (out_all, out_weight), (queries_in, queries), (keys_in, keys), (values_in, values), (mixed_in, mixed),
        )
    ]
    me.greet()
    spawned = []
    pieces = column_pieces(cuts.shape[3], FF_PARTS)

    def weights_work():
        number = 0
        for which, (grad, total) in enumerate(((grad_gate, gate_total), (grad_up, up_total))):
            yield near_loads if grad is grad_gate else [lines.copy(up_in, grad_side)], 4.5, None
            ff = grad_side.shape[1]
            for start in range(0, ff, 256):
                size = min(256, ff - start)
                block = dot_tn(second[...], grad_side[:, start : start + size]).astype(BF)
                grad[:, :, :, :, :, :, start : start + size] = block.reshape(grad.shape[:6] + (size,))
            left = list(pieces)
            for piece in pieces:
                work = piece_work(grad, which, total, buffers[number], piece, left)
                spawned.append((f"ff{number}", work))
                number += 1

    def piece_work(grad, which, total, found, piece, left):
        yield from sum_columns(lines, me, grad, cuts.at[which], found, piece)
        left.remove(piece)
        if not left:
            spawned.append(("join", join_work(which, total)))

    def join_work(which, total):
        yield [], 2, None
        width, kept = cuts.shape[3], []
        for s in range(2):
            sides = [cuts[which, s * 2 + zl].astype(F32) for zl in range(2)]
            for zh, found in enumerate(swap_halves(*sides)):
                joined[which, s * 2 + zh] = found
                at = (s * 2 + zh) * width
                kept.append(lines.copy(joined.at[which, s * 2 + zh], total.at[:, at : at + width]))
        yield kept, 0, None

    def tokens_work():
        yield [], 0, None
        yield from sum_team(lines, me, partial_second, own_second, passed_second, taken_second)
        sums[...] = jnp.zeros_like(sums)

        def body(rows):
            normed, scale_rows = norm_rows(middle[rows])
            grad = team_total(me, own_second, taken_second, rows)
            sums[0:1] += jnp.sum(grad * normed, axis=0, keepdims=True)
            sums[1:2] += jnp.sum(grad, axis=0, keepdims=True)
            grad = upstream[rows].astype(F32) + norm_back(grad * gain[...], normed, scale_rows)
            grad_middle[rows] = grad
            attended[rows] = grad.astype(BF)

        by_rows(middle.shape[0], body)
        yield from gather_team(lines, me, attended, attended_all)
        yield loads, 4, None
        count, width = mixed.shape[0], attended_all.shape[3]
        for start in range(0, width, 512):
            block = dot_tn(mixed[...], attended_all[:, :, :, start : start + 512].reshape(count, 512))
            grad_out[:, :, :, :, start : start + 512] = block.astype(BF).reshape(grad_out.shape[:4] + (512,))
        for at, piece in enumerate(row_pieces(out_total.shape[0], OUT_PARTS)):
            spawned.append((f"out{at}", sum_rows(lines, me, grad_out, out_total, *out_buffers[at], piece)))
        grad_mixed[...] = dot_nt(attended_all[...].reshape(count, width), out_weight[...]).astype(BF)
        yield [], 9, None
        yield from backward_attention(grad_mixed, tables, queries, keys, values, grad_projected)
        wait = lines.copy(grad_projected, projected_out)
        for start in range(0, grad_projected.shape[1], 256):
            block = jnp.sum(grad_projected[:, start : start + 256].astype(F32), axis=0, keepdims=True)
            bias_sums[:, start : start + 256] = block
        yield [wait], 0, None

    far = [
        sum_far(lines, me, down_part, down_total, found, piece)
        for found, piece in zip(down_buffers, row_pieces(down_total.shape[0], DOWN_PARTS))
    ]
    run(lines, [
        ("tokens", tokens_work()),
        ("weights", weights_work()),
        *[(f"down{at}", work) for at, work in enumerate(far)],
        spawned,
    ], BACK_PLAN)
    lines.finish()


def leave_kernel(
    zhs, tokens, grad_middle, gain, second_sums, bias_sums, grad_projected, first_in, qkv_in,
    grad_inputs, sums, qkv_total,
    first, weight, partial, grad_qkv, cut, own, passed, taken, steps, buffers, send, recv, local,
):
    me, lines = Place(zhs), Lines(send, recv, local)
    loads = [lines.copy(first_in, first), lines.copy(qkv_in, weight)]
    me.greet(corners=True)

    spawned = []
    pieces = column_pieces(cut.shape[2], QKV_PARTS)
    left = list(pieces)

    def piece_work(at):
        yield from sum_columns(lines, me, grad_qkv, cut, buffers[at], pieces[at])
        left.remove(pieces[at])
        if not left:
            block = cut.shape[2] // 3 // zhs
            for s in range(2):
                for zl in range(2):
                    for start in range(0, cut.shape[2], block):
                        number, zh = start // (zhs * block), start // block % zhs
                        column = (number * 4 * zhs + (s * zhs + zh) * 2 + zl) * block
                        found = cut[s * 2 + zl, :, start : start + block]
                        qkv_total[:, column : column + block] = found.astype(F32)

    def weights_work():
        for number in range(QKV_PARTS):
            yield loads[:1] if number == 0 else [], 2.6, None
            _, start, size = pieces[number]
            for at in range(start, start + size, 256):
                block = dot_tn(first[...], grad_projected[:, at : at + 256]).astype(BF)
                grad_qkv[:, :, :, :, :, :, at : at + 256] = block.reshape(grad_qkv.shape[:6] + (256,))
            for at in (number, number + QKV_PARTS):
                spawned.append((f"qkv{at}", piece_work(at)))

    def tokens_work():
        yield loads[1:], 5, None
        for at in range(weight.shape[0] // 256):
            block = dot_nt(grad_projected[...], weight[at * 256 : at * 256 + 256])
            partial[:, :, :, at * 256 : at * 256 + 256] = block.astype(BF).reshape(partial.shape[:3] + (256,))
        yield from sum_team(lines, me, partial, own, passed, taken)
        steps[0] = jnp.zeros_like(steps[0])
        steps[0, 2:4] = second_sums[0:2]
        part = bias_sums.shape[1] // 3
        block = part // zhs
        for number in range(3):
            for zh in range(zhs):
                at = ((me.s * zhs + zh) * 2 + me.zl) * block
                steps[0, 4 + number : 5 + number, pl.ds(pl.multiple_of(at, 64), block)] = bias_sums[
                    :, number * part + zh * block : number * part + (zh + 1) * block
                ]

        def body(rows):
            normed, scale_rows = norm_rows(tokens[rows].astype(F32))
            grad = team_total(me, own, taken, rows)
            steps[0, 0:1] += jnp.sum(grad * normed, axis=0, keepdims=True)
            steps[0, 1:2] += jnp.sum(grad, axis=0, keepdims=True)
            grad_inputs[rows] = grad_middle[rows] + norm_back(grad * gain[...], normed, scale_rows)

        by_rows(tokens.shape[0], body)
        others = [(zh, y) for y in (me.y, 1 - me.y) for zh in (me.zh, *me.highs())][1:]
        groups = [
            [(me.at(s=mate_s, zl=mate_zl), link) for (mate_s, mate_zl), link in zip(me.mates(), ("zl", "s", "diagonal"))],
            [(me.at(zh=zh, y=y), "zh" if y is me.y else "y") for zh, y in others],
            [(me.at(c=1 - me.c), "c")],
        ]
        at = 0
        for group in groups:
            arrived = [
                lines.push(steps.at[at], steps.at[at + 1 + number], device, link)
                for number, (device, link) in enumerate(group)
            ]
            yield arrived, 0.3, None
            total = steps[at]
            for number in range(len(group)):
                total = total + steps[at + 1 + number]
            at += len(group) + 1
            steps[at] = total
        sums[...] = steps[at]

    run(lines, [("weights", weights_work()), ("tokens", tokens_work()), spawned], LEAVE_PLAN)
    lines.finish()


def near_buffers(zhs, size, width):
    return tuple(pltpu.VMEM(shape + (size, width), BF) for shape in ((zhs, 2), (zhs,)))


def far_buffers(zhs, size, width):
    return (
        pltpu.VMEM((size, width), BF), pltpu.VMEM((zhs - 1, size, width), BF), pltpu.VMEM((size, width), F32)
    )


def column_buffers(zhs, own, columns):
    return tuple(
        pltpu.VMEM(shape + (own, columns), BF) for shape in ((zhs, 2, 2), (zhs, 2), (zhs - 1, 2))
    )


IN_HBM = pl.BlockSpec(memory_space=pl.ANY)
IN_VMEM = pl.BlockSpec(memory_space=pltpu.VMEM)


def call(kernel, zhs, number, inputs, outputs, scratch, copies, locals_, limit):
    return pl.pallas_call(
        lambda *refs: kernel(zhs, *refs),
        out_shape=[jax.ShapeDtypeStruct(shape, kind) for shape, kind, _ in outputs],
        in_specs=[spec for _, spec in inputs],
        out_specs=[spec for _, _, spec in outputs],
        scratch_shapes=[
            *scratch,
            pltpu.SemaphoreType.DMA((copies,)),
            pltpu.SemaphoreType.DMA((copies,)),
            pltpu.SemaphoreType.DMA((locals_,)),
        ],
        compiler_params=pltpu.CompilerParams(
            collective_id=number, has_side_effects=True, vmem_limit_bytes=limit << 20
        ),
    )(*[array for array, _ in inputs])


def per_device(
    tokens, cotangent, norm1_gain, norm1_bias, qkv_weight, qkv_bias, out_weight,
    norm2_gain, norm2_bias, gate_weight, up_weight, down_weight,
):
    zh = lax.axis_size("zh")
    rows = tokens.shape[1]
    width = tokens.shape[2]
    own = qkv_weight.shape[0]
    ff = gate_weight.shape[1]
    ff_own = down_weight.shape[0]
    half = lax.axis_size("seq")
    length = rows * half
    seqs = lax.axis_size("zl")
    team = half * seqs
    part = width // team
    ff_part = ff // team
    devices = width // own
    tokens, cotangent = tokens[0], cotangent[0]
    index = (lax.axis_index("seq") * (devices // half)
             + ((lax.axis_index("zh") * 2 + lax.axis_index("zl")) * 2 + lax.axis_index("y")) * 2
             + lax.axis_index("c"))

    def mine_columns(whole, parts):
        block = whole.shape[0] // parts // (half * zh * seqs)
        cut = whole.reshape(parts, half, zh, seqs, block)
        cut = lax.dynamic_index_in_dim(cut, lax.axis_index("seq"), 1, keepdims=False)
        cut = lax.dynamic_index_in_dim(cut, lax.axis_index("zl"), 2, keepdims=False)
        return cut.reshape(-1)

    small = jnp.concatenate([norm1_gain, norm1_bias, norm2_gain, norm2_bias, qkv_bias]).astype(F32)
    small = jnp.pad(small, (0, 1024 - small.shape[0])).reshape(8, 128)
    small = jnp.broadcast_to(small, (team, 8, 128))
    token_shape = (seqs, half, rows, width)
    owners = (half, zh, seqs, 2, 2)
    count = team * rows
    limit = 60
    tables = rotary_tables(length)
    tokens_all, small_all, qkv_all, out_all, gate_cut, up_cut = call(
        enter_kernel, zh, 0,
        [
            (tokens, IN_HBM), (small, IN_HBM), (qkv_weight, IN_HBM), (out_weight, IN_HBM),
            (gate_weight, IN_HBM), (up_weight, IN_HBM),
        ],
        [
            (token_shape, BF, IN_HBM),
            (owners + (8, 128), F32, IN_HBM),
            (owners + (own, 3 * part), BF, IN_HBM),
            ((zh, 2, 2, own, width), BF, IN_HBM),
            ((team, own, ff_part), BF, IN_HBM),
            ((team, own, ff_part), BF, IN_HBM),
        ],
        [pltpu.VMEM((2, own, ff), BF), pltpu.VMEM((2, team, own, ff_part), BF)],
        3 + (2 + OUT_PARTS) * (zh + 4) + DOWN_PARTS * zh + 2 * QKV_GATHERS * (3 * zh + 2), 32, 60,
    )
    small = small_all.reshape(devices, 1024)
    first_gain = small[:, :own].reshape(1, width)
    first_bias = small[:, own : 2 * own].reshape(1, width)
    second_gain = small[:, 2 * own : 3 * own].reshape(1, width)
    second_bias = small[:, 3 * own : 4 * own].reshape(1, width)
    qkv_offset = mine_columns(small[:, 4 * own : 7 * own].reshape(-1), 3).reshape(1, 3 * part)
    qkv_matrix = qkv_all.reshape(width, 3 * part)
    out_matrix = out_all.reshape(part, width)

    token_scratch = [
        pltpu.VMEM((rows, width), BF), pltpu.VMEM((rows, width), BF), pltpu.VMEM((3, rows, width), BF)
    ]
    head_shape = (count, part)
    heads = [(head_shape, BF, IN_HBM)] * 4
    head_scratch = [pltpu.VMEM(head_shape, BF)] * 4
    (
        middle, first_input, queries, keys, values, mixed, upstream_all, input_all, gate_all, up_all, down_all,
    ) = call(
        middle_kernel, zh, 1,
        [
            (tokens, IN_VMEM), (cotangent, IN_HBM), (tokens_all.reshape(count, width), IN_HBM),
            (qkv_matrix, IN_HBM), (out_matrix, IN_HBM),
            (gate_cut, IN_HBM), (up_cut, IN_HBM), (down_weight, IN_HBM),
            (first_gain, IN_VMEM), (first_bias, IN_VMEM), (qkv_offset, IN_VMEM),
            (second_gain, IN_VMEM), (second_bias, IN_VMEM), (tables, IN_VMEM),
        ],
        [
            ((rows, width), F32, IN_VMEM),
            ((count, width), BF, IN_HBM),
            *heads,
            (token_shape, BF, IN_HBM),
            (token_shape, BF, IN_HBM),
            (owners + (own, ff_part), BF, IN_HBM),
            (owners + (own, ff_part), BF, IN_HBM),
            ((zh, 2, 2, ff_own, width), BF, IN_HBM),
        ],
        [
            pltpu.VMEM((count, width), BF), pltpu.VMEM((count, width), BF),
            pltpu.VMEM((width, 3 * part), BF), pltpu.VMEM((part, width), BF),
            *head_scratch, pltpu.VMEM(token_shape, BF),
            *token_scratch, pltpu.VMEM((rows, width), BF),
        ],
        9 + (DOWN_PARTS + 4 * FF_PARTS) * (zh + 4), 40, limit,
    )
    second_input = input_all.reshape(count, width)
    ff_shape = (count, ff_part)
    down_pieces = [size for _, size in row_pieces(ff_own, DOWN_PARTS)]
    result, partial_second, grad_gate, grad_up, down_part = call(
        feed_kernel, zh, 4,
        [
            (middle, IN_VMEM), (second_input, IN_HBM), (upstream_all.reshape(count, width), IN_HBM),
            (gate_all.reshape(width, ff_part), IN_HBM), (up_all.reshape(width, ff_part), IN_HBM),
            (down_all.reshape(ff_part, width), IN_HBM),
        ],
        [
            ((rows, width), BF, IN_VMEM),
            ((count, width), BF, IN_HBM),
            (ff_shape, BF, IN_HBM),
            (ff_shape, BF, IN_HBM),
            ((zh, ff_own, width), BF, IN_HBM),
        ],
        [
            pltpu.VMEM((count, width), BF), pltpu.VMEM((count, width), BF),
            pltpu.VMEM((width, ff_part), BF), pltpu.VMEM((width, ff_part), BF), pltpu.VMEM((ff_part, width), BF),
            pltpu.VMEM(ff_shape, F32), pltpu.VMEM(ff_shape, F32),
            *[pltpu.VMEM(ff_shape, BF)] * 3,
            pltpu.VMEM(token_shape, BF), pltpu.VMEM((count, width), BF), pltpu.VMEM(down_all.shape, BF),
            *token_scratch, [near_buffers(zh, size, width) for size in down_pieces],
        ],
        3 + DOWN_PARTS * 2, 32, 62,
    )
    grad_middle, second_sums, down_total, gate_total, up_total, out_total, grad_projected, bias_sums = call(
        back_kernel, zh, 2,
        [
            (middle, IN_VMEM), (cotangent, IN_VMEM), (second_gain, IN_VMEM),
            (partial_second.reshape(token_shape), IN_HBM),
            (down_part, IN_HBM), (second_input, IN_HBM), (grad_gate, IN_HBM), (grad_up, IN_HBM),
            (out_matrix, IN_HBM), (queries, IN_HBM), (keys, IN_HBM), (values, IN_HBM), (mixed, IN_HBM),
            (tables, IN_VMEM),
        ],
        [
            ((rows, width), F32, IN_VMEM),
            ((8, width), F32, IN_VMEM),
            ((ff_own, width), F32, IN_HBM),
            ((own, ff), F32, IN_HBM),
            ((own, ff), F32, IN_HBM),
            ((own, width), F32, IN_HBM),
            ((count, 3 * part), BF, IN_HBM),
            ((1, 3 * part), F32, IN_VMEM),
        ],
        [
            *token_scratch, pltpu.VMEM((rows, width), BF), pltpu.VMEM(token_shape, BF),
            pltpu.VMEM((part, width), BF), *head_scratch, pltpu.VMEM(head_shape, BF),
            pltpu.VMEM((count, 3 * part), BF), pltpu.VMEM(out_all.shape, BF),
            pltpu.VMEM((count, width), BF), pltpu.VMEM(ff_shape, BF),
            pltpu.VMEM(gate_all.shape, BF), pltpu.VMEM(gate_all.shape, BF),
            pltpu.VMEM((2, team, own, ff_part), BF), pltpu.VMEM((2, team, own, ff_part), F32),
            [far_buffers(zh, size, width) for size in down_pieces],
            [
                (near_buffers(zh, size, width), far_buffers(zh, size, width))
                for _, size in row_pieces(own, OUT_PARTS)
            ],
            [
                column_buffers(zh, own, size)
                for _ in range(2)
                for _, _, size in column_pieces(ff_part, FF_PARTS)
            ],
        ],
        9 + (OUT_PARTS + DOWN_PARTS + 4 * FF_PARTS) * (zh + 4), 60, 62,
    )
    grad_inputs, sums, qkv_total = call(
        leave_kernel, zh, 3,
        [
            (tokens, IN_VMEM), (grad_middle, IN_VMEM), (first_gain, IN_VMEM),
            (second_sums, IN_VMEM), (bias_sums, IN_VMEM), (grad_projected, IN_VMEM),
            (first_input, IN_HBM), (qkv_matrix, IN_HBM),
        ],
        [
            ((rows, width), F32, IN_VMEM),
            ((8, width), F32, IN_VMEM),
            ((own, 3 * width), F32, IN_VMEM),
        ],
        [
            pltpu.VMEM((count, width), BF), pltpu.VMEM((width, 3 * part), BF), pltpu.VMEM(token_shape, BF),
            pltpu.VMEM(qkv_all.shape, BF), pltpu.VMEM((team, own, 3 * part), BF),
            *token_scratch, pltpu.VMEM((2 * zh + 8, 8, width), F32),
            [column_buffers(zh, own, size) for _, _, size in column_pieces(3 * part, QKV_PARTS)],
        ],
        2 * zh + 8 + (2 * QKV_PARTS) * (zh + 4), 24, limit,
    )

    def mine(vector_row, size):
        return lax.dynamic_slice_in_dim(vector_row, index * size, size, 0)

    return (
        result[None],
        grad_inputs[None],
        mine(sums[0], own),
        mine(sums[1], own),
        qkv_total,
        mine(sums[4:7].reshape(-1), 3 * own),
        out_total,
        mine(sums[2], own),
        mine(sums[3], own),
        gate_total,
        up_total,
        down_total,
    )


def solution(mesh):
    half, shards = mesh.shape["seq"], mesh.shape["shard"]
    fine = jax.sharding.Mesh(mesh.devices.reshape(half, shards // 8, 2, 2, 2), ALL)
    token = P(("zh", "zl", "y", "c"), "seq", None)
    row = P(ALL)

    def program(*arguments):
        whole_tiles = shards == 16 and arguments[-1].shape[0] // (half * shards) % ROWS == 0
        return jax.shard_map(
            per_device if whole_tiles else plain_device,
            mesh=fine,
            in_specs=(token, token) + (row,) * 10,
            out_specs=(token, token) + (row,) * 10,
            check_vma=False,
        )(*arguments)

    return program
```

```python
import jax
import jax.numpy as jnp
import numpy as np
from jax import lax
from jax.experimental import pallas as pl
from jax.experimental.pallas import tpu as pltpu
from jax.sharding import PartitionSpec as P

HEADS = 32
HEAD_DIM = 64
ROTARY = 16
TEAM = ("seq", "zl")
PEERS = ("zh", "y", "c")
ALL = ("seq", "zh", "zl", "y", "c")
BF = jnp.bfloat16
F32 = jnp.float32


def norm_rows(values):
    centre = jnp.mean(values, axis=-1, keepdims=True)
    centred = values - centre
    spread = jnp.mean(centred * centred, axis=-1, keepdims=True)
    scale_rows = lax.rsqrt(spread + 1e-05)
    return (centred * scale_rows, scale_rows)


def norm_back(grad_normed, normed, scale_rows):
    return scale_rows * (
        grad_normed
        - jnp.mean(grad_normed, axis=-1, keepdims=True)
        - normed * jnp.mean(grad_normed * normed, axis=-1, keepdims=True)
    )


def rotate(values, positions, direction):
    halves = ROTARY // 2
    frequency = 10000.0 ** (-2.0 * jnp.arange(halves, dtype=F32) / ROTARY)
    angles = positions.astype(F32)[:, None] * frequency[None, :]
    cosine_table = jnp.cos(angles)[:, None, :]
    sine_table = jnp.sin(angles)[:, None, :] * direction
    first_half = values[..., :halves]
    second_half = values[..., halves:ROTARY]
    return jnp.concatenate(
        [
            first_half * cosine_table - second_half * sine_table,
            second_half * cosine_table + first_half * sine_table,
            values[..., ROTARY:],
        ],
        axis=-1,
    )


def dot(left, right):
    return jnp.dot(left, right, preferred_element_type=F32)


def dot_nt(left, right):
    return lax.dot_general(left, right, (((1,), (1,)), ((), ())), preferred_element_type=F32)


def dot_tn(left, right):
    return lax.dot_general(left, right, (((0,), (0,)), ((), ())), preferred_element_type=F32)


def plain_device(
    tokens, cotangent, norm1_gain, norm1_bias, qkv_weight, qkv_bias, out_weight,
    norm2_gain, norm2_bias, gate_weight, up_weight, down_weight,
):
    zh = lax.axis_size("zh")
    rows = tokens.shape[1]
    width = tokens.shape[2]
    own = qkv_weight.shape[0]
    ff = gate_weight.shape[1]
    half = lax.axis_size("seq")
    length = rows * half
    team = half * lax.axis_size("zl")
    seqs = lax.axis_size("zl")

    def cut_columns(shard, parts):
        block = shard.shape[1] // parts // (half * zh * seqs)
        cut = shard.reshape(own, parts, half, zh, seqs, block).transpose(2, 4, 0, 1, 3, 5)
        return cut.reshape(team, own, parts * zh * block)

    def join_columns(cut, parts):
        block = cut.shape[2] // parts // zh
        cut = cut.reshape(half, seqs, own, parts, zh, block).transpose(2, 3, 0, 4, 1, 5)
        return cut.reshape(own, -1)

    def mine_columns(whole, parts):
        block = whole.shape[0] // parts // (half * zh * seqs)
        cut = whole.reshape(parts, half, zh, seqs, block)
        cut = lax.dynamic_index_in_dim(cut, lax.axis_index("seq"), 1, keepdims=False)
        cut = lax.dynamic_index_in_dim(cut, lax.axis_index("zl"), 2, keepdims=False)
        return cut.reshape(-1)

    def to_owner_order(values):
        n = values.shape[0]
        return values.reshape(n, half, zh, seqs, 4, own).transpose(0, 2, 4, 1, 3, 5).reshape(n, width)

    def from_owner_order(values):
        n = values.shape[0]
        return values.reshape(n, zh, 4, half, seqs, own).transpose(0, 3, 1, 4, 2, 5).reshape(n, width)

    def gather_columns(shard, parts):
        cut = cut_columns(shard, parts)
        cut = lax.all_to_all(cut, TEAM, split_axis=0, concat_axis=0, tiled=True)
        return lax.all_gather(cut.reshape(team * own, -1), PEERS, axis=0, tiled=True)

    def gather_rows(shard):
        return lax.all_gather(shard, PEERS, axis=0, tiled=True)

    def gather_tokens(values):
        return lax.all_gather(values, ("zl", "seq"), axis=0, tiled=True)

    def sum_tokens(values):
        return lax.psum_scatter(values.astype(BF), ("zl", "seq"), scatter_dimension=0, tiled=True).astype(F32)

    def sum_rows(values):
        return lax.psum_scatter(values.astype(BF), PEERS, scatter_dimension=0, tiled=True)

    def sum_columns(values, parts):
        part = sum_rows(values).reshape(team, own, -1)
        part = lax.all_to_all(part, TEAM, split_axis=0, concat_axis=0, tiled=True)
        return join_columns(part, parts).astype(F32)

    small = jnp.concatenate([norm1_gain, norm1_bias, norm2_gain, norm2_bias, qkv_bias])
    small = lax.all_gather(small, ALL, axis=0, tiled=False)
    first_gain = small[:, :own].reshape(-1).astype(F32)
    first_bias = small[:, own : 2 * own].reshape(-1).astype(F32)
    second_gain = small[:, 2 * own : 3 * own].reshape(-1).astype(F32)
    second_bias = small[:, 3 * own : 4 * own].reshape(-1).astype(F32)
    qkv_offset = mine_columns(small[:, 4 * own :].reshape(-1), 3).astype(F32)

    inputs = tokens[0].astype(F32)
    first_normed, first_scale = norm_rows(inputs)
    first_own = to_owner_order((first_normed * first_gain + first_bias).astype(BF))
    first_input = gather_tokens(first_own)
    qkv_matrix = gather_columns(qkv_weight, 3)
    out_matrix = gather_rows(out_weight)
    gate_matrix = gather_columns(gate_weight, 1)
    up_matrix = gather_columns(up_weight, 1)
    down_matrix = gather_rows(down_weight)
    upstream = gather_tokens(cotangent[0])

    projected = dot(first_input, qkv_matrix) + qkv_offset
    part = width // team
    group_heads = part // HEAD_DIM
    positions = jnp.tile(jnp.arange(length, dtype=jnp.int32), seqs)

    def heads_of(values):
        return values.reshape(seqs, length, group_heads, HEAD_DIM).transpose(0, 2, 1, 3)

    def unheads(values):
        return values.transpose(0, 2, 1, 3).reshape(seqs * length, part)

    queries = heads_of(rotate(projected[:, :part].reshape(-1, group_heads, HEAD_DIM), positions, 1.0).astype(BF))
    keys = heads_of(rotate(projected[:, part : 2 * part].reshape(-1, group_heads, HEAD_DIM), positions, 1.0).astype(BF))
    values = heads_of(projected[:, 2 * part :].astype(BF))
    causal = jnp.arange(length)[:, None] >= jnp.arange(length)[None, :]
    scores = jnp.einsum("shqd,shkd->shqk", queries, keys, preferred_element_type=F32) * 0.125
    scores = jnp.where(causal, scores, -1e30)
    highest = jnp.max(scores, axis=-1, keepdims=True)
    exponent = jnp.exp(scores - highest)
    probs = exponent / jnp.sum(exponent, axis=-1, keepdims=True)
    probs_low = probs.astype(BF)
    mixed = unheads(jnp.einsum("shqk,shkd->shqd", probs_low, values, preferred_element_type=F32).astype(BF))
    middle = inputs + sum_tokens(dot(mixed, out_matrix))

    second_normed, second_scale = norm_rows(middle)
    second_own = to_owner_order((second_normed * second_gain + second_bias).astype(BF))
    second_input = gather_tokens(second_own)
    gate_rows = dot(second_input, gate_matrix)
    up_rows = dot(second_input, up_matrix)
    sigmoid_gate = jax.nn.sigmoid(gate_rows)
    silu_gate = gate_rows * sigmoid_gate
    hidden = (silu_gate * up_rows).astype(BF)
    result = middle + sum_tokens(dot(hidden, down_matrix))

    down_total = sum_rows(dot_tn(hidden, upstream)).astype(F32)
    grad_hidden = dot_nt(upstream, down_matrix)
    grad_gate = (grad_hidden * up_rows * sigmoid_gate * (1.0 + gate_rows * (1.0 - sigmoid_gate))).astype(BF)
    grad_up = (grad_hidden * silu_gate).astype(BF)
    gate_total = sum_columns(dot_tn(second_input, grad_gate), 1)
    up_total = sum_columns(dot_tn(second_input, grad_up), 1)
    grad_second = from_owner_order(sum_tokens(dot_nt(grad_gate, gate_matrix) + dot_nt(grad_up, up_matrix)))
    grad_middle = cotangent[0].astype(F32) + norm_back(grad_second * second_gain, second_normed, second_scale)
    grad_attended = gather_tokens(grad_middle.astype(BF))
    out_total = sum_rows(dot_tn(mixed, grad_attended)).astype(F32)
    grad_mixed = heads_of(dot_nt(grad_attended, out_matrix).astype(BF))
    grad_probs = jnp.einsum("shqd,shkd->shqk", grad_mixed, values, preferred_element_type=F32)
    grad_scores = (probs * (grad_probs - jnp.sum(probs * grad_probs, axis=-1, keepdims=True))).astype(BF)
    grad_queries = (jnp.einsum("shqk,shkd->shqd", grad_scores, keys, preferred_element_type=F32) * 0.125).astype(BF)
    grad_keys = (jnp.einsum("shqk,shqd->shkd", grad_scores, queries, preferred_element_type=F32) * 0.125).astype(BF)
    grad_values = jnp.einsum("shqk,shqd->shkd", probs_low, grad_mixed, preferred_element_type=F32).astype(BF)
    grad_queries = rotate(unheads(grad_queries).astype(F32).reshape(-1, group_heads, HEAD_DIM), positions, -1.0)
    grad_keys = rotate(unheads(grad_keys).astype(F32).reshape(-1, group_heads, HEAD_DIM), positions, -1.0)
    grad_projected = jnp.concatenate(
        [grad_queries.reshape(-1, part).astype(BF), grad_keys.reshape(-1, part).astype(BF), unheads(grad_values)],
        axis=1,
    )
    qkv_total = sum_columns(dot_tn(first_input, grad_projected), 3)
    grad_first = from_owner_order(sum_tokens(dot_nt(grad_projected, qkv_matrix)))
    grad_inputs = grad_middle + norm_back(grad_first * first_gain, first_normed, first_scale)

    bias_part = jnp.sum(grad_projected.astype(F32), axis=0).reshape(3, zh, -1)
    bias_whole = jnp.zeros((3, half, zh, seqs, bias_part.shape[2]), F32)
    bias_whole = lax.dynamic_update_slice(
        bias_whole, bias_part[:, None, :, None], (0, lax.axis_index("seq"), 0, lax.axis_index("zl"), 0)
    ).reshape(-1)
    count = width // own
    sums = jnp.concatenate(
        [
            jnp.sum(grad_first * first_normed, axis=0).reshape(count, own),
            jnp.sum(grad_first, axis=0).reshape(count, own),
            jnp.sum(grad_second * second_normed, axis=0).reshape(count, own),
            jnp.sum(grad_second, axis=0).reshape(count, own),
            bias_whole.reshape(count, 3 * own),
        ],
        axis=1,
    )
    sums = lax.psum_scatter(sums, ALL, scatter_dimension=0, tiled=True)[0]
    return (
        result.astype(BF)[None],
        grad_inputs[None],
        sums[:own],
        sums[own : 2 * own],
        qkv_total,
        sums[4 * own :],
        out_total,
        sums[2 * own : 3 * own],
        sums[3 * own : 4 * own],
        gate_total,
        up_total,
        down_total,
    )


MESH = pl.DeviceIdType.MESH
ROWS = 16
QKV_PARTS, QKV_GATHERS, OUT_PARTS, FF_PARTS, DOWN_PARTS = 2, 3, 2, 2, 4


class Place:
    def __init__(self, zhs):
        self.s, self.zh, self.zl, self.y, self.c = (lax.axis_index(axis) for axis in ALL)
        self.zhs = zhs

    def at(self, **changed):
        return tuple(changed.get(name, getattr(self, name)) for name in ("s", "zh", "zl", "y", "c"))

    def mates(self):
        for flip_s, flip_z in ((0, 1), (1, 0), (1, 1)):
            yield (1 - self.s if flip_s else self.s), (1 - self.zl if flip_z else self.zl)

    def highs(self):
        for step in range(1, self.zhs):
            yield (self.zh + step) % self.zhs

    def greet(self, corners=False):
        partners = [self.at(s=s, zl=zl) for s, zl in self.mates()]
        partners += [self.at(zh=zh) for zh in self.highs()]
        partners += [self.at(y=1 - self.y), self.at(c=1 - self.c)]
        if corners:
            partners += [self.at(zh=zh, y=1 - self.y) for zh in self.highs()]
        barrier = pltpu.get_barrier_semaphore()
        for partner in partners:
            pl.semaphore_signal(barrier, inc=1, device_id=partner, device_id_type=MESH)
        pl.semaphore_wait(barrier, len(partners))


class Traffic:
    def __init__(self):
        self.now, self.active = 0.0, []

    def start(self, demands):
        transfer = {"left": {link: time for link, time in demands.items()}, "done": None}
        self.active.append(transfer)
        return transfer

    def backlog(self, link):
        return sum(transfer["left"].get(link, 0.0) for transfer in self.active)

    def advance(self, until):
        while self.now < until:
            shares = {}
            for transfer in self.active:
                for link in transfer["left"]:
                    shares[link] = shares.get(link, 0) + 1
            step = until - self.now
            for transfer in self.active:
                for link, left in transfer["left"].items():
                    step = min(step, left * shares[link])
            self.now += step
            for transfer in list(self.active):
                transfer["left"] = {
                    link: left - step / shares[link]
                    for link, left in transfer["left"].items()
                    if left - step / shares[link] > 1e-6
                }
                if not transfer["left"]:
                    transfer["done"] = self.now + LATENCY
                    self.active.remove(transfer)


LATENCY = 2.0
ENTER_PLAN = {"small": (7.8, 43), "qkv0": (4.9, 33), "qkv1": (10.8, 0), "qkv2": (6.1, 1), "qkv3": (10.6, 19), "qkv4": (3.8, 13), "qkv5": (11.5, 41), "out0": (2.2, 0), "out1": (2.6, 32), "tokens": (5.8, 13), "cut": (2.3, 40), "backlog": 12}
MIDDLE_PLAN = {"tokens": (0, 0), "ff0": (1, 0), "ff1": (3, 0), "ff2": (4, 0), "ff3": (5, 0), "ff4": (6, 0), "ff5": (7, 0), "ff6": (8, 0), "ff7": (9, 0), "down0": (2, 0), "down1": (10, 0), "down2": (11, 0), "down3": (12, 0), "upstream": (13, 8)}
FEED_PLAN = {"work": (4.9, 0), "down0": (5.9, 0), "down1": (1, 0), "down2": (2.3, 35), "down3": (4.1, 43), "result": (1.3, 0)}
BACK_PLAN = {"tokens": (16.9, 0), "weights": (17.1, 0), "down0": (12.9, 0), "down1": (7.6, 0), "down2": (12.3, 11), "down3": (0.2, 34), "ff0": (14.7, 49), "ff1": (12.6, 10), "ff2": (12.3, 29), "ff3": (3.9, 0), "ff4": (16, 0), "ff5": (6, 0), "ff6": (10.6, 61), "ff7": (9.2, 2), "out0": (6.2, 0), "out1": (16.3, 40), "join": (17.7, 21)}
LEAVE_PLAN = {"weights": (4, 0), "tokens": (1.5, 0), "qkv0": (0.8, 24), "qkv2": (0.1, 0), "qkv1": (0.1, 33), "qkv3": (3.9, 19), "backlog": 7}
BACKLOG = 12.0
LINK_TIME = {
    "s": {"s": 2 / 92e3},
    "zl": {"zl": 2 / 92e3},
    "y": {"y": 2 / 92e3},
    "zh": {"zh": 4 / 92e3, "zl": 2 / 92e3},
    "c": {"c": 1 / 300e3},
    "diagonal": {"s": 2 / 92e3, "zl": 2 / 92e3},
    "local": {"local": 1 / 1500e3},
}


class Lines:
    def __init__(self, send, recv, local):
        self.send, self.recv, self.local = send, recv, local
        self.sent, self.copied, self.traffic = [], 0, Traffic()

    def track(self, wait, source, link):
        size = int(np.prod(source.shape)) * jnp.dtype(source.dtype).itemsize
        return wait, self.traffic.start({name: time * size for name, time in LINK_TIME[link].items()})

    def push(self, source, target, device, link):
        at = len(self.sent)
        copy = pltpu.make_async_remote_copy(
            src_ref=source, dst_ref=target, send_sem=self.send.at[at], recv_sem=self.recv.at[at],
            device_id=device, device_id_type=MESH,
        )
        copy.start()
        self.sent.append(copy)
        return self.track(copy.wait_recv, source, link)

    def copy(self, source, target):
        copy = pltpu.make_async_copy(source, target, self.local.at[self.copied])
        copy.start()
        self.copied += 1
        return self.track(copy.wait, source, "local")

    def finish(self):
        for copy in self.sent:
            copy.wait_send()


def run(lines, works, plan, start=3.0):
    traffic, now = lines.traffic, start
    open_works, late, plan = [], None, dict(plan)
    limit = plan.get("backlog", BACKLOG)

    def add(label, work):
        rank, begin = plan.get(label, (0.0, 0.0))
        open_works.append([rank, begin, work, next(work)])
        open_works.sort(key=lambda entry: entry[0])

    for work in works:
        if isinstance(work, list):
            late = work
        else:
            add(*work)
    while open_works:
        traffic.advance(now)
        for entry in open_works:
            waits, cost, link = entry[3]
            arrived = all(transfer["done"] is not None and transfer["done"] <= now for _, transfer in waits)
            if arrived and now >= entry[1] and (link is None or traffic.backlog(link) < limit):
                break
        else:
            now += 0.25
            continue
        for wait, _ in waits:
            wait()
        entry[1], entry[3] = 0.0, next(entry[2], None)
        now += cost + 0.15
        if entry[3] is None:
            open_works.remove(entry)
        while late:
            add(*late.pop(0))


def gather_team(lines, me, source, whole):
    yield [], 0, None
    mine, other = whole.at[me.zl, me.s], whole.at[1 - me.zl, me.s]
    across = lines.push(source, mine, me.at(zl=1 - me.zl), "zl")
    waits = [lines.copy(source, mine), lines.push(source, mine, me.at(s=1 - me.s), "s")]
    yield [across], 0, None
    waits.append(lines.push(other, other, me.at(s=1 - me.s), "s"))
    yield waits, 0, None


def gather_columns(lines, me, cut, whole, piece):
    other, start, size = piece
    s, columns = 1 - me.s if other else me.s, pl.ds(start, size)
    yield [], 0, "s"
    waits = []
    for flip in (0, 1):
        zl = 1 - me.zl if flip else me.zl
        for source, at in cut(s, zl, start, size):
            mine = whole.at[me.s, me.zh, me.zl, me.y, me.c, :, pl.ds(at, source.shape[1])]
            if other or flip:
                link = "diagonal" if other and flip else "s" if other else "zl"
                waits.append(lines.push(source, mine, me.at(s=s, zl=zl), link))
            else:
                waits.append(lines.copy(source, mine))
    yield waits, 0, "zh"
    part = whole.at[s, me.zh, :, me.y, me.c, :, columns]
    waits = [lines.push(part, part, me.at(zh=zh), "zh") for zh in me.highs()]
    yield waits, 0, "y"
    part = whole.at[s, :, :, me.y, me.c, :, columns]
    wait = lines.push(part, part, me.at(y=1 - me.y), "y")
    yield [wait], 0, None
    part = whole.at[s, :, :, :, me.c, :, columns]
    wait = lines.push(part, part, me.at(c=1 - me.c), "c")
    yield [wait], 0, None


def ready_cut(cut):
    return lambda s, zl, start, size: [(cut.at[s * 2 + zl, :, pl.ds(start, size)], start)]


def block_cut(zhs, shard, block):
    def cut(s, zl, start, size):
        found = []
        for at in range(start, start + size, block):
            number, zh = at // (zhs * block), at // block % zhs
            column = (number * 4 * zhs + (s * zhs + zh) * 2 + zl) * block
            found.append((shard.at[:, pl.ds(pl.multiple_of(column, block), block)], at))
        return found

    return cut


def swap_halves(left, right):
    width = left.shape[1]
    first = lax.broadcasted_iota(jnp.int32, (1, width), 1) < width // 2
    return (
        jnp.where(first, left, pltpu.roll(right, width // 2, 1)),
        jnp.where(first, pltpu.roll(left, width // 2, 1), right),
    )


def gather_rows(lines, me, source, whole, start, size):
    rows = pl.ds(start, size)
    yield [], 0, "zh"
    mine = whole.at[me.zh, me.y, me.c, rows]
    waits = [lines.copy(source.at[rows], mine)]
    waits += [lines.push(source.at[rows], mine, me.at(zh=zh), "zh") for zh in me.highs()]
    yield waits, 0, "y"
    part = whole.at[:, me.y, me.c, rows]
    wait = lines.push(part, part, me.at(y=1 - me.y), "y")
    yield [wait], 0, None
    part = whole.at[:, :, me.c, rows]
    wait = lines.push(part, part, me.at(c=1 - me.c), "c")
    yield [wait], 0, None


def add_into(target, sources, result=None):
    result = target if result is None else result

    size = 2 * ROWS if target.shape[0] % (2 * ROWS) == 0 else ROWS

    def step(at, carry):
        rows = pl.ds(pl.multiple_of(at * size, size), size)
        total = target[rows].astype(F32)
        for source in sources:
            total = total + source[rows].astype(F32)
        result[rows] = total.astype(result.dtype)
        return carry

    lax.fori_loop(0, target.shape[0] // size, step, 0)


def add_time(*refs):
    return sum(int(np.prod(ref.shape)) for ref in refs) * ADD_TIME


ADD_TIME = 1.6e-6


def sum_columns(lines, me, grad, cut, buffers, piece):
    first, second, third = buffers
    other, start, size = piece
    s, columns = 1 - me.s if other else me.s, pl.ds(start, size)
    mine = grad.at[s, :, :, :, me.c, :, columns]
    yield [], 0, "c"
    wait = lines.push(grad.at[s, :, :, :, 1 - me.c, :, columns], first, me.at(c=1 - me.c), "c")
    yield [wait], add_time(first) / 2, "y"

    def fold(y):
        for zh in range(me.zhs):
            for zl in range(2):
                add_into(mine.at[zh, zl, y], [first.at[zh, zl, y]])

    fold(1 - me.y)
    wait = lines.push(mine.at[:, :, 1 - me.y], second, me.at(y=1 - me.y), "y")
    yield [], add_time(first) / 2, None
    fold(me.y)
    yield [wait], add_time(second), "zh"
    waits = []
    for step, zh in enumerate([*me.highs(), me.zh]):
        for zl in range(2):
            add_into(mine.at[zh, zl, me.y], [second.at[zh, zl]])
        if step < me.zhs - 1:
            waits.append(lines.push(mine.at[zh, :, me.y], third.at[step], me.at(zh=zh), "zh"))
    yield waits, add_time(third), None
    for zl in range(2):
        add_into(mine.at[me.zh, zl, me.y], [third.at[step, zl] for step in range(me.zhs - 1)])
    waits = []
    for flip in (0, 1):
        zl = 1 - me.zl if flip else me.zl
        source, target = mine.at[me.zh, zl, me.y], cut.at[me.s * 2 + me.zl, :, columns]
        if other or flip:
            link = "diagonal" if other and flip else "s" if other else "zl"
            waits.append(lines.push(source, target, me.at(s=s, zl=zl), link))
        else:
            waits.append(lines.copy(source, target))
    yield waits, 0, None


def sum_near(lines, me, grad, buffers, piece):
    first, second = buffers
    rows = pl.ds(*piece)
    mine = grad.at[:, :, me.c, rows]
    yield [], 0, "c"
    wait = lines.push(grad.at[:, :, 1 - me.c, rows], first, me.at(c=1 - me.c), "c")
    yield [wait], add_time(first) / 2, "y"
    for zh in range(me.zhs):
        add_into(mine.at[zh, 1 - me.y], [first.at[zh, 1 - me.y]])
    wait = lines.push(mine.at[:, 1 - me.y], second, me.at(y=1 - me.y), "y")
    yield [], add_time(first) / 2, None
    for zh in range(me.zhs):
        add_into(mine.at[zh, me.y], [first.at[zh, me.y]])
    yield [wait], add_time(second), None
    for zh in range(me.zhs):
        add_into(mine.at[zh, me.y], [second.at[zh]])


def sum_far(lines, me, part, total, buffers, piece):
    mine, third, final = buffers
    rows = pl.ds(*piece)
    yield [], 0, "zh"
    waits = [lines.copy(part.at[me.zh, rows], mine)]
    for step, zh in enumerate(me.highs()):
        waits.append(lines.push(part.at[zh, rows], third.at[step], me.at(zh=zh), "zh"))
    yield waits, add_time(third), None
    add_into(mine, [third.at[step] for step in range(me.zhs - 1)], final)
    wait = lines.copy(final, total.at[rows])
    yield [wait], 0, None


def sum_rows(lines, me, grad, total, near, far, piece):
    yield from sum_near(lines, me, grad, near, piece)
    yield from sum_far(lines, me, grad.at[:, me.y, me.c], total, far, piece)


def sum_team(lines, me, partial, own, passed, taken):
    load = lines.copy(partial.at[1 - me.zl, me.s], passed)
    first = send_rows(lines, me, partial, taken, 1 - me.zl)
    yield [load, first], add_time(passed), None
    waits = [lines.copy(partial.at[me.zl, me.s], own), send_rows(lines, me, partial, taken, me.zl)]
    add_into(passed, [taken.at[1 - me.zl]])
    waits.append(lines.push(passed, taken.at[2], me.at(zl=1 - me.zl), "zl"))
    yield waits, 3, None


def send_rows(lines, me, partial, taken, zl):
    return lines.push(partial.at[zl, 1 - me.s], taken.at[zl], me.at(s=1 - me.s), "s")


def end_team(lines, me, partial, own, passed, taken, started):
    load = lines.copy(partial.at[1 - me.zl, me.s], passed)
    keep = lines.copy(partial.at[me.zl, me.s], own)
    yield [load, *started], add_time(passed), None
    add_into(passed, [taken.at[1 - me.zl]])
    wait = lines.push(passed, taken.at[2], me.at(zl=1 - me.zl), "zl")
    yield [keep, wait], 3, None


def team_total(me, own, taken, rows):
    return own[rows].astype(F32) + taken[me.zl, rows].astype(F32) + taken[2, rows].astype(F32)


def by_rows(count, body):
    def step(at, carry):
        body(pl.ds(pl.multiple_of(at * ROWS, ROWS), ROWS))
        return carry

    lax.fori_loop(0, count // ROWS, step, 0)


def row_pieces(size, parts):
    tiles, pieces, start = size // ROWS, [], 0
    for part in range(parts):
        count = (tiles * (part + 1) // parts - tiles * part // parts) * ROWS
        pieces.append((start, count))
        start += count
    return pieces


def column_pieces(columns, parts):
    lanes, pieces, start = columns // 128, [], 0
    for part in range(parts):
        size = (lanes * (part + 1) // parts - lanes * part // parts) * 128
        pieces.append((start, size))
        start += size
    return [(other, *piece) for other in (False, True) for piece in pieces]


def turn_pairs(values, tables, sign):
    return (
        values * tables[0]
        + pltpu.roll(values, 128 - ROTARY // 2, 1) * (tables[1] * sign)
        + pltpu.roll(values, ROTARY // 2, 1) * (tables[2] * sign)
    )


def rotary_tables(length):
    lane = np.arange(128) % HEAD_DIM
    halves = ROTARY // 2
    frequency = np.float32(10000.0) ** (np.float32(-2.0) * np.arange(halves, dtype=np.float32) / np.float32(ROTARY))
    angles = np.arange(length, dtype=np.float32)[:, None] * frequency[lane % halves][None, :]
    rotated = lane < ROTARY
    return np.stack([
        np.where(rotated, np.cos(angles), 1.0),
        np.where(lane < halves, -np.sin(angles), 0.0),
        np.where(rotated & (lane >= halves), np.sin(angles), 0.0),
    ]).astype(np.float32)


def lane_masks():
    lane = lax.broadcasted_iota(jnp.int32, (1, 128), 1)
    return [(lane < HEAD_DIM).astype(F32).astype(BF), (lane >= HEAD_DIM).astype(F32).astype(BF)], lane < HEAD_DIM


def softmax_rows(query, key):
    length = query.shape[0]
    scores = dot_nt(query, key) * 0.125
    below = lax.broadcasted_iota(jnp.int32, (length, length), 0) >= lax.broadcasted_iota(
        jnp.int32, (length, length), 1
    )
    scores = jnp.where(below, scores, -1e30)
    exponent = jnp.exp(scores - jnp.max(scores, axis=-1, keepdims=True))
    return exponent / jnp.sum(exponent, axis=-1, keepdims=True)


def pairs_of(seq, length, part, body):
    def step(at, carry):
        body(pl.ds(seq * length, length), pl.ds(pl.multiple_of(at * 128, 128), 128))
        return carry

    lax.fori_loop(0, part // 128, step, 0)


def forward_attention(first, weight, offset, tables, queries, keys, values, mixed, leave):
    length, part = tables.shape[1], queries.shape[1]
    seqs = queries.shape[0] // length
    for number, target in enumerate((queries, keys, values)):
        for start in range(0, part, 256):
            at = number * part + start
            block = dot(first[...], weight[:, at : at + 256]) + offset[:, at : at + 256]
            if target is values:
                target[:, start : start + 256] = block.astype(BF)
                continue
            for seq in range(seqs):
                for lanes in range(0, 256, 128):
                    rows = slice(seq * length, (seq + 1) * length)
                    turned = turn_pairs(block[rows, lanes : lanes + 128], tables, 1.0)
                    target[rows, start + lanes : start + lanes + 128] = turned.astype(BF)
        yield [], 2.5 if number < 2 else 7, None

    masks, left = lane_masks()
    for seq in range(seqs):

        def body(rows, lanes):
            query, key, value = queries[rows, lanes], keys[rows, lanes], values[rows, lanes]
            sides = [dot(softmax_rows(query * mask, key).astype(BF), value) for mask in masks]
            mixed[rows, lanes] = jnp.where(left, *sides).astype(BF)

        pairs_of(seq, length, part, body)
        leave(seq)
        if seq < seqs - 1:
            yield [], 7, None


def backward_attention(grad_mixed, tables, queries, keys, values, grad_projected):
    length, part = tables.shape[1], queries.shape[1]
    seqs = queries.shape[0] // length
    masks, left = lane_masks()
    for seq in range(seqs):

        def body(rows, lanes):
            query, key, value = queries[rows, lanes], keys[rows, lanes], values[rows, lanes]
            grad = grad_mixed[rows, lanes]
            sides = []
            for mask in masks:
                probs = softmax_rows(query * mask, key)
                grad_probs = dot_nt(grad * mask, value)
                grad_scores = (
                    probs * (grad_probs - jnp.sum(probs * grad_probs, axis=-1, keepdims=True))
                ).astype(BF)
                sides.append((
                    dot(grad_scores, key) * 0.125,
                    dot_tn(grad_scores, query) * 0.125,
                    dot_tn(probs.astype(BF), grad),
                ))
            grads = [jnp.where(left, *pair).astype(BF) for pair in zip(*sides)]
            start = lanes.start
            for number, found in enumerate(grads):
                if number < 2:
                    found = turn_pairs(found.astype(F32), tables, -1.0).astype(BF)
                grad_projected[rows, pl.ds(pl.multiple_of(start + number * part, 128), 128)] = found

        pairs_of(seq, length, part, body)
        yield [], 9 if seq < seqs - 1 else 1, None


def enter_kernel(
    zhs, tokens, small, qkv, out, gate, up,
    tokens_all, small_all, qkv_all, out_all, gate_cut, up_cut, shard, cuts, send, recv, local,
):
    me, lines = Place(zhs), Lines(send, recv, local)
    loads = [lines.copy(gate, shard.at[0]), lines.copy(up, shard.at[1])]
    me.greet()
    block = qkv_all.shape[6] // 3 // zhs

    def cut_work():
        width = cuts.shape[3]
        kept = []
        for number, target in enumerate((gate_cut, up_cut)):
            yield loads if number == 0 else [], 2, None
            for s in range(2):
                at = 2 * s * width
                left = shard[number, :, at : at + width].astype(F32)
                right = shard[number, :, at + width : at + 2 * width].astype(F32)
                for zl, found in enumerate(swap_halves(left, right)):
                    cuts[number, s * 2 + zl] = found.astype(BF)
            kept.append(lines.copy(cuts.at[number], target))
        yield kept, 0, None

    run(lines, [
        *[("small", gather_columns(lines, me, lambda *_: [(small, 0)], small_all, (other, 0, 128))) for other in (False, True)],
        *[
            (f"qkv{at}", gather_columns(lines, me, block_cut(zhs, qkv, block), qkv_all, piece))
            for at, piece in enumerate(column_pieces(qkv_all.shape[6], QKV_GATHERS))
        ],
        *[
            (f"out{at}", gather_rows(lines, me, out, out_all, *piece))
            for at, piece in enumerate(row_pieces(out.shape[0], OUT_PARTS))
        ],
        ("tokens", gather_team(lines, me, tokens, tokens_all)),
        ("cut", cut_work()),
    ], ENTER_PLAN)
    lines.finish()


def middle_kernel(
    zhs, tokens, upstream, tokens_all, qkv_all, out_all, gate_cut, up_cut, down,
    first_gain, first_bias, offset, gain, bias, tables,
    middle, first_out, queries_out, keys_out, values_out, mixed_out,
    upstream_all, input_all, gate_all, up_all, down_all,
    whole, first, weight, out_weight, queries, keys, values, mixed, partial,
    own, passed, taken, second, send, recv, local,
):
    me, lines = Place(zhs), Lines(send, recv, local)
    loads = [lines.copy(tokens_all, whole), lines.copy(qkv_all, weight), lines.copy(out_all, out_weight)]
    me.greet()

    def tokens_work():
        yield loads[:1], 4, None

        def normed(rows):
            first[rows] = (norm_rows(whole[rows].astype(F32))[0] * first_gain[...] + first_bias[...]).astype(BF)

        by_rows(whole.shape[0], normed)
        yield loads[1:], 2.5, None
        started = []

        def leave(seq):
            rows = slice(seq * tables.shape[1], (seq + 1) * tables.shape[1])
            for start in range(0, partial.shape[3], 512):
                block = dot(mixed[rows], out_weight[:, start : start + 512]).astype(BF)
                partial[seq, :, :, start : start + 512] = block.reshape(partial.shape[1:3] + (512,))
            started.append(send_rows(lines, me, partial, taken, seq))

        yield from forward_attention(first, weight, offset, tables, queries, keys, values, mixed, leave)
        yield from end_team(lines, me, partial, own, passed, taken, started)

        def body(rows):
            values = tokens[rows].astype(F32) + team_total(me, own, taken, rows)
            middle[rows] = values
            second[rows] = (norm_rows(values)[0] * gain[...] + bias[...]).astype(BF)

        by_rows(middle.shape[0], body)
        kept = [
            lines.copy(source, target)
            for source, target in (
                (first, first_out), (queries, queries_out), (keys, keys_out), (values, values_out), (mixed, mixed_out),
            )
        ]
        yield from gather_team(lines, me, second, input_all)
        yield kept, 0, None

    rows = [gather_rows(lines, me, down, down_all, *piece) for piece in row_pieces(down.shape[0], DOWN_PARTS)]
    columns = [
        gather_columns(lines, me, ready_cut(cut), found, piece)
        for piece in column_pieces(gate_cut.shape[2], FF_PARTS)
        for cut, found in ((gate_cut, gate_all), (up_cut, up_all))
    ]
    run(lines, [
        ("tokens", tokens_work()),
        *[(f"ff{at}", work) for at, work in enumerate(columns)],
        *[(f"down{at}", work) for at, work in enumerate(rows)],
        ("upstream", gather_team(lines, me, upstream, upstream_all)),
    ], MIDDLE_PLAN)
    lines.finish()


def feed_kernel(
    zhs, middle, input_all, upstream_all, gate_all, up_all, down_all,
    result, partial_second_out, grad_gate_out, grad_up_out, down_part,
    second, upstream, gate_weight, up_weight, down_weight, gate, up, hidden, grad_gate, grad_up,
    partial_down, partial_second, grad_down, own, passed, taken, buffers, send, recv, local,
):
    me, lines = Place(zhs), Lines(send, recv, local)
    loads = [
        lines.copy(source, target)
        for source, target in (
            (input_all, second), (gate_all, gate_weight), (up_all, up_weight),
            (upstream_all, upstream), (down_all, down_weight),
        )
    ]
    me.greet()
    spawned, pieces = [], row_pieces(grad_down.shape[3], DOWN_PARTS)
    width, ff = gate_weight.shape
    tiles = [(start, min(256, ff - start)) for start in range(0, ff, 256)]

    def sums(piece, near):
        yield from sum_near(lines, me, grad_down, near, piece)
        rows = pl.ds(*piece)
        wait = lines.copy(grad_down.at[:, me.y, me.c, rows], down_part.at[:, rows])
        yield [wait], 0, None

    def work():
        yield loads[:3], 9, None
        for start, size in tiles:
            at = slice(start, start + size)
            gate_rows = dot(second[...], gate_weight[:, at])
            up_rows = dot(second[...], up_weight[:, at])
            gate[:, at], up[:, at] = gate_rows, up_rows
            hidden[:, at] = (gate_rows * jax.nn.sigmoid(gate_rows) * up_rows).astype(BF)
        yield loads[3:], 4.5, None
        for start in range(0, width, 512):
            block = dot_tn(hidden[...], upstream[:, start : start + 512]).astype(BF)
            grad_down[:, :, :, :, start : start + 512] = block.reshape(grad_down.shape[:4] + (512,))
        spawned.extend((f"down{at}", sums(piece, near)) for at, (piece, near) in enumerate(zip(pieces, buffers)))
        yield [], 4.5, None
        for start in range(0, width, 512):
            block = dot(hidden[...], down_weight[:, start : start + 512]).astype(BF)
            partial_down[:, :, :, start : start + 512] = block.reshape(partial_down.shape[:3] + (512,))
        spawned.append(("result", result_work()))
        yield [], 5, None
        for start, size in tiles:
            at = slice(start, start + size)
            grad_hidden = dot_nt(upstream[...], down_weight[at])
            gate_rows = gate[:, at]
            sigmoid_gate = jax.nn.sigmoid(gate_rows)
            grad_gate[:, at] = (
                grad_hidden * up[:, at] * sigmoid_gate * (1.0 + gate_rows * (1.0 - sigmoid_gate))
            ).astype(BF)
            grad_up[:, at] = (grad_hidden * gate_rows * sigmoid_gate).astype(BF)
        waits = [lines.copy(grad_gate, grad_gate_out), lines.copy(grad_up, grad_up_out)]
        for start in range(0, width, 512):
            yield [], 2.5, None
            block = dot_nt(grad_gate[...], gate_weight[start : start + 512]) + dot_nt(
                grad_up[...], up_weight[start : start + 512]
            )
            partial_second[:, start : start + 512] = block.astype(BF)
        waits.append(lines.copy(partial_second, partial_second_out))
        yield waits, 0, None

    def result_work():
        yield from sum_team(lines, me, partial_down, own, passed, taken)

        def body(rows):
            result[rows] = (middle[rows] + team_total(me, own, taken, rows)).astype(BF)

        by_rows(middle.shape[0], body)

    run(lines, [("work", work()), spawned], FEED_PLAN)
    lines.finish()


def back_kernel(
    zhs, middle, upstream, gain, partial_second, down_part, input_all, gate_in, up_in,
    out_all, queries_in, keys_in, values_in, mixed_in, tables,
    grad_middle, sums, down_total, gate_total, up_total, out_total, projected_out, bias_sums,
    own_second, passed_second, taken_second, attended,
    attended_all, out_weight, queries, keys, values, mixed, grad_mixed, grad_projected, grad_out,
    second, grad_side, grad_gate, grad_up, cuts, joined, down_buffers, out_buffers, buffers, send, recv, local,
):
    me, lines = Place(zhs), Lines(send, recv, local)
    near_loads = [lines.copy(input_all, second), lines.copy(gate_in, grad_side)]
    loads = [
        lines.copy(source, target)
        for source, target in (
            (out_all, out_weight), (queries_in, queries), (keys_in, keys), (values_in, values), (mixed_in, mixed),
        )
    ]
    me.greet()
    spawned = []
    pieces = column_pieces(cuts.shape[3], FF_PARTS)

    def weights_work():
        number = 0
        for which, (grad, total) in enumerate(((grad_gate, gate_total), (grad_up, up_total))):
            yield near_loads if grad is grad_gate else [lines.copy(up_in, grad_side)], 4.5, None
            ff = grad_side.shape[1]
            for start in range(0, ff, 256):
                size = min(256, ff - start)
                block = dot_tn(second[...], grad_side[:, start : start + size]).astype(BF)
                grad[:, :, :, :, :, :, start : start + size] = block.reshape(grad.shape[:6] + (size,))
            left = list(pieces)
            for piece in pieces:
                work = piece_work(grad, which, total, buffers[number], piece, left)
                spawned.append((f"ff{number}", work))
                number += 1

    def piece_work(grad, which, total, found, piece, left):
        yield from sum_columns(lines, me, grad, cuts.at[which], found, piece)
        left.remove(piece)
        if not left:
            spawned.append(("join", join_work(which, total)))

    def join_work(which, total):
        yield [], 2, None
        width, kept = cuts.shape[3], []
        for s in range(2):
            sides = [cuts[which, s * 2 + zl].astype(F32) for zl in range(2)]
            for zh, found in enumerate(swap_halves(*sides)):
                joined[which, s * 2 + zh] = found
                at = (s * 2 + zh) * width
                kept.append(lines.copy(joined.at[which, s * 2 + zh], total.at[:, at : at + width]))
        yield kept, 0, None

    def tokens_work():
        yield [], 0, None
        yield from sum_team(lines, me, partial_second, own_second, passed_second, taken_second)
        sums[...] = jnp.zeros_like(sums)

        def body(rows):
            normed, scale_rows = norm_rows(middle[rows])
            grad = team_total(me, own_second, taken_second, rows)
            sums[0:1] += jnp.sum(grad * normed, axis=0, keepdims=True)
            sums[1:2] += jnp.sum(grad, axis=0, keepdims=True)
            grad = upstream[rows].astype(F32) + norm_back(grad * gain[...], normed, scale_rows)
            grad_middle[rows] = grad
            attended[rows] = grad.astype(BF)

        by_rows(middle.shape[0], body)
        yield from gather_team(lines, me, attended, attended_all)
        yield loads, 4, None
        count, width = mixed.shape[0], attended_all.shape[3]
        for start in range(0, width, 512):
            block = dot_tn(mixed[...], attended_all[:, :, :, start : start + 512].reshape(count, 512))
            grad_out[:, :, :, :, start : start + 512] = block.astype(BF).reshape(grad_out.shape[:4] + (512,))
        for at, piece in enumerate(row_pieces(out_total.shape[0], OUT_PARTS)):
            spawned.append((f"out{at}", sum_rows(lines, me, grad_out, out_total, *out_buffers[at], piece)))
        grad_mixed[...] = dot_nt(attended_all[...].reshape(count, width), out_weight[...]).astype(BF)
        yield [], 9, None
        yield from backward_attention(grad_mixed, tables, queries, keys, values, grad_projected)
        wait = lines.copy(grad_projected, projected_out)
        for start in range(0, grad_projected.shape[1], 256):
            block = jnp.sum(grad_projected[:, start : start + 256].astype(F32), axis=0, keepdims=True)
            bias_sums[:, start : start + 256] = block
        yield [wait], 0, None

    far = [
        sum_far(lines, me, down_part, down_total, found, piece)
        for found, piece in zip(down_buffers, row_pieces(down_total.shape[0], DOWN_PARTS))
    ]
    run(lines, [
        ("tokens", tokens_work()),
        ("weights", weights_work()),
        *[(f"down{at}", work) for at, work in enumerate(far)],
        spawned,
    ], BACK_PLAN)
    lines.finish()


def leave_kernel(
    zhs, tokens, grad_middle, gain, second_sums, bias_sums, grad_projected, first_in, qkv_in,
    grad_inputs, sums, qkv_total,
    first, weight, partial, grad_qkv, cut, own, passed, taken, steps, buffers, send, recv, local,
):
    me, lines = Place(zhs), Lines(send, recv, local)
    loads = [lines.copy(first_in, first), lines.copy(qkv_in, weight)]
    me.greet(corners=True)

    spawned = []
    pieces = column_pieces(cut.shape[2], QKV_PARTS)
    left = list(pieces)

    def piece_work(at):
        yield from sum_columns(lines, me, grad_qkv, cut, buffers[at], pieces[at])
        left.remove(pieces[at])
        if not left:
            block = cut.shape[2] // 3 // zhs
            for s in range(2):
                for zl in range(2):
                    for start in range(0, cut.shape[2], block):
                        number, zh = start // (zhs * block), start // block % zhs
                        column = (number * 4 * zhs + (s * zhs + zh) * 2 + zl) * block
                        found = cut[s * 2 + zl, :, start : start + block]
                        qkv_total[:, column : column + block] = found.astype(F32)

    def weights_work():
        for number in range(QKV_PARTS):
            yield loads[:1] if number == 0 else [], 2.6, None
            _, start, size = pieces[number]
            for at in range(start, start + size, 256):
                block = dot_tn(first[...], grad_projected[:, at : at + 256]).astype(BF)
                grad_qkv[:, :, :, :, :, :, at : at + 256] = block.reshape(grad_qkv.shape[:6] + (256,))
            for at in (number, number + QKV_PARTS):
                spawned.append((f"qkv{at}", piece_work(at)))

    def tokens_work():
        yield loads[1:], 5, None
        for at in range(weight.shape[0] // 256):
            block = dot_nt(grad_projected[...], weight[at * 256 : at * 256 + 256])
            partial[:, :, :, at * 256 : at * 256 + 256] = block.astype(BF).reshape(partial.shape[:3] + (256,))
        yield from sum_team(lines, me, partial, own, passed, taken)
        steps[0] = jnp.zeros_like(steps[0])
        steps[0, 2:4] = second_sums[0:2]
        part = bias_sums.shape[1] // 3
        block = part // zhs
        for number in range(3):
            for zh in range(zhs):
                at = ((me.s * zhs + zh) * 2 + me.zl) * block
                steps[0, 4 + number : 5 + number, pl.ds(pl.multiple_of(at, 64), block)] = bias_sums[
                    :, number * part + zh * block : number * part + (zh + 1) * block
                ]

        def body(rows):
            normed, scale_rows = norm_rows(tokens[rows].astype(F32))
            grad = team_total(me, own, taken, rows)
            steps[0, 0:1] += jnp.sum(grad * normed, axis=0, keepdims=True)
            steps[0, 1:2] += jnp.sum(grad, axis=0, keepdims=True)
            grad_inputs[rows] = grad_middle[rows] + norm_back(grad * gain[...], normed, scale_rows)

        by_rows(tokens.shape[0], body)
        others = [(zh, y) for y in (me.y, 1 - me.y) for zh in (me.zh, *me.highs())][1:]
        groups = [
            [(me.at(s=mate_s, zl=mate_zl), link) for (mate_s, mate_zl), link in zip(me.mates(), ("zl", "s", "diagonal"))],
            [(me.at(zh=zh, y=y), "zh" if y is me.y else "y") for zh, y in others],
            [(me.at(c=1 - me.c), "c")],
        ]
        at = 0
        for group in groups:
            arrived = [
                lines.push(steps.at[at], steps.at[at + 1 + number], device, link)
                for number, (device, link) in enumerate(group)
            ]
            yield arrived, 0.3, None
            total = steps[at]
            for number in range(len(group)):
                total = total + steps[at + 1 + number]
            at += len(group) + 1
            steps[at] = total
        sums[...] = steps[at]

    run(lines, [("weights", weights_work()), ("tokens", tokens_work()), spawned], LEAVE_PLAN)
    lines.finish()


def near_buffers(zhs, size, width):
    return tuple(pltpu.VMEM(shape + (size, width), BF) for shape in ((zhs, 2), (zhs,)))


def far_buffers(zhs, size, width):
    return (
        pltpu.VMEM((size, width), BF), pltpu.VMEM((zhs - 1, size, width), BF), pltpu.VMEM((size, width), F32)
    )


def column_buffers(zhs, own, columns):
    return tuple(
        pltpu.VMEM(shape + (own, columns), BF) for shape in ((zhs, 2, 2), (zhs, 2), (zhs - 1, 2))
    )


IN_HBM = pl.BlockSpec(memory_space=pl.ANY)
IN_VMEM = pl.BlockSpec(memory_space=pltpu.VMEM)


def call(kernel, zhs, number, inputs, outputs, scratch, copies, locals_, limit):
    return pl.pallas_call(
        lambda *refs: kernel(zhs, *refs),
        out_shape=[jax.ShapeDtypeStruct(shape, kind) for shape, kind, _ in outputs],
        in_specs=[spec for _, spec in inputs],
        out_specs=[spec for _, _, spec in outputs],
        scratch_shapes=[
            *scratch,
            pltpu.SemaphoreType.DMA((copies,)),
            pltpu.SemaphoreType.DMA((copies,)),
            pltpu.SemaphoreType.DMA((locals_,)),
        ],
        compiler_params=pltpu.CompilerParams(
            collective_id=number, has_side_effects=True, vmem_limit_bytes=limit << 20
        ),
    )(*[array for array, _ in inputs])


def per_device(
    tokens, cotangent, norm1_gain, norm1_bias, qkv_weight, qkv_bias, out_weight,
    norm2_gain, norm2_bias, gate_weight, up_weight, down_weight,
):
    zh = lax.axis_size("zh")
    rows = tokens.shape[1]
    width = tokens.shape[2]
    own = qkv_weight.shape[0]
    ff = gate_weight.shape[1]
    ff_own = down_weight.shape[0]
    half = lax.axis_size("seq")
    length = rows * half
    seqs = lax.axis_size("zl")
    team = half * seqs
    part = width // team
    ff_part = ff // team
    devices = width // own
    tokens, cotangent = tokens[0], cotangent[0]
    index = (lax.axis_index("seq") * (devices // half)
             + ((lax.axis_index("zh") * 2 + lax.axis_index("zl")) * 2 + lax.axis_index("y")) * 2
             + lax.axis_index("c"))

    def mine_columns(whole, parts):
        block = whole.shape[0] // parts // (half * zh * seqs)
        cut = whole.reshape(parts, half, zh, seqs, block)
        cut = lax.dynamic_index_in_dim(cut, lax.axis_index("seq"), 1, keepdims=False)
        cut = lax.dynamic_index_in_dim(cut, lax.axis_index("zl"), 2, keepdims=False)
        return cut.reshape(-1)

    small, at = jnp.zeros((1024,), F32), 0
    for vector in (norm1_gain, norm1_bias, norm2_gain, norm2_bias, qkv_bias):
        small += jnp.pad(vector.astype(F32), (at, 1024 - at - vector.shape[0]))
        at += vector.shape[0]
    small = small.reshape(8, 128)
    token_shape = (seqs, half, rows, width)
    owners = (half, zh, seqs, 2, 2)
    count = team * rows
    limit = 60
    tables = rotary_tables(length)
    tokens_all, small_all, qkv_all, out_all, gate_cut, up_cut = call(
        enter_kernel, zh, 0,
        [
            (tokens, IN_HBM), (small, IN_HBM), (qkv_weight, IN_HBM), (out_weight, IN_HBM),
            (gate_weight, IN_HBM), (up_weight, IN_HBM),
        ],
        [
            (token_shape, BF, IN_HBM),
            (owners + (8, 128), F32, IN_HBM),
            (owners + (own, 3 * part), BF, IN_HBM),
            ((zh, 2, 2, own, width), BF, IN_HBM),
            ((team, own, ff_part), BF, IN_HBM),
            ((team, own, ff_part), BF, IN_HBM),
        ],
        [pltpu.VMEM((2, own, ff), BF), pltpu.VMEM((2, team, own, ff_part), BF)],
        3 + (2 + OUT_PARTS) * (zh + 4) + DOWN_PARTS * zh + 2 * QKV_GATHERS * (3 * zh + 2), 32, 60,
    )
    small = small_all.reshape(devices, 1024)
    first_gain = small[:, :own].reshape(1, width)
    first_bias = small[:, own : 2 * own].reshape(1, width)
    second_gain = small[:, 2 * own : 3 * own].reshape(1, width)
    second_bias = small[:, 3 * own : 4 * own].reshape(1, width)
    qkv_offset = mine_columns(small[:, 4 * own : 7 * own].reshape(-1), 3).reshape(1, 3 * part)
    qkv_matrix = qkv_all.reshape(width, 3 * part)
    out_matrix = out_all.reshape(part, width)

    token_scratch = [
        pltpu.VMEM((rows, width), BF), pltpu.VMEM((rows, width), BF), pltpu.VMEM((3, rows, width), BF)
    ]
    head_shape = (count, part)
    heads = [(head_shape, BF, IN_HBM)] * 4
    head_scratch = [pltpu.VMEM(head_shape, BF)] * 4
    (
        middle, first_input, queries, keys, values, mixed, upstream_all, input_all, gate_all, up_all, down_all,
    ) = call(
        middle_kernel, zh, 1,
        [
            (tokens, IN_VMEM), (cotangent, IN_HBM), (tokens_all.reshape(count, width), IN_HBM),
            (qkv_matrix, IN_HBM), (out_matrix, IN_HBM),
            (gate_cut, IN_HBM), (up_cut, IN_HBM), (down_weight, IN_HBM),
            (first_gain, IN_VMEM), (first_bias, IN_VMEM), (qkv_offset, IN_VMEM),
            (second_gain, IN_VMEM), (second_bias, IN_VMEM), (tables, IN_VMEM),
        ],
        [
            ((rows, width), F32, IN_VMEM),
            ((count, width), BF, IN_HBM),
            *heads,
            (token_shape, BF, IN_HBM),
            (token_shape, BF, IN_HBM),
            (owners + (own, ff_part), BF, IN_HBM),
            (owners + (own, ff_part), BF, IN_HBM),
            ((zh, 2, 2, ff_own, width), BF, IN_HBM),
        ],
        [
            pltpu.VMEM((count, width), BF), pltpu.VMEM((count, width), BF),
            pltpu.VMEM((width, 3 * part), BF), pltpu.VMEM((part, width), BF),
            *head_scratch, pltpu.VMEM(token_shape, BF),
            *token_scratch, pltpu.VMEM((rows, width), BF),
        ],
        9 + (DOWN_PARTS + 4 * FF_PARTS) * (zh + 4), 40, limit,
    )
    second_input = input_all.reshape(count, width)
    ff_shape = (count, ff_part)
    down_pieces = [size for _, size in row_pieces(ff_own, DOWN_PARTS)]
    result, partial_second, grad_gate, grad_up, down_part = call(
        feed_kernel, zh, 4,
        [
            (middle, IN_VMEM), (second_input, IN_HBM), (upstream_all.reshape(count, width), IN_HBM),
            (gate_all.reshape(width, ff_part), IN_HBM), (up_all.reshape(width, ff_part), IN_HBM),
            (down_all.reshape(ff_part, width), IN_HBM),
        ],
        [
            ((rows, width), BF, IN_VMEM),
            ((count, width), BF, IN_HBM),
            (ff_shape, BF, IN_HBM),
            (ff_shape, BF, IN_HBM),
            ((zh, ff_own, width), BF, IN_HBM),
        ],
        [
            pltpu.VMEM((count, width), BF), pltpu.VMEM((count, width), BF),
            pltpu.VMEM((width, ff_part), BF), pltpu.VMEM((width, ff_part), BF), pltpu.VMEM((ff_part, width), BF),
            pltpu.VMEM(ff_shape, F32), pltpu.VMEM(ff_shape, F32),
            *[pltpu.VMEM(ff_shape, BF)] * 3,
            pltpu.VMEM(token_shape, BF), pltpu.VMEM((count, width), BF), pltpu.VMEM(down_all.shape, BF),
            *token_scratch, [near_buffers(zh, size, width) for size in down_pieces],
        ],
        3 + DOWN_PARTS * 2, 32, 62,
    )
    grad_middle, second_sums, down_total, gate_total, up_total, out_total, grad_projected, bias_sums = call(
        back_kernel, zh, 2,
        [
            (middle, IN_VMEM), (cotangent, IN_VMEM), (second_gain, IN_VMEM),
            (partial_second.reshape(token_shape), IN_HBM),
            (down_part, IN_HBM), (second_input, IN_HBM), (grad_gate, IN_HBM), (grad_up, IN_HBM),
            (out_matrix, IN_HBM), (queries, IN_HBM), (keys, IN_HBM), (values, IN_HBM), (mixed, IN_HBM),
            (tables, IN_VMEM),
        ],
        [
            ((rows, width), F32, IN_VMEM),
            ((8, width), F32, IN_VMEM),
            ((ff_own, width), F32, IN_HBM),
            ((own, ff), F32, IN_HBM),
            ((own, ff), F32, IN_HBM),
            ((own, width), F32, IN_HBM),
            ((count, 3 * part), BF, IN_HBM),
            ((1, 3 * part), F32, IN_VMEM),
        ],
        [
            *token_scratch, pltpu.VMEM((rows, width), BF), pltpu.VMEM(token_shape, BF),
            pltpu.VMEM((part, width), BF), *head_scratch, pltpu.VMEM(head_shape, BF),
            pltpu.VMEM((count, 3 * part), BF), pltpu.VMEM(out_all.shape, BF),
            pltpu.VMEM((count, width), BF), pltpu.VMEM(ff_shape, BF),
            pltpu.VMEM(gate_all.shape, BF), pltpu.VMEM(gate_all.shape, BF),
            pltpu.VMEM((2, team, own, ff_part), BF), pltpu.VMEM((2, team, own, ff_part), F32),
            [far_buffers(zh, size, width) for size in down_pieces],
            [
                (near_buffers(zh, size, width), far_buffers(zh, size, width))
                for _, size in row_pieces(own, OUT_PARTS)
            ],
            [
                column_buffers(zh, own, size)
                for _ in range(2)
                for _, _, size in column_pieces(ff_part, FF_PARTS)
            ],
        ],
        9 + (OUT_PARTS + DOWN_PARTS + 4 * FF_PARTS) * (zh + 4), 60, 62,
    )
    grad_inputs, sums, qkv_total = call(
        leave_kernel, zh, 3,
        [
            (tokens, IN_VMEM), (grad_middle, IN_VMEM), (first_gain, IN_VMEM),
            (second_sums, IN_VMEM), (bias_sums, IN_VMEM), (grad_projected, IN_VMEM),
            (first_input, IN_HBM), (qkv_matrix, IN_HBM),
        ],
        [
            ((rows, width), F32, IN_VMEM),
            ((8, width), F32, IN_VMEM),
            ((own, 3 * width), F32, IN_VMEM),
        ],
        [
            pltpu.VMEM((count, width), BF), pltpu.VMEM((width, 3 * part), BF), pltpu.VMEM(token_shape, BF),
            pltpu.VMEM(qkv_all.shape, BF), pltpu.VMEM((team, own, 3 * part), BF),
            *token_scratch, pltpu.VMEM((2 * zh + 8, 8, width), F32),
            [column_buffers(zh, own, size) for _, _, size in column_pieces(3 * part, QKV_PARTS)],
        ],
        2 * zh + 8 + (2 * QKV_PARTS) * (zh + 4), 24, limit,
    )

    def mine(vector_row, size):
        return lax.dynamic_slice_in_dim(vector_row, index * size, size, 0)

    return (
        result[None],
        grad_inputs[None],
        mine(sums[0], own),
        mine(sums[1], own),
        qkv_total,
        mine(sums[4:7].reshape(-1), 3 * own),
        out_total,
        mine(sums[2], own),
        mine(sums[3], own),
        gate_total,
        up_total,
        down_total,
    )


def solution(mesh):
    half, shards = mesh.shape["seq"], mesh.shape["shard"]
    fine = jax.sharding.Mesh(mesh.devices.reshape(half, shards // 8, 2, 2, 2), ALL)
    token = P(("zh", "zl", "y", "c"), "seq", None)
    row = P(ALL)

    def program(*arguments):
        whole_tiles = shards == 16 and arguments[-1].shape[0] // (half * shards) % ROWS == 0
        return jax.shard_map(
            per_device if whole_tiles else plain_device,
            mesh=fine,
            in_specs=(token, token) + (row,) * 10,
            out_specs=(token, token) + (row,) * 10,
            check_vma=False,
        )(*arguments)

    return program
```

```python
import jax
import jax.numpy as jnp
import numpy as np
from jax import lax
from jax.experimental import pallas as pl
from jax.experimental.pallas import tpu as pltpu
from jax.sharding import PartitionSpec as P

HEADS = 32
HEAD_DIM = 64
ROTARY = 16
TEAM = ("seq", "zl")
PEERS = ("zh", "y", "c")
ALL = ("seq", "zh", "zl", "y", "c")
BF = jnp.bfloat16
F32 = jnp.float32


def norm_rows(values):
    centre = jnp.mean(values, axis=-1, keepdims=True)
    centred = values - centre
    spread = jnp.mean(centred * centred, axis=-1, keepdims=True)
    scale_rows = lax.rsqrt(spread + 1e-05)
    return (centred * scale_rows, scale_rows)


def norm_back(grad_normed, normed, scale_rows):
    return scale_rows * (
        grad_normed
        - jnp.mean(grad_normed, axis=-1, keepdims=True)
        - normed * jnp.mean(grad_normed * normed, axis=-1, keepdims=True)
    )


def rotate(values, positions, direction):
    halves = ROTARY // 2
    frequency = 10000.0 ** (-2.0 * jnp.arange(halves, dtype=F32) / ROTARY)
    angles = positions.astype(F32)[:, None] * frequency[None, :]
    cosine_table = jnp.cos(angles)[:, None, :]
    sine_table = jnp.sin(angles)[:, None, :] * direction
    first_half = values[..., :halves]
    second_half = values[..., halves:ROTARY]
    return jnp.concatenate(
        [
            first_half * cosine_table - second_half * sine_table,
            second_half * cosine_table + first_half * sine_table,
            values[..., ROTARY:],
        ],
        axis=-1,
    )


def dot(left, right):
    return jnp.dot(left, right, preferred_element_type=F32)


def dot_nt(left, right):
    return lax.dot_general(left, right, (((1,), (1,)), ((), ())), preferred_element_type=F32)


def dot_tn(left, right):
    return lax.dot_general(left, right, (((0,), (0,)), ((), ())), preferred_element_type=F32)


def plain_device(
    tokens, cotangent, norm1_gain, norm1_bias, qkv_weight, qkv_bias, out_weight,
    norm2_gain, norm2_bias, gate_weight, up_weight, down_weight,
):
    zh = lax.axis_size("zh")
    rows = tokens.shape[1]
    width = tokens.shape[2]
    own = qkv_weight.shape[0]
    ff = gate_weight.shape[1]
    half = lax.axis_size("seq")
    length = rows * half
    team = half * lax.axis_size("zl")
    seqs = lax.axis_size("zl")

    def cut_columns(shard, parts):
        block = shard.shape[1] // parts // (half * zh * seqs)
        cut = shard.reshape(own, parts, half, zh, seqs, block).transpose(2, 4, 0, 1, 3, 5)
        return cut.reshape(team, own, parts * zh * block)

    def join_columns(cut, parts):
        block = cut.shape[2] // parts // zh
        cut = cut.reshape(half, seqs, own, parts, zh, block).transpose(2, 3, 0, 4, 1, 5)
        return cut.reshape(own, -1)

    def mine_columns(whole, parts):
        block = whole.shape[0] // parts // (half * zh * seqs)
        cut = whole.reshape(parts, half, zh, seqs, block)
        cut = lax.dynamic_index_in_dim(cut, lax.axis_index("seq"), 1, keepdims=False)
        cut = lax.dynamic_index_in_dim(cut, lax.axis_index("zl"), 2, keepdims=False)
        return cut.reshape(-1)

    def to_owner_order(values):
        n = values.shape[0]
        return values.reshape(n, half, zh, seqs, 4, own).transpose(0, 2, 4, 1, 3, 5).reshape(n, width)

    def from_owner_order(values):
        n = values.shape[0]
        return values.reshape(n, zh, 4, half, seqs, own).transpose(0, 3, 1, 4, 2, 5).reshape(n, width)

    def gather_columns(shard, parts):
        cut = cut_columns(shard, parts)
        cut = lax.all_to_all(cut, TEAM, split_axis=0, concat_axis=0, tiled=True)
        return lax.all_gather(cut.reshape(team * own, -1), PEERS, axis=0, tiled=True)

    def gather_rows(shard):
        return lax.all_gather(shard, PEERS, axis=0, tiled=True)

    def gather_tokens(values):
        return lax.all_gather(values, ("zl", "seq"), axis=0, tiled=True)

    def sum_tokens(values):
        return lax.psum_scatter(values.astype(BF), ("zl", "seq"), scatter_dimension=0, tiled=True).astype(F32)

    def sum_rows(values):
        return lax.psum_scatter(values.astype(BF), PEERS, scatter_dimension=0, tiled=True)

    def sum_columns(values, parts):
        part = sum_rows(values).reshape(team, own, -1)
        part = lax.all_to_all(part, TEAM, split_axis=0, concat_axis=0, tiled=True)
        return join_columns(part, parts).astype(F32)

    small = jnp.concatenate([norm1_gain, norm1_bias, norm2_gain, norm2_bias, qkv_bias])
    small = lax.all_gather(small, ALL, axis=0, tiled=False)
    first_gain = small[:, :own].reshape(-1).astype(F32)
    first_bias = small[:, own : 2 * own].reshape(-1).astype(F32)
    second_gain = small[:, 2 * own : 3 * own].reshape(-1).astype(F32)
    second_bias = small[:, 3 * own : 4 * own].reshape(-1).astype(F32)
    qkv_offset = mine_columns(small[:, 4 * own :].reshape(-1), 3).astype(F32)

    inputs = tokens[0].astype(F32)
    first_normed, first_scale = norm_rows(inputs)
    first_own = to_owner_order((first_normed * first_gain + first_bias).astype(BF))
    first_input = gather_tokens(first_own)
    qkv_matrix = gather_columns(qkv_weight, 3)
    out_matrix = gather_rows(out_weight)
    gate_matrix = gather_columns(gate_weight, 1)
    up_matrix = gather_columns(up_weight, 1)
    down_matrix = gather_rows(down_weight)
    upstream = gather_tokens(cotangent[0])

    projected = dot(first_input, qkv_matrix) + qkv_offset
    part = width // team
    group_heads = part // HEAD_DIM
    positions = jnp.tile(jnp.arange(length, dtype=jnp.int32), seqs)

    def heads_of(values):
        return values.reshape(seqs, length, group_heads, HEAD_DIM).transpose(0, 2, 1, 3)

    def unheads(values):
        return values.transpose(0, 2, 1, 3).reshape(seqs * length, part)

    queries = heads_of(rotate(projected[:, :part].reshape(-1, group_heads, HEAD_DIM), positions, 1.0).astype(BF))
    keys = heads_of(rotate(projected[:, part : 2 * part].reshape(-1, group_heads, HEAD_DIM), positions, 1.0).astype(BF))
    values = heads_of(projected[:, 2 * part :].astype(BF))
    causal = jnp.arange(length)[:, None] >= jnp.arange(length)[None, :]
    scores = jnp.einsum("shqd,shkd->shqk", queries, keys, preferred_element_type=F32) * 0.125
    scores = jnp.where(causal, scores, -1e30)
    highest = jnp.max(scores, axis=-1, keepdims=True)
    exponent = jnp.exp(scores - highest)
    probs = exponent / jnp.sum(exponent, axis=-1, keepdims=True)
    probs_low = probs.astype(BF)
    mixed = unheads(jnp.einsum("shqk,shkd->shqd", probs_low, values, preferred_element_type=F32).astype(BF))
    middle = inputs + sum_tokens(dot(mixed, out_matrix))

    second_normed, second_scale = norm_rows(middle)
    second_own = to_owner_order((second_normed * second_gain + second_bias).astype(BF))
    second_input = gather_tokens(second_own)
    gate_rows = dot(second_input, gate_matrix)
    up_rows = dot(second_input, up_matrix)
    sigmoid_gate = jax.nn.sigmoid(gate_rows)
    silu_gate = gate_rows * sigmoid_gate
    hidden = (silu_gate * up_rows).astype(BF)
    result = middle + sum_tokens(dot(hidden, down_matrix))

    down_total = sum_rows(dot_tn(hidden, upstream)).astype(F32)
    grad_hidden = dot_nt(upstream, down_matrix)
    grad_gate = (grad_hidden * up_rows * sigmoid_gate * (1.0 + gate_rows * (1.0 - sigmoid_gate))).astype(BF)
    grad_up = (grad_hidden * silu_gate).astype(BF)
    gate_total = sum_columns(dot_tn(second_input, grad_gate), 1)
    up_total = sum_columns(dot_tn(second_input, grad_up), 1)
    grad_second = from_owner_order(sum_tokens(dot_nt(grad_gate, gate_matrix) + dot_nt(grad_up, up_matrix)))
    grad_middle = cotangent[0].astype(F32) + norm_back(grad_second * second_gain, second_normed, second_scale)
    grad_attended = gather_tokens(grad_middle.astype(BF))
    out_total = sum_rows(dot_tn(mixed, grad_attended)).astype(F32)
    grad_mixed = heads_of(dot_nt(grad_attended, out_matrix).astype(BF))
    grad_probs = jnp.einsum("shqd,shkd->shqk", grad_mixed, values, preferred_element_type=F32)
    grad_scores = (probs * (grad_probs - jnp.sum(probs * grad_probs, axis=-1, keepdims=True))).astype(BF)
    grad_queries = (jnp.einsum("shqk,shkd->shqd", grad_scores, keys, preferred_element_type=F32) * 0.125).astype(BF)
    grad_keys = (jnp.einsum("shqk,shqd->shkd", grad_scores, queries, preferred_element_type=F32) * 0.125).astype(BF)
    grad_values = jnp.einsum("shqk,shqd->shkd", probs_low, grad_mixed, preferred_element_type=F32).astype(BF)
    grad_queries = rotate(unheads(grad_queries).astype(F32).reshape(-1, group_heads, HEAD_DIM), positions, -1.0)
    grad_keys = rotate(unheads(grad_keys).astype(F32).reshape(-1, group_heads, HEAD_DIM), positions, -1.0)
    grad_projected = jnp.concatenate(
        [grad_queries.reshape(-1, part).astype(BF), grad_keys.reshape(-1, part).astype(BF), unheads(grad_values)],
        axis=1,
    )
    qkv_total = sum_columns(dot_tn(first_input, grad_projected), 3)
    grad_first = from_owner_order(sum_tokens(dot_nt(grad_projected, qkv_matrix)))
    grad_inputs = grad_middle + norm_back(grad_first * first_gain, first_normed, first_scale)

    bias_part = jnp.sum(grad_projected.astype(F32), axis=0).reshape(3, zh, -1)
    bias_whole = jnp.zeros((3, half, zh, seqs, bias_part.shape[2]), F32)
    bias_whole = lax.dynamic_update_slice(
        bias_whole, bias_part[:, None, :, None], (0, lax.axis_index("seq"), 0, lax.axis_index("zl"), 0)
    ).reshape(-1)
    count = width // own
    sums = jnp.concatenate(
        [
            jnp.sum(grad_first * first_normed, axis=0).reshape(count, own),
            jnp.sum(grad_first, axis=0).reshape(count, own),
            jnp.sum(grad_second * second_normed, axis=0).reshape(count, own),
            jnp.sum(grad_second, axis=0).reshape(count, own),
            bias_whole.reshape(count, 3 * own),
        ],
        axis=1,
    )
    sums = lax.psum_scatter(sums, ALL, scatter_dimension=0, tiled=True)[0]
    return (
        result.astype(BF)[None],
        grad_inputs[None],
        sums[:own],
        sums[own : 2 * own],
        qkv_total,
        sums[4 * own :],
        out_total,
        sums[2 * own : 3 * own],
        sums[3 * own : 4 * own],
        gate_total,
        up_total,
        down_total,
    )


MESH = pl.DeviceIdType.MESH
ROWS = 16
QKV_PARTS, QKV_GATHERS, OUT_PARTS, FF_PARTS, DOWN_PARTS = 2, 3, 2, 2, 4


class Place:
    def __init__(self, zhs):
        self.s, self.zh, self.zl, self.y, self.c = (lax.axis_index(axis) for axis in ALL)
        self.zhs = zhs

    def at(self, **changed):
        return tuple(changed.get(name, getattr(self, name)) for name in ("s", "zh", "zl", "y", "c"))

    def mates(self):
        for flip_s, flip_z in ((0, 1), (1, 0), (1, 1)):
            yield (1 - self.s if flip_s else self.s), (1 - self.zl if flip_z else self.zl)

    def highs(self):
        for step in range(1, self.zhs):
            yield (self.zh + step) % self.zhs

    def greet(self, corners=False):
        partners = [self.at(s=s, zl=zl) for s, zl in self.mates()]
        partners += [self.at(zh=zh) for zh in self.highs()]
        partners += [self.at(y=1 - self.y), self.at(c=1 - self.c)]
        if corners:
            partners += [self.at(zh=zh, y=1 - self.y) for zh in self.highs()]
        barrier = pltpu.get_barrier_semaphore()
        for partner in partners:
            pl.semaphore_signal(barrier, inc=1, device_id=partner, device_id_type=MESH)
        pl.semaphore_wait(barrier, len(partners))


class Traffic:
    def __init__(self):
        self.now, self.active = 0.0, []

    def start(self, demands):
        transfer = {"left": {link: time for link, time in demands.items()}, "done": None}
        self.active.append(transfer)
        return transfer

    def backlog(self, link):
        return sum(transfer["left"].get(link, 0.0) for transfer in self.active)

    def advance(self, until):
        while self.now < until:
            shares = {}
            for transfer in self.active:
                for link in transfer["left"]:
                    shares[link] = shares.get(link, 0) + 1
            step = until - self.now
            for transfer in self.active:
                for link, left in transfer["left"].items():
                    step = min(step, left * shares[link])
            self.now += step
            for transfer in list(self.active):
                transfer["left"] = {
                    link: left - step / shares[link]
                    for link, left in transfer["left"].items()
                    if left - step / shares[link] > 1e-6
                }
                if not transfer["left"]:
                    transfer["done"] = self.now + LATENCY
                    self.active.remove(transfer)


LATENCY = 2.0
ENTER_PLAN = {"small": (7.8, 43), "qkv0": (4.9, 33), "qkv1": (10.8, 0), "qkv2": (6.1, 1), "qkv3": (10.6, 19), "qkv4": (3.8, 13), "qkv5": (11.5, 41), "out0": (2.2, 0), "out1": (2.6, 32), "tokens": (5.8, 13), "cut": (2.3, 40), "backlog": 12}
MIDDLE_PLAN = {"tokens": (0, 0), "ff0": (1, 0), "ff1": (3, 0), "ff2": (4, 0), "ff3": (5, 0), "ff4": (6, 0), "ff5": (7, 0), "ff6": (8, 0), "ff7": (9, 0), "down0": (2, 0), "down1": (10, 0), "down2": (11, 0), "down3": (12, 0), "upstream": (13, 8)}
FEED_PLAN = {"work": (4.9, 0), "down0": (5.9, 0), "down1": (1, 0), "down2": (2.3, 35), "down3": (4.1, 43), "result": (1.3, 0)}
BACK_PLAN = {"tokens": (16.9, 0), "weights": (17.1, 0), "down0": (12.9, 0), "down1": (7.6, 0), "down2": (12.3, 11), "down3": (0.2, 34), "ff0": (14.7, 49), "ff1": (12.6, 10), "ff2": (12.3, 29), "ff3": (3.9, 0), "ff4": (16, 0), "ff5": (6, 0), "ff6": (10.6, 61), "ff7": (9.2, 2), "out0": (6.2, 0), "out1": (16.3, 40), "join": (17.7, 21)}
LEAVE_PLAN = {"weights": (4, 0), "tokens": (1.5, 0), "qkv0": (0.8, 24), "qkv2": (0.1, 0), "qkv1": (0.1, 33), "qkv3": (3.9, 19), "backlog": 7}
BACKLOG = 12.0
LINK_TIME = {
    "s": {"s": 2 / 92e3},
    "zl": {"zl": 2 / 92e3},
    "y": {"y": 2 / 92e3},
    "zh": {"zh": 4 / 92e3, "zl": 2 / 92e3},
    "c": {"c": 1 / 300e3},
    "diagonal": {"s": 2 / 92e3, "zl": 2 / 92e3},
    "local": {"local": 1 / 1500e3},
}


class Lines:
    def __init__(self, send, recv, local):
        self.send, self.recv, self.local = send, recv, local
        self.sent, self.copied, self.traffic = [], 0, Traffic()

    def track(self, wait, source, link):
        size = int(np.prod(source.shape)) * jnp.dtype(source.dtype).itemsize
        return wait, self.traffic.start({name: time * size for name, time in LINK_TIME[link].items()})

    def push(self, source, target, device, link):
        at = len(self.sent)
        copy = pltpu.make_async_remote_copy(
            src_ref=source, dst_ref=target, send_sem=self.send.at[at], recv_sem=self.recv.at[at],
            device_id=device, device_id_type=MESH,
        )
        copy.start()
        self.sent.append(copy)
        return self.track(copy.wait_recv, source, link)

    def copy(self, source, target):
        copy = pltpu.make_async_copy(source, target, self.local.at[self.copied])
        copy.start()
        self.copied += 1
        return self.track(copy.wait, source, "local")

    def finish(self):
        for copy in self.sent:
            copy.wait_send()


def run(lines, works, plan, start=3.0):
    traffic, now = lines.traffic, start
    open_works, late, plan = [], None, dict(plan)
    limit = plan.get("backlog", BACKLOG)

    def add(label, work):
        rank, begin = plan.get(label, (0.0, 0.0))
        open_works.append([rank, begin, work, next(work)])
        open_works.sort(key=lambda entry: entry[0])

    for work in works:
        if isinstance(work, list):
            late = work
        else:
            add(*work)
    while open_works:
        traffic.advance(now)
        for entry in open_works:
            waits, cost, link = entry[3]
            arrived = all(transfer["done"] is not None and transfer["done"] <= now for _, transfer in waits)
            if arrived and now >= entry[1] and (link is None or traffic.backlog(link) < limit):
                break
        else:
            now += 0.25
            continue
        for wait, _ in waits:
            wait()
        entry[1], entry[3] = 0.0, next(entry[2], None)
        now += cost + 0.15
        if entry[3] is None:
            open_works.remove(entry)
        while late:
            add(*late.pop(0))


def gather_team(lines, me, source, whole):
    yield [], 0, None
    mine, other = whole.at[me.zl, me.s], whole.at[1 - me.zl, me.s]
    across = lines.push(source, mine, me.at(zl=1 - me.zl), "zl")
    waits = [lines.copy(source, mine), lines.push(source, mine, me.at(s=1 - me.s), "s")]
    yield [across], 0, None
    waits.append(lines.push(other, other, me.at(s=1 - me.s), "s"))
    yield waits, 0, None


def gather_columns(lines, me, cut, whole, piece):
    other, start, size = piece
    s, columns = 1 - me.s if other else me.s, pl.ds(start, size)
    yield [], 0, "s"
    waits = []
    for flip in (0, 1):
        zl = 1 - me.zl if flip else me.zl
        for source, at in cut(s, zl, start, size):
            mine = whole.at[me.s, me.zh, me.zl, me.y, me.c, :, pl.ds(at, source.shape[1])]
            if other or flip:
                link = "diagonal" if other and flip else "s" if other else "zl"
                waits.append(lines.push(source, mine, me.at(s=s, zl=zl), link))
            else:
                waits.append(lines.copy(source, mine))
    yield waits, 0, "zh"
    part = whole.at[s, me.zh, :, me.y, me.c, :, columns]
    waits = [lines.push(part, part, me.at(zh=zh), "zh") for zh in me.highs()]
    yield waits, 0, "y"
    part = whole.at[s, :, :, me.y, me.c, :, columns]
    wait = lines.push(part, part, me.at(y=1 - me.y), "y")
    yield [wait], 0, None
    part = whole.at[s, :, :, :, me.c, :, columns]
    wait = lines.push(part, part, me.at(c=1 - me.c), "c")
    yield [wait], 0, None


def ready_cut(cut):
    return lambda s, zl, start, size: [(cut.at[s * 2 + zl, :, pl.ds(start, size)], start)]


def block_cut(zhs, shard, block):
    def cut(s, zl, start, size):
        found = []
        for at in range(start, start + size, block):
            number, zh = at // (zhs * block), at // block % zhs
            column = (number * 4 * zhs + (s * zhs + zh) * 2 + zl) * block
            found.append((shard.at[:, pl.ds(pl.multiple_of(column, block), block)], at))
        return found

    return cut


def swap_halves(left, right):
    width = left.shape[1]
    first = lax.broadcasted_iota(jnp.int32, (1, width), 1) < width // 2
    return (
        jnp.where(first, left, pltpu.roll(right, width // 2, 1)),
        jnp.where(first, pltpu.roll(left, width // 2, 1), right),
    )


def gather_rows(lines, me, source, whole, start, size):
    rows = pl.ds(start, size)
    yield [], 0, "zh"
    mine = whole.at[me.zh, me.y, me.c, rows]
    waits = [lines.copy(source.at[rows], mine)]
    waits += [lines.push(source.at[rows], mine, me.at(zh=zh), "zh") for zh in me.highs()]
    yield waits, 0, "y"
    part = whole.at[:, me.y, me.c, rows]
    wait = lines.push(part, part, me.at(y=1 - me.y), "y")
    yield [wait], 0, None
    part = whole.at[:, :, me.c, rows]
    wait = lines.push(part, part, me.at(c=1 - me.c), "c")
    yield [wait], 0, None


def add_into(target, sources, result=None):
    result = target if result is None else result

    size = 2 * ROWS if target.shape[0] % (2 * ROWS) == 0 else ROWS

    def step(at, carry):
        rows = pl.ds(pl.multiple_of(at * size, size), size)
        total = target[rows].astype(F32)
        for source in sources:
            total = total + source[rows].astype(F32)
        result[rows] = total.astype(result.dtype)
        return carry

    lax.fori_loop(0, target.shape[0] // size, step, 0)


def add_time(*refs):
    return sum(int(np.prod(ref.shape)) for ref in refs) * ADD_TIME


ADD_TIME = 1.6e-6


def sum_columns(lines, me, grad, cut, buffers, piece):
    first, second, third = buffers
    other, start, size = piece
    s, columns = 1 - me.s if other else me.s, pl.ds(start, size)
    mine = grad.at[s, :, :, :, me.c, :, columns]
    yield [], 0, "c"
    wait = lines.push(grad.at[s, :, :, :, 1 - me.c, :, columns], first, me.at(c=1 - me.c), "c")
    yield [wait], add_time(first) / 2, "y"

    def fold(y):
        for zh in range(me.zhs):
            for zl in range(2):
                add_into(mine.at[zh, zl, y], [first.at[zh, zl, y]])

    fold(1 - me.y)
    wait = lines.push(mine.at[:, :, 1 - me.y], second, me.at(y=1 - me.y), "y")
    yield [], add_time(first) / 2, None
    fold(me.y)
    yield [wait], add_time(second), "zh"
    waits = []
    for step, zh in enumerate([*me.highs(), me.zh]):
        for zl in range(2):
            add_into(mine.at[zh, zl, me.y], [second.at[zh, zl]])
        if step < me.zhs - 1:
            waits.append(lines.push(mine.at[zh, :, me.y], third.at[step], me.at(zh=zh), "zh"))
    yield waits, add_time(third), None
    for zl in range(2):
        add_into(mine.at[me.zh, zl, me.y], [third.at[step, zl] for step in range(me.zhs - 1)])
    waits = []
    for flip in (0, 1):
        zl = 1 - me.zl if flip else me.zl
        source, target = mine.at[me.zh, zl, me.y], cut.at[me.s * 2 + me.zl, :, columns]
        if other or flip:
            link = "diagonal" if other and flip else "s" if other else "zl"
            waits.append(lines.push(source, target, me.at(s=s, zl=zl), link))
        else:
            waits.append(lines.copy(source, target))
    yield waits, 0, None


def sum_near(lines, me, grad, buffers, piece):
    first, second = buffers
    rows = pl.ds(*piece)
    mine = grad.at[:, :, me.c, rows]
    yield [], 0, "c"
    wait = lines.push(grad.at[:, :, 1 - me.c, rows], first, me.at(c=1 - me.c), "c")
    yield [wait], add_time(first) / 2, "y"
    for zh in range(me.zhs):
        add_into(mine.at[zh, 1 - me.y], [first.at[zh, 1 - me.y]])
    wait = lines.push(mine.at[:, 1 - me.y], second, me.at(y=1 - me.y), "y")
    yield [], add_time(first) / 2, None
    for zh in range(me.zhs):
        add_into(mine.at[zh, me.y], [first.at[zh, me.y]])
    yield [wait], add_time(second), None
    for zh in range(me.zhs):
        add_into(mine.at[zh, me.y], [second.at[zh]])


def sum_far(lines, me, part, total, buffers, piece):
    mine, third, final = buffers
    rows = pl.ds(*piece)
    yield [], 0, "zh"
    waits = [lines.copy(part.at[me.zh, rows], mine)]
    for step, zh in enumerate(me.highs()):
        waits.append(lines.push(part.at[zh, rows], third.at[step], me.at(zh=zh), "zh"))
    yield waits, add_time(third), None
    add_into(mine, [third.at[step] for step in range(me.zhs - 1)], final)
    wait = lines.copy(final, total.at[rows])
    yield [wait], 0, None


def sum_rows(lines, me, grad, total, near, far, piece):
    yield from sum_near(lines, me, grad, near, piece)
    yield from sum_far(lines, me, grad.at[:, me.y, me.c], total, far, piece)


def sum_team(lines, me, partial, own, passed, taken):
    load = lines.copy(partial.at[1 - me.zl, me.s], passed)
    first = send_rows(lines, me, partial, taken, 1 - me.zl)
    yield [load, first], add_time(passed), None
    waits = [lines.copy(partial.at[me.zl, me.s], own), send_rows(lines, me, partial, taken, me.zl)]
    add_into(passed, [taken.at[1 - me.zl]])
    waits.append(lines.push(passed, taken.at[2], me.at(zl=1 - me.zl), "zl"))
    yield waits, 3, None


def send_rows(lines, me, partial, taken, zl):
    return lines.push(partial.at[zl, 1 - me.s], taken.at[zl], me.at(s=1 - me.s), "s")


def end_team(lines, me, partial, own, passed, taken, started):
    load = lines.copy(partial.at[1 - me.zl, me.s], passed)
    keep = lines.copy(partial.at[me.zl, me.s], own)
    yield [load, *started], add_time(passed), None
    add_into(passed, [taken.at[1 - me.zl]])
    wait = lines.push(passed, taken.at[2], me.at(zl=1 - me.zl), "zl")
    yield [keep, wait], 3, None


def team_total(me, own, taken, rows):
    return own[rows].astype(F32) + taken[me.zl, rows].astype(F32) + taken[2, rows].astype(F32)


def by_rows(count, body):
    def step(at, carry):
        body(pl.ds(pl.multiple_of(at * ROWS, ROWS), ROWS))
        return carry

    lax.fori_loop(0, count // ROWS, step, 0)


def row_pieces(size, parts):
    tiles, pieces, start = size // ROWS, [], 0
    for part in range(parts):
        count = (tiles * (part + 1) // parts - tiles * part // parts) * ROWS
        pieces.append((start, count))
        start += count
    return pieces


def column_pieces(columns, parts):
    lanes, pieces, start = columns // 128, [], 0
    for part in range(parts):
        size = (lanes * (part + 1) // parts - lanes * part // parts) * 128
        pieces.append((start, size))
        start += size
    return [(other, *piece) for other in (False, True) for piece in pieces]


def turn_pairs(values, tables, sign):
    return (
        values * tables[0]
        + pltpu.roll(values, 128 - ROTARY // 2, 1) * (tables[1] * sign)
        + pltpu.roll(values, ROTARY // 2, 1) * (tables[2] * sign)
    )


def rotary_tables(length):
    lane = np.arange(128) % HEAD_DIM
    halves = ROTARY // 2
    frequency = np.float32(10000.0) ** (np.float32(-2.0) * np.arange(halves, dtype=np.float32) / np.float32(ROTARY))
    angles = np.arange(length, dtype=np.float32)[:, None] * frequency[lane % halves][None, :]
    rotated = lane < ROTARY
    return np.stack([
        np.where(rotated, np.cos(angles), 1.0),
        np.where(lane < halves, -np.sin(angles), 0.0),
        np.where(rotated & (lane >= halves), np.sin(angles), 0.0),
    ]).astype(np.float32)


def lane_masks():
    lane = lax.broadcasted_iota(jnp.int32, (1, 128), 1)
    return [(lane < HEAD_DIM).astype(F32).astype(BF), (lane >= HEAD_DIM).astype(F32).astype(BF)], lane < HEAD_DIM


def softmax_rows(query, key):
    length = query.shape[0]
    scores = dot_nt(query, key) * 0.125
    below = lax.broadcasted_iota(jnp.int32, (length, length), 0) >= lax.broadcasted_iota(
        jnp.int32, (length, length), 1
    )
    scores = jnp.where(below, scores, -1e30)
    exponent = jnp.exp(scores - jnp.max(scores, axis=-1, keepdims=True))
    return exponent / jnp.sum(exponent, axis=-1, keepdims=True)


def pairs_of(seq, length, part, body):
    def step(at, carry):
        body(pl.ds(seq * length, length), pl.ds(pl.multiple_of(at * 128, 128), 128))
        return carry

    lax.fori_loop(0, part // 128, step, 0)


def forward_attention(first, weight, offset, tables, queries, keys, values, mixed, leave):
    length, part = tables.shape[1], queries.shape[1]
    seqs = queries.shape[0] // length
    for number, target in enumerate((queries, keys, values)):
        for start in range(0, part, 256):
            at = number * part + start
            block = dot(first[...], weight[:, at : at + 256]) + offset[:, at : at + 256]
            if target is values:
                target[:, start : start + 256] = block.astype(BF)
                continue
            for seq in range(seqs):
                for lanes in range(0, 256, 128):
                    rows = slice(seq * length, (seq + 1) * length)
                    turned = turn_pairs(block[rows, lanes : lanes + 128], tables, 1.0)
                    target[rows, start + lanes : start + lanes + 128] = turned.astype(BF)
        yield [], 2.5 if number < 2 else 7, None

    masks, left = lane_masks()
    for seq in range(seqs):

        def body(rows, lanes):
            query, key, value = queries[rows, lanes], keys[rows, lanes], values[rows, lanes]
            sides = [dot(softmax_rows(query * mask, key).astype(BF), value) for mask in masks]
            mixed[rows, lanes] = jnp.where(left, *sides).astype(BF)

        pairs_of(seq, length, part, body)
        leave(seq)
        if seq < seqs - 1:
            yield [], 7, None


def backward_attention(grad_mixed, tables, queries, keys, values, grad_projected):
    length, part = tables.shape[1], queries.shape[1]
    seqs = queries.shape[0] // length
    masks, left = lane_masks()
    for seq in range(seqs):

        def body(rows, lanes):
            query, key, value = queries[rows, lanes], keys[rows, lanes], values[rows, lanes]
            grad = grad_mixed[rows, lanes]
            sides = []
            for mask in masks:
                probs = softmax_rows(query * mask, key)
                grad_probs = dot_nt(grad * mask, value)
                grad_scores = (
                    probs * (grad_probs - jnp.sum(probs * grad_probs, axis=-1, keepdims=True))
                ).astype(BF)
                sides.append((
                    dot(grad_scores, key) * 0.125,
                    dot_tn(grad_scores, query) * 0.125,
                    dot_tn(probs.astype(BF), grad),
                ))
            grads = [jnp.where(left, *pair).astype(BF) for pair in zip(*sides)]
            start = lanes.start
            for number, found in enumerate(grads):
                if number < 2:
                    found = turn_pairs(found.astype(F32), tables, -1.0).astype(BF)
                grad_projected[rows, pl.ds(pl.multiple_of(start + number * part, 128), 128)] = found

        pairs_of(seq, length, part, body)
        yield [], 9 if seq < seqs - 1 else 1, None


def enter_kernel(
    zhs, tokens, small, qkv, out, gate, up,
    tokens_all, small_all, qkv_all, out_all, gate_cut, up_cut, shard, cuts, send, recv, local,
):
    me, lines = Place(zhs), Lines(send, recv, local)
    loads = [lines.copy(gate, shard.at[0]), lines.copy(up, shard.at[1])]
    me.greet()
    block = qkv_all.shape[6] // 3 // zhs

    def cut_work():
        width = cuts.shape[3]
        kept = []
        for number, target in enumerate((gate_cut, up_cut)):
            yield loads if number == 0 else [], 2, None
            for s in range(2):
                at = 2 * s * width
                left = shard[number, :, at : at + width].astype(F32)
                right = shard[number, :, at + width : at + 2 * width].astype(F32)
                for zl, found in enumerate(swap_halves(left, right)):
                    cuts[number, s * 2 + zl] = found.astype(BF)
            kept.append(lines.copy(cuts.at[number], target))
        yield kept, 0, None

    run(lines, [
        *[("small", gather_columns(lines, me, lambda *_: [(small, 0)], small_all, (other, 0, 128))) for other in (False, True)],
        *[
            (f"qkv{at}", gather_columns(lines, me, block_cut(zhs, qkv, block), qkv_all, piece))
            for at, piece in enumerate(column_pieces(qkv_all.shape[6], QKV_GATHERS))
        ],
        *[
            (f"out{at}", gather_rows(lines, me, out, out_all, *piece))
            for at, piece in enumerate(row_pieces(out.shape[0], OUT_PARTS))
        ],
        ("tokens", gather_team(lines, me, tokens, tokens_all)),
        ("cut", cut_work()),
    ], ENTER_PLAN)
    lines.finish()


def middle_kernel(
    zhs, tokens, upstream, tokens_all, qkv_all, out_all, gate_cut, up_cut, down,
    norms, offset, tables,
    middle, first_out, queries_out, keys_out, values_out, mixed_out,
    upstream_all, input_all, gate_all, up_all, down_all,
    whole, first, weight, out_weight, queries, keys, values, mixed, partial,
    own, passed, taken, second, send, recv, local,
):
    me, lines = Place(zhs), Lines(send, recv, local)
    first_gain, first_bias, gain, bias = (norms.at[row : row + 1] for row in range(4))
    loads = [lines.copy(tokens_all, whole), lines.copy(qkv_all, weight), lines.copy(out_all, out_weight)]
    me.greet()

    def tokens_work():
        yield loads[:1], 4, None

        def normed(rows):
            first[rows] = (norm_rows(whole[rows].astype(F32))[0] * first_gain[...] + first_bias[...]).astype(BF)

        by_rows(whole.shape[0], normed)
        yield loads[1:], 2.5, None
        started = []

        def leave(seq):
            rows = slice(seq * tables.shape[1], (seq + 1) * tables.shape[1])
            for start in range(0, partial.shape[3], 512):
                block = dot(mixed[rows], out_weight[:, start : start + 512]).astype(BF)
                partial[seq, :, :, start : start + 512] = block.reshape(partial.shape[1:3] + (512,))
            started.append(send_rows(lines, me, partial, taken, seq))

        yield from forward_attention(first, weight, offset, tables, queries, keys, values, mixed, leave)
        yield from end_team(lines, me, partial, own, passed, taken, started)

        def body(rows):
            values = tokens[rows].astype(F32) + team_total(me, own, taken, rows)
            middle[rows] = values
            second[rows] = (norm_rows(values)[0] * gain[...] + bias[...]).astype(BF)

        by_rows(middle.shape[0], body)
        kept = [
            lines.copy(source, target)
            for source, target in (
                (first, first_out), (queries, queries_out), (keys, keys_out), (values, values_out), (mixed, mixed_out),
            )
        ]
        yield from gather_team(lines, me, second, input_all)
        yield kept, 0, None

    rows = [gather_rows(lines, me, down, down_all, *piece) for piece in row_pieces(down.shape[0], DOWN_PARTS)]
    columns = [
        gather_columns(lines, me, ready_cut(cut), found, piece)
        for piece in column_pieces(gate_cut.shape[2], FF_PARTS)
        for cut, found in ((gate_cut, gate_all), (up_cut, up_all))
    ]
    run(lines, [
        ("tokens", tokens_work()),
        *[(f"ff{at}", work) for at, work in enumerate(columns)],
        *[(f"down{at}", work) for at, work in enumerate(rows)],
        ("upstream", gather_team(lines, me, upstream, upstream_all)),
    ], MIDDLE_PLAN)
    lines.finish()


def feed_kernel(
    zhs, middle, input_all, upstream_all, gate_all, up_all, down_all,
    result, partial_second_out, grad_gate_out, grad_up_out, down_part,
    second, upstream, gate_weight, up_weight, down_weight, gate, up, hidden, grad_gate, grad_up,
    partial_down, partial_second, grad_down, own, passed, taken, buffers, send, recv, local,
):
    me, lines = Place(zhs), Lines(send, recv, local)
    loads = [
        lines.copy(source, target)
        for source, target in (
            (input_all, second), (gate_all, gate_weight), (up_all, up_weight),
            (upstream_all, upstream), (down_all, down_weight),
        )
    ]
    me.greet()
    spawned, pieces = [], row_pieces(grad_down.shape[3], DOWN_PARTS)
    width, ff = gate_weight.shape
    tiles = [(start, min(256, ff - start)) for start in range(0, ff, 256)]

    def sums(piece, near):
        yield from sum_near(lines, me, grad_down, near, piece)
        rows = pl.ds(*piece)
        wait = lines.copy(grad_down.at[:, me.y, me.c, rows], down_part.at[:, rows])
        yield [wait], 0, None

    def work():
        yield loads[:3], 9, None
        for start, size in tiles:
            at = slice(start, start + size)
            gate_rows = dot(second[...], gate_weight[:, at])
            up_rows = dot(second[...], up_weight[:, at])
            gate[:, at], up[:, at] = gate_rows, up_rows
            hidden[:, at] = (gate_rows * jax.nn.sigmoid(gate_rows) * up_rows).astype(BF)
        yield loads[3:], 4.5, None
        for start in range(0, width, 512):
            block = dot_tn(hidden[...], upstream[:, start : start + 512]).astype(BF)
            grad_down[:, :, :, :, start : start + 512] = block.reshape(grad_down.shape[:4] + (512,))
        spawned.extend((f"down{at}", sums(piece, near)) for at, (piece, near) in enumerate(zip(pieces, buffers)))
        yield [], 4.5, None
        for start in range(0, width, 512):
            block = dot(hidden[...], down_weight[:, start : start + 512]).astype(BF)
            partial_down[:, :, :, start : start + 512] = block.reshape(partial_down.shape[:3] + (512,))
        spawned.append(("result", result_work()))
        yield [], 5, None
        for start, size in tiles:
            at = slice(start, start + size)
            grad_hidden = dot_nt(upstream[...], down_weight[at])
            gate_rows = gate[:, at]
            sigmoid_gate = jax.nn.sigmoid(gate_rows)
            grad_gate[:, at] = (
                grad_hidden * up[:, at] * sigmoid_gate * (1.0 + gate_rows * (1.0 - sigmoid_gate))
            ).astype(BF)
            grad_up[:, at] = (grad_hidden * gate_rows * sigmoid_gate).astype(BF)
        waits = [lines.copy(grad_gate, grad_gate_out), lines.copy(grad_up, grad_up_out)]
        for start in range(0, width, 512):
            yield [], 2.5, None
            block = dot_nt(grad_gate[...], gate_weight[start : start + 512]) + dot_nt(
                grad_up[...], up_weight[start : start + 512]
            )
            partial_second[:, start : start + 512] = block.astype(BF)
        waits.append(lines.copy(partial_second, partial_second_out))
        yield waits, 0, None

    def result_work():
        yield from sum_team(lines, me, partial_down, own, passed, taken)

        def body(rows):
            result[rows] = (middle[rows] + team_total(me, own, taken, rows)).astype(BF)

        by_rows(middle.shape[0], body)

    run(lines, [("work", work()), spawned], FEED_PLAN)
    lines.finish()


def back_kernel(
    zhs, middle, upstream, norms, partial_second, down_part, input_all, gate_in, up_in,
    out_all, queries_in, keys_in, values_in, mixed_in, tables,
    grad_middle, sums, down_total, gate_total, up_total, out_total, projected_out, bias_sums,
    own_second, passed_second, taken_second, attended,
    attended_all, out_weight, queries, keys, values, mixed, grad_mixed, grad_projected, grad_out,
    second, grad_side, grad_gate, grad_up, cuts, joined, down_buffers, out_buffers, buffers, send, recv, local,
):
    me, lines = Place(zhs), Lines(send, recv, local)
    gain = norms.at[2:3]
    near_loads = [lines.copy(input_all, second), lines.copy(gate_in, grad_side)]
    loads = [
        lines.copy(source, target)
        for source, target in (
            (out_all, out_weight), (queries_in, queries), (keys_in, keys), (values_in, values), (mixed_in, mixed),
        )
    ]
    me.greet()
    spawned = []
    pieces = column_pieces(cuts.shape[3], FF_PARTS)

    def weights_work():
        number = 0
        for which, (grad, total) in enumerate(((grad_gate, gate_total), (grad_up, up_total))):
            yield near_loads if grad is grad_gate else [lines.copy(up_in, grad_side)], 4.5, None
            ff = grad_side.shape[1]
            for start in range(0, ff, 256):
                size = min(256, ff - start)
                block = dot_tn(second[...], grad_side[:, start : start + size]).astype(BF)
                grad[:, :, :, :, :, :, start : start + size] = block.reshape(grad.shape[:6] + (size,))
            left = list(pieces)
            for piece in pieces:
                work = piece_work(grad, which, total, buffers[number], piece, left)
                spawned.append((f"ff{number}", work))
                number += 1

    def piece_work(grad, which, total, found, piece, left):
        yield from sum_columns(lines, me, grad, cuts.at[which], found, piece)
        left.remove(piece)
        if not left:
            spawned.append(("join", join_work(which, total)))

    def join_work(which, total):
        yield [], 2, None
        width, kept = cuts.shape[3], []
        for s in range(2):
            sides = [cuts[which, s * 2 + zl].astype(F32) for zl in range(2)]
            for zh, found in enumerate(swap_halves(*sides)):
                joined[which, s * 2 + zh] = found
                at = (s * 2 + zh) * width
                kept.append(lines.copy(joined.at[which, s * 2 + zh], total.at[:, at : at + width]))
        yield kept, 0, None

    def tokens_work():
        yield [], 0, None
        yield from sum_team(lines, me, partial_second, own_second, passed_second, taken_second)
        sums[...] = jnp.zeros_like(sums)

        def body(rows):
            normed, scale_rows = norm_rows(middle[rows])
            grad = team_total(me, own_second, taken_second, rows)
            sums[0:1] += jnp.sum(grad * normed, axis=0, keepdims=True)
            sums[1:2] += jnp.sum(grad, axis=0, keepdims=True)
            grad = upstream[rows].astype(F32) + norm_back(grad * gain[...], normed, scale_rows)
            grad_middle[rows] = grad
            attended[rows] = grad.astype(BF)

        by_rows(middle.shape[0], body)
        yield from gather_team(lines, me, attended, attended_all)
        yield loads, 4, None
        count, width = mixed.shape[0], attended_all.shape[3]
        for start in range(0, width, 512):
            block = dot_tn(mixed[...], attended_all[:, :, :, start : start + 512].reshape(count, 512))
            grad_out[:, :, :, :, start : start + 512] = block.astype(BF).reshape(grad_out.shape[:4] + (512,))
        for at, piece in enumerate(row_pieces(out_total.shape[0], OUT_PARTS)):
            spawned.append((f"out{at}", sum_rows(lines, me, grad_out, out_total, *out_buffers[at], piece)))
        grad_mixed[...] = dot_nt(attended_all[...].reshape(count, width), out_weight[...]).astype(BF)
        yield [], 9, None
        yield from backward_attention(grad_mixed, tables, queries, keys, values, grad_projected)
        wait = lines.copy(grad_projected, projected_out)
        for start in range(0, grad_projected.shape[1], 256):
            block = jnp.sum(grad_projected[:, start : start + 256].astype(F32), axis=0, keepdims=True)
            bias_sums[:, start : start + 256] = block
        yield [wait], 0, None

    far = [
        sum_far(lines, me, down_part, down_total, found, piece)
        for found, piece in zip(down_buffers, row_pieces(down_total.shape[0], DOWN_PARTS))
    ]
    run(lines, [
        ("tokens", tokens_work()),
        ("weights", weights_work()),
        *[(f"down{at}", work) for at, work in enumerate(far)],
        spawned,
    ], BACK_PLAN)
    lines.finish()


def leave_kernel(
    zhs, tokens, grad_middle, norms, second_sums, bias_sums, grad_projected, first_in, qkv_in,
    grad_inputs, sums, qkv_total,
    first, weight, partial, grad_qkv, cut, own, passed, taken, steps, buffers, send, recv, local,
):
    me, lines = Place(zhs), Lines(send, recv, local)
    gain = norms.at[0:1]
    loads = [lines.copy(first_in, first), lines.copy(qkv_in, weight)]
    me.greet(corners=True)

    spawned = []
    pieces = column_pieces(cut.shape[2], QKV_PARTS)
    left = list(pieces)

    def piece_work(at):
        yield from sum_columns(lines, me, grad_qkv, cut, buffers[at], pieces[at])
        left.remove(pieces[at])
        if not left:
            block = cut.shape[2] // 3 // zhs
            for s in range(2):
                for zl in range(2):
                    for start in range(0, cut.shape[2], block):
                        number, zh = start // (zhs * block), start // block % zhs
                        column = (number * 4 * zhs + (s * zhs + zh) * 2 + zl) * block
                        found = cut[s * 2 + zl, :, start : start + block]
                        qkv_total[:, column : column + block] = found.astype(F32)

    def weights_work():
        for number in range(QKV_PARTS):
            yield loads[:1] if number == 0 else [], 2.6, None
            _, start, size = pieces[number]
            for at in range(start, start + size, 256):
                block = dot_tn(first[...], grad_projected[:, at : at + 256]).astype(BF)
                grad_qkv[:, :, :, :, :, :, at : at + 256] = block.reshape(grad_qkv.shape[:6] + (256,))
            for at in (number, number + QKV_PARTS):
                spawned.append((f"qkv{at}", piece_work(at)))

    def tokens_work():
        yield loads[1:], 5, None
        for at in range(weight.shape[0] // 256):
            block = dot_nt(grad_projected[...], weight[at * 256 : at * 256 + 256])
            partial[:, :, :, at * 256 : at * 256 + 256] = block.astype(BF).reshape(partial.shape[:3] + (256,))
        yield from sum_team(lines, me, partial, own, passed, taken)
        steps[0] = jnp.zeros_like(steps[0])
        steps[0, 2:4] = second_sums[0:2]
        part = bias_sums.shape[1] // 3
        block = part // zhs
        for number in range(3):
            for zh in range(zhs):
                at = ((me.s * zhs + zh) * 2 + me.zl) * block
                steps[0, 4 + number : 5 + number, pl.ds(pl.multiple_of(at, 64), block)] = bias_sums[
                    :, number * part + zh * block : number * part + (zh + 1) * block
                ]

        def body(rows):
            normed, scale_rows = norm_rows(tokens[rows].astype(F32))
            grad = team_total(me, own, taken, rows)
            steps[0, 0:1] += jnp.sum(grad * normed, axis=0, keepdims=True)
            steps[0, 1:2] += jnp.sum(grad, axis=0, keepdims=True)
            grad_inputs[rows] = grad_middle[rows] + norm_back(grad * gain[...], normed, scale_rows)

        by_rows(tokens.shape[0], body)
        others = [(zh, y) for y in (me.y, 1 - me.y) for zh in (me.zh, *me.highs())][1:]
        groups = [
            [(me.at(s=mate_s, zl=mate_zl), link) for (mate_s, mate_zl), link in zip(me.mates(), ("zl", "s", "diagonal"))],
            [(me.at(zh=zh, y=y), "zh" if y is me.y else "y") for zh, y in others],
            [(me.at(c=1 - me.c), "c")],
        ]
        at = 0
        for group in groups:
            arrived = [
                lines.push(steps.at[at], steps.at[at + 1 + number], device, link)
                for number, (device, link) in enumerate(group)
            ]
            yield arrived, 0.3, None
            total = steps[at]
            for number in range(len(group)):
                total = total + steps[at + 1 + number]
            at += len(group) + 1
            steps[at] = total
        sums[...] = steps[at]

    run(lines, [("weights", weights_work()), ("tokens", tokens_work()), spawned], LEAVE_PLAN)
    lines.finish()


def near_buffers(zhs, size, width):
    return tuple(pltpu.VMEM(shape + (size, width), BF) for shape in ((zhs, 2), (zhs,)))


def far_buffers(zhs, size, width):
    return (
        pltpu.VMEM((size, width), BF), pltpu.VMEM((zhs - 1, size, width), BF), pltpu.VMEM((size, width), F32)
    )


def column_buffers(zhs, own, columns):
    return tuple(
        pltpu.VMEM(shape + (own, columns), BF) for shape in ((zhs, 2, 2), (zhs, 2), (zhs - 1, 2))
    )


IN_HBM = pl.BlockSpec(memory_space=pl.ANY)
IN_VMEM = pl.BlockSpec(memory_space=pltpu.VMEM)


def call(kernel, zhs, number, inputs, outputs, scratch, copies, locals_, limit):
    return pl.pallas_call(
        lambda *refs: kernel(zhs, *refs),
        out_shape=[jax.ShapeDtypeStruct(shape, kind) for shape, kind, _ in outputs],
        in_specs=[spec for _, spec in inputs],
        out_specs=[spec for _, _, spec in outputs],
        scratch_shapes=[
            *scratch,
            pltpu.SemaphoreType.DMA((copies,)),
            pltpu.SemaphoreType.DMA((copies,)),
            pltpu.SemaphoreType.DMA((locals_,)),
        ],
        compiler_params=pltpu.CompilerParams(
            collective_id=number, has_side_effects=True, vmem_limit_bytes=limit << 20
        ),
    )(*[array for array, _ in inputs])


def per_device(
    tokens, cotangent, norm1_gain, norm1_bias, qkv_weight, qkv_bias, out_weight,
    norm2_gain, norm2_bias, gate_weight, up_weight, down_weight,
):
    zh = lax.axis_size("zh")
    rows = tokens.shape[1]
    width = tokens.shape[2]
    own = qkv_weight.shape[0]
    ff = gate_weight.shape[1]
    ff_own = down_weight.shape[0]
    half = lax.axis_size("seq")
    length = rows * half
    seqs = lax.axis_size("zl")
    team = half * seqs
    part = width // team
    ff_part = ff // team
    devices = width // own
    tokens, cotangent = tokens[0], cotangent[0]
    index = (lax.axis_index("seq") * (devices // half)
             + ((lax.axis_index("zh") * 2 + lax.axis_index("zl")) * 2 + lax.axis_index("y")) * 2
             + lax.axis_index("c"))

    def mine_columns(whole, parts):
        block = whole.shape[0] // parts // (half * zh * seqs)
        cut = whole.reshape(parts, half, zh, seqs, block)
        cut = lax.dynamic_index_in_dim(cut, lax.axis_index("seq"), 1, keepdims=False)
        cut = lax.dynamic_index_in_dim(cut, lax.axis_index("zl"), 2, keepdims=False)
        return cut.reshape(-1)

    small, at = jnp.zeros((1024,), F32), 0
    for vector in (norm1_gain, norm1_bias, norm2_gain, norm2_bias, qkv_bias):
        small += jnp.pad(vector.astype(F32), (at, 1024 - at - vector.shape[0]))
        at += vector.shape[0]
    small = small.reshape(8, 128)
    token_shape = (seqs, half, rows, width)
    owners = (half, zh, seqs, 2, 2)
    count = team * rows
    limit = 60
    tables = rotary_tables(length)
    tokens_all, small_all, qkv_all, out_all, gate_cut, up_cut = call(
        enter_kernel, zh, 0,
        [
            (tokens, IN_HBM), (small, IN_HBM), (qkv_weight, IN_HBM), (out_weight, IN_HBM),
            (gate_weight, IN_HBM), (up_weight, IN_HBM),
        ],
        [
            (token_shape, BF, IN_HBM),
            (owners + (8, 128), F32, IN_HBM),
            (owners + (own, 3 * part), BF, IN_HBM),
            ((zh, 2, 2, own, width), BF, IN_HBM),
            ((team, own, ff_part), BF, IN_HBM),
            ((team, own, ff_part), BF, IN_HBM),
        ],
        [pltpu.VMEM((2, own, ff), BF), pltpu.VMEM((2, team, own, ff_part), BF)],
        3 + (2 + OUT_PARTS) * (zh + 4) + DOWN_PARTS * zh + 2 * QKV_GATHERS * (3 * zh + 2), 32, 60,
    )
    small = small_all.reshape(devices, 1024)
    norms = small[:, : 4 * own].reshape(devices, 4, own).transpose(1, 0, 2).reshape(4, width)
    qkv_offset = mine_columns(small[:, 4 * own : 7 * own].reshape(-1), 3).reshape(1, 3 * part)
    qkv_matrix = qkv_all.reshape(width, 3 * part)
    out_matrix = out_all.reshape(part, width)

    token_scratch = [
        pltpu.VMEM((rows, width), BF), pltpu.VMEM((rows, width), BF), pltpu.VMEM((3, rows, width), BF)
    ]
    head_shape = (count, part)
    heads = [(head_shape, BF, IN_HBM)] * 4
    head_scratch = [pltpu.VMEM(head_shape, BF)] * 4
    (
        middle, first_input, queries, keys, values, mixed, upstream_all, input_all, gate_all, up_all, down_all,
    ) = call(
        middle_kernel, zh, 1,
        [
            (tokens, IN_VMEM), (cotangent, IN_HBM), (tokens_all.reshape(count, width), IN_HBM),
            (qkv_matrix, IN_HBM), (out_matrix, IN_HBM),
            (gate_cut, IN_HBM), (up_cut, IN_HBM), (down_weight, IN_HBM),
            (norms, IN_VMEM), (qkv_offset, IN_VMEM), (tables, IN_VMEM),
        ],
        [
            ((rows, width), F32, IN_VMEM),
            ((count, width), BF, IN_HBM),
            *heads,
            (token_shape, BF, IN_HBM),
            (token_shape, BF, IN_HBM),
            (owners + (own, ff_part), BF, IN_HBM),
            (owners + (own, ff_part), BF, IN_HBM),
            ((zh, 2, 2, ff_own, width), BF, IN_HBM),
        ],
        [
            pltpu.VMEM((count, width), BF), pltpu.VMEM((count, width), BF),
            pltpu.VMEM((width, 3 * part), BF), pltpu.VMEM((part, width), BF),
            *head_scratch, pltpu.VMEM(token_shape, BF),
            *token_scratch, pltpu.VMEM((rows, width), BF),
        ],
        9 + (DOWN_PARTS + 4 * FF_PARTS) * (zh + 4), 40, limit,
    )
    second_input = input_all.reshape(count, width)
    ff_shape = (count, ff_part)
    down_pieces = [size for _, size in row_pieces(ff_own, DOWN_PARTS)]
    result, partial_second, grad_gate, grad_up, down_part = call(
        feed_kernel, zh, 4,
        [
            (middle, IN_VMEM), (second_input, IN_HBM), (upstream_all.reshape(count, width), IN_HBM),
            (gate_all.reshape(width, ff_part), IN_HBM), (up_all.reshape(width, ff_part), IN_HBM),
            (down_all.reshape(ff_part, width), IN_HBM),
        ],
        [
            ((rows, width), BF, IN_VMEM),
            ((count, width), BF, IN_HBM),
            (ff_shape, BF, IN_HBM),
            (ff_shape, BF, IN_HBM),
            ((zh, ff_own, width), BF, IN_HBM),
        ],
        [
            pltpu.VMEM((count, width), BF), pltpu.VMEM((count, width), BF),
            pltpu.VMEM((width, ff_part), BF), pltpu.VMEM((width, ff_part), BF), pltpu.VMEM((ff_part, width), BF),
            pltpu.VMEM(ff_shape, F32), pltpu.VMEM(ff_shape, F32),
            *[pltpu.VMEM(ff_shape, BF)] * 3,
            pltpu.VMEM(token_shape, BF), pltpu.VMEM((count, width), BF), pltpu.VMEM(down_all.shape, BF),
            *token_scratch, [near_buffers(zh, size, width) for size in down_pieces],
        ],
        3 + DOWN_PARTS * 2, 32, 62,
    )
    grad_middle, second_sums, down_total, gate_total, up_total, out_total, grad_projected, bias_sums = call(
        back_kernel, zh, 2,
        [
            (middle, IN_VMEM), (cotangent, IN_VMEM), (norms, IN_VMEM),
            (partial_second.reshape(token_shape), IN_HBM),
            (down_part, IN_HBM), (second_input, IN_HBM), (grad_gate, IN_HBM), (grad_up, IN_HBM),
            (out_matrix, IN_HBM), (queries, IN_HBM), (keys, IN_HBM), (values, IN_HBM), (mixed, IN_HBM),
            (tables, IN_VMEM),
        ],
        [
            ((rows, width), F32, IN_VMEM),
            ((8, width), F32, IN_VMEM),
            ((ff_own, width), F32, IN_HBM),
            ((own, ff), F32, IN_HBM),
            ((own, ff), F32, IN_HBM),
            ((own, width), F32, IN_HBM),
            ((count, 3 * part), BF, IN_HBM),
            ((1, 3 * part), F32, IN_VMEM),
        ],
        [
            *token_scratch, pltpu.VMEM((rows, width), BF), pltpu.VMEM(token_shape, BF),
            pltpu.VMEM((part, width), BF), *head_scratch, pltpu.VMEM(head_shape, BF),
            pltpu.VMEM((count, 3 * part), BF), pltpu.VMEM(out_all.shape, BF),
            pltpu.VMEM((count, width), BF), pltpu.VMEM(ff_shape, BF),
            pltpu.VMEM(gate_all.shape, BF), pltpu.VMEM(gate_all.shape, BF),
            pltpu.VMEM((2, team, own, ff_part), BF), pltpu.VMEM((2, team, own, ff_part), F32),
            [far_buffers(zh, size, width) for size in down_pieces],
            [
                (near_buffers(zh, size, width), far_buffers(zh, size, width))
                for _, size in row_pieces(own, OUT_PARTS)
            ],
            [
                column_buffers(zh, own, size)
                for _ in range(2)
                for _, _, size in column_pieces(ff_part, FF_PARTS)
            ],
        ],
        9 + (OUT_PARTS + DOWN_PARTS + 4 * FF_PARTS) * (zh + 4), 60, 62,
    )
    grad_inputs, sums, qkv_total = call(
        leave_kernel, zh, 3,
        [
            (tokens, IN_VMEM), (grad_middle, IN_VMEM), (norms, IN_VMEM),
            (second_sums, IN_VMEM), (bias_sums, IN_VMEM), (grad_projected, IN_VMEM),
            (first_input, IN_HBM), (qkv_matrix, IN_HBM),
        ],
        [
            ((rows, width), F32, IN_VMEM),
            ((8, width), F32, IN_VMEM),
            ((own, 3 * width), F32, IN_VMEM),
        ],
        [
            pltpu.VMEM((count, width), BF), pltpu.VMEM((width, 3 * part), BF), pltpu.VMEM(token_shape, BF),
            pltpu.VMEM(qkv_all.shape, BF), pltpu.VMEM((team, own, 3 * part), BF),
            *token_scratch, pltpu.VMEM((2 * zh + 8, 8, width), F32),
            [column_buffers(zh, own, size) for _, _, size in column_pieces(3 * part, QKV_PARTS)],
        ],
        2 * zh + 8 + (2 * QKV_PARTS) * (zh + 4), 24, limit,
    )

    def mine(vector_row, size):
        return lax.dynamic_slice_in_dim(vector_row, index * size, size, 0)

    return (
        result[None],
        grad_inputs[None],
        mine(sums[0], own),
        mine(sums[1], own),
        qkv_total,
        mine(sums[4:7].reshape(-1), 3 * own),
        out_total,
        mine(sums[2], own),
        mine(sums[3], own),
        gate_total,
        up_total,
        down_total,
    )


def solution(mesh):
    half, shards = mesh.shape["seq"], mesh.shape["shard"]
    fine = jax.sharding.Mesh(mesh.devices.reshape(half, shards // 8, 2, 2, 2), ALL)
    token = P(("zh", "zl", "y", "c"), "seq", None)
    row = P(ALL)

    def program(*arguments):
        whole_tiles = shards == 16 and arguments[-1].shape[0] // (half * shards) % ROWS == 0
        return jax.shard_map(
            per_device if whole_tiles else plain_device,
            mesh=fine,
            in_specs=(token, token) + (row,) * 10,
            out_specs=(token, token) + (row,) * 10,
            check_vma=False,
        )(*arguments)

    return program
```
